32 devices in a mesh: dp: 8 (over y, x, core), tensor: 4 (over z).
Axes of the slice: x: 2, y: 2, z: 4, core: 2. Of those that a mesh axis runs over, the one named last changes fastest.
Arguments:
- inputs: bfloat16 [16384, 512], P(('dp', 'tensor')), may hold values from -6 to 6
- segment_ids: int32 [16384], P('dp'), may hold values from -1 to 7, as said below
- query_weight: bfloat16 [512, 512], P(None, 'tensor'), may hold values from -0.25 to 0.25
- query_bias: float32 [512], P('tensor'), may hold values from -3 to 3
- key_weight: bfloat16 [512, 512], P(None, 'tensor'), may hold values from -0.25 to 0.25
- value_weight: bfloat16 [512, 512], P(None, 'tensor'), may hold values from -0.25 to 0.25
- value_bias: float32 [512], P('tensor'), may hold values from -3 to 3
- out_weight: bfloat16 [512, 512], P('tensor'), may hold values from -1 to 1
- out_bias: float32 [512], replicated, may hold values from -2 to 2
- first_gain: float32 [512], replicated, may hold values from 0.5 to 1.5
- first_shift: float32 [512], replicated, may hold values from -2 to 2
- up_weight: bfloat16 [512, 2048], P(None, 'tensor'), may hold values from -0.25 to 0.25
- up_bias: float32 [2048], P('tensor'), may hold values from -2 to 2
- down_weight: bfloat16 [2048, 512], P('tensor'), may hold values from -0.1875 to 0.1875
- down_bias: float32 [512], replicated, may hold values from -2 to 2
- second_gain: float32 [512], replicated, may hold values from 0.5 to 1.5
- second_shift: float32 [512], replicated, may hold values from -2 to 2
- cotangent: bfloat16 [16384, 512], P(('dp', 'tensor')), may hold values from -6 to 6
Outputs:
- result: bfloat16 [16384, 512], P(('dp', 'tensor'))
- input_grad: float32 [16384, 512], P(('dp', 'tensor'))
- query_weight_grad: float32 [512, 512], P(None, 'tensor')
- query_bias_grad: float32 [512], P('tensor')
- key_weight_grad: float32 [512, 512], P(None, 'tensor')
- value_weight_grad: float32 [512, 512], P(None, 'tensor')
- value_bias_grad: float32 [512], P('tensor')
- out_weight_grad: float32 [512, 512], P('tensor')
- out_bias_grad: float32 [512], replicated
- first_gain_grad: float32 [512], replicated
- first_shift_grad: float32 [512], replicated
- up_weight_grad: float32 [512, 2048], P(None, 'tensor')
- up_bias_grad: float32 [2048], P('tensor')
- down_weight_grad: float32 [2048, 512], P('tensor')
- down_bias_grad: float32 [512], replicated
- second_gain_grad: float32 [512], replicated
- second_shift_grad: float32 [512], replicated
The draws below stay inside these ranges and needn't reach their ends.
Inputs may be any that keep to these rules, and one draw needn't show every extreme that they name: `segment_ids`: each packed sequence of 1024 tokens holds documents numbered 0 to 7 in order (some may be empty), then 1024 / 16 to 128 tokens of padding numbered -1.
All inputs are finite; a program needn't handle non-finite values.
Results may differ from the reference program's by a relative error of at most 0.03.
Values may be sent and summed in bfloat16 or wider, within the bound.
No kernel may reach another device: no remote copies, remote signals or barrier semaphores. Data moves between devices by JAX's collectives and lax.ppermute only.
A program may use at most 128 MiB of HBM per device.

```python
import math
import jax
import jax.numpy as jnp
from jax import lax

D = 512
FF = 2048
HEADS = 8
HEAD_DIM = 64
LEN = 1024
DOCS = 8
TOKENS = 16384


def draw_segment_ids(key, part):
    key = jax.random.fold_in(key, 11)
    key_pad, key_cut = jax.random.split(key)
    row_count = TOKENS // LEN
    padding = jax.random.randint(key_pad, (row_count, 1), LEN // 16, LEN // 8 + 1)
    used_len = LEN - padding
    raw_cuts = jax.random.randint(key_cut, (row_count, DOCS - 1), 0, 1 << 30)
    cut_points = 1 + raw_cuts % (used_len - 1)
    places = jnp.arange(LEN, dtype=jnp.int32)[None, :]
    labels = jnp.sum((cut_points[:, None, :] <= places[:, :, None]).astype(jnp.int32), -1)
    labels = jnp.where(places < used_len, labels, -1)
    return labels.reshape(TOKENS).astype(jnp.int32)


def levels(stream_key, shape, cuts, low, high):
    gain = 1.0
    for dim, parts in cuts:
        steps = jax.random.uniform(jax.random.fold_in(jax.random.fold_in(stream_key, 6), dim), (parts,), jnp.float32, low / len(cuts), high / len(cuts))
        gain = gain * jnp.repeat(jnp.exp(steps), shape[dim] // parts).reshape((-1,) + (1,) * (len(shape) - 1 - dim))
    return gain


def bell_draw(key, extent, deviation, reach, cuts=(), held_as=jnp.bfloat16):
    values = deviation * jax.random.normal(key, extent, jnp.float32)
    if cuts:
        values = values * levels(key, extent, cuts, -0.22, 0.18)
    return jnp.clip(values, -reach, reach).astype(held_as)


def setup_inputs(seed: int = 0) -> dict:
    keys = jax.random.split(jax.random.key(seed), 19)
    return {
        "inputs": bell_draw(keys[0], (TOKENS, D), 1.0, 6.0, ((0, 32),)),
        "segment_ids": draw_segment_ids(jax.random.fold_in(keys[18], 71), 0),
        "query_weight": bell_draw(keys[2], (D, D), D ** -0.5, 0.25, ((1, 4),)),
        "query_bias": bell_draw(keys[3], (D,), 0.5, 3.0, ((0, 4),), jnp.float32),
        "key_weight": bell_draw(keys[4], (D, D), D ** -0.5, 0.25, ((1, 4),)),
        "value_weight": bell_draw(keys[5], (D, D), D ** -0.5, 0.25, ((1, 4),)),
        "value_bias": bell_draw(keys[6], (D,), 0.5, 3.0, ((0, 4),), jnp.float32),
        "out_weight": bell_draw(keys[7], (D, D), (D // 16) ** -0.5, 1.0, ((0, 4),)),
        "out_bias": bell_draw(keys[8], (D,), 0.3, 2.0, (), jnp.float32),
        "first_gain": jnp.clip(1.0 + 0.1 * jax.random.normal(keys[9], (D,), jnp.float32), 0.5, 1.5),
        "first_shift": bell_draw(keys[10], (D,), 0.3, 2.0, (), jnp.float32),
        "up_weight": bell_draw(keys[11], (D, FF), D ** -0.5, 0.25, ((1, 4),)),
        "up_bias": bell_draw(keys[12], (FF,), 0.3, 2.0, ((0, 4),), jnp.float32),
        "down_weight": bell_draw(keys[13], (FF, D), (FF // 2) ** -0.5, 0.1875, ((0, 4),)),
        "down_bias": bell_draw(keys[14], (D,), 0.3, 2.0, (), jnp.float32),
        "second_gain": jnp.clip(1.0 + 0.1 * jax.random.normal(keys[15], (D,), jnp.float32), 0.5, 1.5),
        "second_shift": bell_draw(keys[16], (D,), 0.3, 2.0, (), jnp.float32),
        "cotangent": bell_draw(keys[17], (TOKENS, D), 1.0, 6.0, ((0, 32),)),
    }


epsilon = 1e-05

@jax.custom_vjp
def low(v):
    return lax.optimization_barrier(v.astype(jnp.bfloat16)).astype(jnp.float32)

@jax.custom_vjp
def low_back(v):
    return v

def low_keep(v):
    return (low(v), None)

def low_pass(kept, grad):
    return (grad,)

def back_keep(v):
    return (v, None)

def back_low(kept, grad):
    return (low(grad),)
low.defvjp(low_keep, low_pass)
low_back.defvjp(back_keep, back_low)

def matmul_hi(operand, weight):
    return jnp.dot(operand, weight, precision=lax.Precision.HIGHEST)

def layer_norm(hidden, norm_gain, norm_shift):
    center = hidden - lax.optimization_barrier(jnp.mean(hidden, -1, keepdims=True))
    spread = lax.optimization_barrier(jnp.mean(center * center, -1, keepdims=True))
    return center * lax.rsqrt(spread + epsilon) * norm_gain + norm_shift

def attend_one(pieces):
    queries, key_rows, values, labels = pieces
    length = queries.shape[0]
    query_heads = queries.reshape(length, HEADS, HEAD_DIM)
    key_heads = key_rows.reshape(length, HEADS, HEAD_DIM)
    value_heads = values.reshape(length, HEADS, HEAD_DIM)
    scores = jnp.einsum('qhd,khd->hqk', query_heads, key_heads, precision=lax.Precision.HIGHEST) * (1.0 / math.sqrt(HEAD_DIM))
    scores = low_back(scores)
    allowed = (labels[:, None] == labels[None, :])[None]
    scores = jnp.where(allowed, scores, -1000000000.0)
    row_max = lax.optimization_barrier(jnp.max(scores, -1, keepdims=True))
    exponent = jnp.exp(scores - row_max)
    attn_probs = exponent / lax.optimization_barrier(jnp.sum(exponent, -1, keepdims=True))
    mixed = jnp.einsum('hqk,khd->qhd', low(attn_probs), value_heads, precision=lax.Precision.HIGHEST)
    return mixed.reshape(length, HEADS * HEAD_DIM)

def layer(layer_in, weights, labels):
    query_weight, query_bias, key_weight, value_weight, value_bias, out_weight, out_bias, first_gain, first_shift, up_weight, up_bias, down_weight, down_bias, second_gain, second_shift = weights
    seq_count = labels.shape[0]
    layer_low = low(layer_in)
    queries = low(low_back(matmul_hi(layer_low, query_weight) + query_bias))
    key_rows = low(low_back(matmul_hi(layer_low, key_weight)))
    values = low(low_back(matmul_hi(layer_low, value_weight) + value_bias))
    attended = lax.map(jax.checkpoint(attend_one), (queries.reshape(seq_count, LEN, D), key_rows.reshape(seq_count, LEN, D), values.reshape(seq_count, LEN, D), labels))
    attended = low(low_back(attended.reshape(seq_count * LEN, D)))
    branch = low_back(matmul_hi(attended, out_weight) + out_bias)
    middle = layer_norm(layer_in + branch, first_gain, first_shift)
    hidden_pre = low_back(matmul_hi(low(middle), up_weight) + up_bias)
    activated = low(jax.nn.gelu(hidden_pre))
    branch_two = low_back(matmul_hi(activated, down_weight) + down_bias)
    return layer_norm(middle + branch_two, second_gain, second_shift)

def reference(inputs, segment_ids, query_weight, query_bias, key_weight, value_weight, value_bias, out_weight, out_bias, first_gain, first_shift, up_weight, up_bias, down_weight, down_bias, second_gain, second_shift, cotangent):
    weights = (query_weight.astype(jnp.float32), query_bias.astype(jnp.float32), key_weight.astype(jnp.float32), value_weight.astype(jnp.float32), value_bias.astype(jnp.float32), out_weight.astype(jnp.float32), out_bias.astype(jnp.float32), first_gain.astype(jnp.float32), first_shift.astype(jnp.float32), up_weight.astype(jnp.float32), up_bias.astype(jnp.float32), down_weight.astype(jnp.float32), down_bias.astype(jnp.float32), second_gain.astype(jnp.float32), second_shift.astype(jnp.float32))
    group = math.gcd(max(1, 4096 // LEN), TOKENS // LEN)
    blocks = TOKENS // (group * LEN)
    block_inputs = inputs.astype(jnp.float32).reshape(blocks, group * LEN, D)
    block_labels = segment_ids.reshape(blocks, group, LEN)
    block_pulls = cotangent.astype(jnp.float32).reshape(blocks, group * LEN, D)

    def scan_step(running, pieces):
        start_rows, labels, pull_rows = pieces

        def forward(params, layer_in):
            return layer(layer(layer_in, params, labels), params, labels)
        output, puller = jax.vjp(forward, weights, start_rows)
        grad_params, grad_rows = puller(pull_rows)
        running = jax.tree.map(jnp.add, running, grad_params)
        return (running, (output.astype(jnp.bfloat16), grad_rows))
    initial = jax.tree.map(jnp.zeros_like, weights)
    totals, (outputs, grad_inputs) = lax.scan(scan_step, initial, (block_inputs, block_labels, block_pulls))
    grad_qw, grad_qb, grad_kw, grad_vw, grad_vb, grad_ow, grad_ob, grad_fg, grad_fs, grad_uw, grad_ub, grad_dw, grad_db, grad_sg, grad_ss = totals
    return (outputs.reshape(TOKENS, D), grad_inputs.reshape(TOKENS, D), grad_qw, grad_qb, grad_kw, grad_vw, grad_vb, grad_ow, grad_ob, grad_fg, grad_fs, grad_uw, grad_ub, grad_dw, grad_db, grad_sg, grad_ss)
```

```python
import math

import jax
import jax.numpy as jnp
from jax import lax
from jax.sharding import PartitionSpec as P

HEAD_DIM = 64
LEN = 1024
EPS = 1e-05
LOW = jnp.bfloat16
F32 = jnp.float32


def swap_dp(value, bit):
    count = lax.axis_size("dp")
    return lax.ppermute(value, "dp", [(i, i ^ bit) for i in range(count)])


def swap_tensor(value, step):
    count = lax.axis_size("tensor")
    return lax.ppermute(value, "tensor", [(i, i ^ step) for i in range(count)])


def regroup(block):
    dp, tensor = lax.axis_size("dp"), lax.axis_size("tensor")
    pairs = [
        ((2 * k + c) * tensor + 2 * a + b, (2 * k + b) * tensor + 2 * a + c)
        for k in range(dp // 2)
        for c in range(2)
        for a in range(tensor // 2)
        for b in range(2)
        if b != c
    ]
    moved = lax.ppermute(block, ("dp", "tensor"), pairs)
    stays = (lax.axis_index("dp") % 2) == (lax.axis_index("tensor") % 2)
    return jnp.where(stays, block, moved)


def gather_units(piece):
    kinds, rows, width = piece.shape
    near = jnp.stack((piece, swap_tensor(piece, 1)), 1)
    far = jnp.stack((swap_tensor(piece, 2), swap_tensor(piece, 3)), 1)
    near = near.reshape(kinds, 2, 1, 1, 1, rows, width)
    far = far.reshape(kinds, 2, 1, 1, 1, rows, width)
    near = jnp.concatenate((near, swap_dp(near, 2)), 3)
    far = jnp.concatenate((far, swap_dp(far, 4)), 2)
    near = jnp.concatenate((near, swap_dp(near, 4)), 2)
    far = jnp.concatenate((far, swap_dp(far, 2)), 3)
    near = jnp.concatenate((near, swap_dp(near, 1)), 4)
    far = jnp.concatenate((far, swap_dp(far, 1)), 4)
    return jnp.concatenate((near, far), 1).reshape(kinds, 32 * rows, width)


def add_half(value, axis, bit):
    first, second = jnp.split(value, 2, axis)
    return (first.astype(F32) + swap_dp(second, bit).astype(F32)).astype(LOW)


def reduce_units(total):
    kinds, rows, width = total.shape
    rows //= 32
    total = total.reshape(kinds, 4, 2, 2, 2, rows, width)
    total = add_half(total, 4, 1)
    near, far = total[:, :2], total[:, 2:]
    near = add_half(near, 3, 2)
    far = add_half(far, 2, 4)
    near = add_half(near, 2, 4)
    far = add_half(far, 3, 2)
    near = near.reshape(kinds, 2, rows, width)
    far = far.reshape(kinds, 2, rows, width)
    own = (
        near[:, 0].astype(F32)
        + swap_tensor(near[:, 1], 1).astype(F32)
        + swap_tensor(far[:, 0], 2).astype(F32)
        + swap_tensor(far[:, 1], 3).astype(F32)
    )
    bit = 8
    while bit < lax.axis_size("dp"):
        own = own + swap_dp(own.astype(LOW), bit).astype(F32)
        bit *= 2
    own = own.astype(LOW).reshape(kinds, 1, 1, 1, rows, width)
    left, right = own[..., : width // 2], own[..., width // 2 :]
    left = both(left, 2, 2)
    right = both(right, 1, 4)
    left = both(left, 1, 4)
    right = both(right, 2, 2)
    left = both(left, 3, 1)
    right = both(right, 3, 1)
    return jnp.concatenate((left, right), -1).reshape(kinds, 8 * rows, width).astype(F32)


def both(value, axis, bit):
    other = swap_dp(value, bit)
    upper = (lax.axis_index("dp") & bit) != 0
    return jnp.where(
        upper, jnp.concatenate((other, value), axis), jnp.concatenate((value, other), axis)
    )


def relative(value, axis, bit_of):
    return jnp.where(bit_of, jnp.flip(value, axis), value)


def unit_flips(value):
    dp, tensor = lax.axis_index("dp"), lax.axis_index("tensor")
    rows = value.shape[-1]
    value = relative(value, 1, (dp & 4) != 0)
    value = relative(value, 2, (dp & 2) != 0)
    value = relative(value, 3, (dp & 1) != 0)
    value = value.reshape(2, 2, 8, rows)
    value = relative(value, 0, (tensor & 2) != 0)
    value = relative(value, 1, (tensor & 1) != 0)
    return value.reshape(4, 2, 2, 2, rows)


def gather_bias(shard):
    rows = shard.shape[0] // 8
    dp = lax.axis_index("dp")
    blocks = shard.reshape(2, 2, 2, rows)
    blocks = relative(blocks, 0, (dp & 4) != 0)
    blocks = relative(blocks, 1, (dp & 2) != 0)
    blocks = relative(blocks, 2, (dp & 1) != 0)
    flat = blocks.reshape(8 * rows)
    return flat


def dot_nt(a, b):
    return lax.dot_general(a, b, (((1,), (1,)), ((), ())), preferred_element_type=F32)


def dot_tn(a, b):
    return lax.dot_general(a, b, (((0,), (0,)), ((), ())), preferred_element_type=F32)


def dot_nn(a, b):
    return jnp.dot(a, b, preferred_element_type=F32)


def norm(value):
    center = value - jnp.mean(value, -1, keepdims=True)
    scale = lax.rsqrt(jnp.mean(center * center, -1, keepdims=True) + EPS)
    return center * scale, scale


def norm_back(grad, gain, unit, scale):
    scaled = grad * gain
    mean_a = jnp.mean(scaled, -1, keepdims=True)
    mean_b = jnp.mean(scaled * unit, -1, keepdims=True)
    return (scaled - mean_a - unit * mean_b) * scale


def split_heads(value):
    return value.reshape(value.shape[0], -1, HEAD_DIM)


def attention_forward(layer_in, low_all, labels_own, labels_all, w):
    rows = layer_in.shape[0]
    low_own = low_all[:rows]
    queries = (dot_nt(low_own, w["q"]) + w["qb"]).astype(LOW)
    keys = dot_nt(low_all, w["k"]).astype(LOW)
    values = (dot_nt(low_all, w["v"]) + w["vb"]).astype(LOW)
    scores = jnp.einsum(
        "qhd,khd->hqk", split_heads(queries), split_heads(keys), preferred_element_type=F32
    ) * (1.0 / math.sqrt(HEAD_DIM))
    scores = jnp.where((labels_own[:, None] == labels_all[None, :])[None], scores, -1e9)
    exponent = jnp.exp(scores - jnp.max(scores, -1, keepdims=True))
    probs = (exponent / jnp.sum(exponent, -1, keepdims=True)).astype(LOW)
    inv_total = 1.0 / jnp.sum(probs.astype(F32), -1, keepdims=True)
    attended = (
        jnp.einsum("hqk,khd->qhd", probs, split_heads(values), preferred_element_type=F32)
        .astype(LOW)
        .reshape(rows, -1)
    )
    pre_one = layer_in + dot_nn(attended, w["o"]) + w["ob"]
    unit_one, scale_one = norm(pre_one)
    middle = unit_one * w["g1"] + w["s1"]
    return middle, (queries, keys, values, probs, inv_total, attended, unit_one, scale_one)


def ffn_forward(middle, w):
    hidden = dot_nt(middle.astype(LOW), w["up"]) + w["upb"]
    active, pull = jax.vjp(jax.nn.gelu, hidden)
    slope = pull(jnp.ones_like(hidden))[0].astype(LOW)
    active = active.astype(LOW)
    pre_two = middle + dot_nn(active, w["down"]) + w["db"]
    unit_two, scale_two = norm(pre_two)
    return unit_two * w["g2"] + w["s2"], (middle.astype(LOW), active, slope, unit_two, scale_two)


def ffn_backward(grad_out, kept, w):
    middle_low, active, slope, unit_two, scale_two = kept
    grad_gain = jnp.sum(grad_out * unit_two, 0)
    grad_shift = jnp.sum(grad_out, 0)
    grad_pre = norm_back(grad_out, w["g2"], unit_two, scale_two)
    grad_branch = grad_pre.astype(LOW)
    grad_db = jnp.sum(grad_branch.astype(F32), 0)
    grad_hidden = (dot_nt(grad_branch, w["down"]) * slope.astype(F32)).astype(LOW)
    grad_upb = jnp.sum(grad_hidden.astype(F32), 0)
    grad_middle = grad_pre + dot_nn(grad_hidden, w["up"])
    return grad_middle, (grad_branch, grad_hidden), (grad_db, grad_gain, grad_shift, grad_upb)


def attention_backward(grad_middle, kept, w):
    queries, keys, values, probs, inv_total, attended, unit_one, scale_one = kept
    rows = grad_middle.shape[0]
    grad_gain = jnp.sum(grad_middle * unit_one, 0)
    grad_shift = jnp.sum(grad_middle, 0)
    grad_pre = norm_back(grad_middle, w["g1"], unit_one, scale_one)
    grad_branch = grad_pre.astype(LOW)
    grad_ob = jnp.sum(grad_branch.astype(F32), 0)
    grad_att = dot_nt(grad_branch, w["o"]).astype(LOW)
    grad_heads = split_heads(grad_att)
    grad_probs = jnp.einsum(
        "qhd,khd->hqk", grad_heads, split_heads(values), preferred_element_type=F32
    )
    inv = 1.0 / math.sqrt(HEAD_DIM)
    delta = jnp.sum(probs.astype(F32) * grad_probs, -1, keepdims=True)
    grad_scores = (probs.astype(F32) * (grad_probs - delta * inv_total)).astype(LOW)
    grad_q = (
        jnp.einsum("hqk,khd->qhd", grad_scores, split_heads(keys), preferred_element_type=F32) * inv
    ).astype(LOW).reshape(rows, -1)
    grad_k = (
        jnp.einsum("hqk,qhd->khd", grad_scores, split_heads(queries), preferred_element_type=F32)
        * inv
    ).astype(LOW).reshape(2 * rows, -1)
    grad_v = jnp.einsum(
        "hqk,qhd->khd", probs, grad_heads, preferred_element_type=F32
    ).astype(LOW).reshape(2 * rows, -1)
    grad_qb = jnp.sum(grad_q.astype(F32), 0)
    grad_vb = jnp.sum(grad_v.astype(F32), 0)
    both_halves = dot_nn(grad_k, w["k"]) + dot_nn(grad_v, w["v"])
    grad_in = grad_pre + dot_nn(grad_q, w["q"]) + both_halves[:rows]
    sent = both_halves[rows:].astype(LOW)
    return (
        grad_in,
        sent,
        (grad_branch, grad_q, grad_k, grad_v),
        (grad_ob, grad_gain, grad_shift, grad_qb, grad_vb),
    )


def per_device(
    inputs, segment_ids, query_weight, query_bias, key_weight, value_weight, value_bias, out_weight, out_bias,
    first_gain, first_shift, up_weight, up_bias, down_weight, down_bias, second_gain, second_shift, cotangent,
):
    rows, width = inputs.shape
    dp, tensor = lax.axis_index("dp"), lax.axis_index("tensor")
    core = dp % 2
    slice_at = dp % 8
    head_rows = query_weight.shape[1] // 8
    unit_rows = up_weight.shape[1] // 8

    def columns(weight, count):
        return lax.dynamic_slice_in_dim(weight, slice_at * count, count, 1).T

    qkv = jnp.stack([columns(v, head_rows) for v in (query_weight, key_weight, value_weight)])
    first_in = regroup(inputs)
    grad_flow = regroup(cotangent).astype(F32)
    qkv = gather_units(qkv)
    out_all = gather_units(lax.dynamic_slice_in_dim(out_weight, slice_at * head_rows, head_rows, 0)[None])[0]
    up_all = gather_units(columns(up_weight, unit_rows)[None])[0]
    down_all = gather_units(
        lax.dynamic_slice_in_dim(down_weight, slice_at * unit_rows, unit_rows, 0)[None]
    )[0]
    flat = jnp.concatenate((gather_bias(query_bias), gather_bias(value_bias), gather_bias(up_bias)))
    flat = jnp.stack([flat] + [swap_tensor(flat, j) for j in (1, 2, 3)])
    heads = query_bias.shape[0]
    w = {
        "q": qkv[0], "k": qkv[1], "v": qkv[2], "o": out_all, "up": up_all, "down": down_all,
        "qb": flat[:, :heads].reshape(-1), "vb": flat[:, heads : 2 * heads].reshape(-1),
        "upb": flat[:, 2 * heads :].reshape(-1),
        "ob": out_bias, "g1": first_gain, "s1": first_shift, "db": down_bias, "g2": second_gain, "s2": second_shift,
    }

    seq = lax.dynamic_slice_in_dim(segment_ids, (tensor // 2) * LEN, LEN)
    seq = jnp.where(core == tensor % 2, seq, swap_dp(seq, 1))
    labels_own = lax.dynamic_slice_in_dim(seq, core * rows, rows)
    labels_all = jnp.concatenate((labels_own, lax.dynamic_slice_in_dim(seq, (1 - core) * rows, rows)))

    kept = []
    layer_in = first_in.astype(F32)
    for _ in range(2):
        low = layer_in.astype(LOW)
        low_all = jnp.concatenate((low, swap_dp(low, 1)))
        middle, kept_attention = attention_forward(layer_in, low_all, labels_own, labels_all, w)
        layer_in, kept_ffn = ffn_forward(middle, w)
        kept.append((low_all, kept_attention, kept_ffn))
    result = regroup(layer_in.astype(LOW))

    pairs_list, sums = [], []
    for position in (1, 0):
        low_all, kept_attention, kept_ffn = kept[position]
        grad_middle, ffn_pairs, ffn_sums = ffn_backward(grad_flow, kept_ffn, w)
        grad_flow, sent, att_pairs, att_sums = attention_backward(grad_middle, kept_attention, w)
        grad_flow = grad_flow + swap_dp(sent, 1).astype(F32)
        pairs_list.append(
            (
                (kept_ffn[1], ffn_pairs[0]),
                (ffn_pairs[1], kept_ffn[0]),
                (kept_attention[5], att_pairs[0]),
                (att_pairs[1], low_all[:rows]),
                (att_pairs[2], low_all),
                (att_pairs[3], low_all),
            )
        )
        sums.append(att_sums + ffn_sums)
    grads = [
        dot_tn(jnp.concatenate((second[0], first[0])), jnp.concatenate((second[1], first[1]))).astype(LOW)
        for second, first in zip(*pairs_list)
    ]
    down_grad = reduce_units(grads[0][None])[0]
    up_grad = reduce_units(grads[1][None])[0].T
    out_grad, q_grad, k_grad, v_grad = reduce_units(jnp.stack(grads[2:]))
    ob, g1, s1, qb, vb, db, g2, s2, upb = (a + b for a, b in zip(*sums))

    def absolute(value):
        return unit_flips(value.reshape(4, 2, 2, 2, -1)).reshape(4, -1)

    small = jnp.concatenate(
        [ob, g1, s1, db, g2, s2]
        + [absolute(v).reshape(-1) for v in (qb, vb, upb)]
    ).reshape(-1, width)
    small = lax.psum(small, ("dp", "tensor")).reshape(-1)
    ob, g1, s1, db, g2, s2 = jnp.split(small[: 6 * width], 6)

    def own(start, count):
        return lax.dynamic_slice_in_dim(small[start : start + 4 * count], tensor * count, count)

    units = up_bias.shape[0]
    qb = own(6 * width, heads)
    vb = own(6 * width + 4 * heads, heads)
    upb = own(6 * width + 8 * heads, units)
    input_grad = regroup(grad_flow.astype(LOW)).astype(F32)
    return (
        result, input_grad, q_grad.T, qb, k_grad.T, v_grad.T, vb, out_grad, ob, g1, s1, up_grad, upb, down_grad, db, g2, s2,
    )


def solution(mesh):
    split = P(("dp", "tensor"), None)
    columns, rows, part = P(None, "tensor"), P("tensor", None), P("tensor")
    return jax.shard_map(
        per_device,
        mesh=mesh,
        in_specs=(
            split, P("dp"), columns, part, columns, columns, part, rows, P(), P(), P(), columns, part, rows, P(), P(),
            P(), split,
        ),
        out_specs=(
            split, split, columns, part, columns, columns, part, rows, P(), P(), P(), columns, part, rows, P(), P(), P(),
        ),
        check_vma=False,
    )
```

```python
import functools
import math

import jax
import jax.numpy as jnp
from jax import lax
from jax.experimental import pallas as pl
from jax.experimental.pallas import tpu as pltpu
from jax.sharding import PartitionSpec as P

HEAD_DIM = 64
LEN = 1024
EPS = 1e-05
LANES = 128
LOW = jnp.bfloat16
F32 = jnp.float32
EXP2_SCALE = math.log2(math.e) / math.sqrt(HEAD_DIM)
INV_SCALE = 1.0 / math.sqrt(HEAD_DIM)
BARRED = -1e9


def swap_dp(value, bits):
    count = lax.axis_size("dp")
    return lax.ppermute(value, "dp", [(i, i ^ bits) for i in range(count)])


def swap_tensor(value, step):
    count = lax.axis_size("tensor")
    return lax.ppermute(value, "tensor", [(i, i ^ step) for i in range(count)])


def regroup(block):
    dp, tensor = lax.axis_size("dp"), lax.axis_size("tensor")
    pairs = [
        ((2 * k + c) * tensor + 2 * a + b, (2 * k + b) * tensor + 2 * a + c)
        for k in range(dp // 2)
        for c in range(2)
        for a in range(tensor // 2)
        for b in range(2)
        if b != c
    ]
    moved = lax.ppermute(block, ("dp", "tensor"), pairs)
    stays = (lax.axis_index("dp") % 2) == (lax.axis_index("tensor") % 2)
    return jnp.where(stays, block, moved)


def gather_units(piece):
    return spread(join_shards(piece))


def join_shards(piece):
    return jnp.stack([piece] + [swap_tensor(piece, step) for step in (1, 2, 3)], 1)


def spread(piece):
    own = [piece] + [swap_dp(piece, bits) for bits in (2, 4, 6)]
    return own, [swap_dp(block, 1) for block in own]


def sum_parts(parts):
    total = parts[0].astype(F32)
    for part in parts[1:]:
        total = total + part.astype(F32)
    return total


def reduce_core(keep, send):
    other = swap_dp(send, 1)
    return [sum_parts((keep[i], other[i])).astype(LOW) for i in range(4)]


def reduce_plane(parts):
    parts = [parts[0]] + [swap_dp(parts[i], 2 * i) for i in (1, 2, 3)]
    return [sum_parts([part[j] for part in parts]).astype(LOW) for j in range(4)]


def reduce_shards(parts):
    total = sum_parts([parts[0]] + [swap_tensor(parts[j], j) for j in (1, 2, 3)])
    bits = 8
    while bits < lax.axis_size("dp"):
        total = total + swap_dp(total.astype(LOW), bits).astype(F32)
        bits *= 2
    return total.astype(LOW)


def sum_everywhere(value):
    for step in (2, 1):
        value = value + swap_tensor(value, step)
    bits = 1
    while bits < lax.axis_size("dp"):
        value = value + swap_dp(value, bits)
        bits *= 2
    return value


def flip(value, axis, wanted):
    return jnp.where(wanted, jnp.flip(value, axis), value)


def relative_bias(shard):
    dp = lax.axis_index("dp")
    blocks = shard.reshape(2, 2, 2, -1)
    blocks = flip(flip(flip(blocks, 2, (dp & 1) != 0), 1, (dp & 2) != 0), 0, (dp & 4) != 0)
    return blocks.reshape(-1)


def dot_nt(a, b):
    return lax.dot_general(a, b, (((1,), (1,)), ((), ())), preferred_element_type=F32)


def dot_tn(a, b):
    return lax.dot_general(a, b, (((0,), (0,)), ((), ())), preferred_element_type=F32)


def dot_nn(a, b):
    return jnp.dot(a, b, preferred_element_type=F32)


def norm(value):
    center = value - jnp.mean(value, -1, keepdims=True)
    scale = lax.rsqrt(jnp.mean(center * center, -1, keepdims=True) + EPS)
    return center * scale, scale


def norm_back(grad, gain, unit, scale):
    scaled = grad * gain
    mean_a = jnp.mean(scaled, -1, keepdims=True)
    mean_b = jnp.mean(scaled * unit, -1, keepdims=True)
    return (scaled - mean_a - unit * mean_b) * scale


def lane_half(which):
    first = lax.broadcasted_iota(jnp.int32, (1, LANES), 1) < HEAD_DIM
    return first if which == 0 else jnp.logical_not(first)


VMEM_LIMIT = 14 * 2**20


def call(kernel, name, micros, outs, scratch, *operands, scalars=0):
    return pl.pallas_call(
        kernel,
        in_specs=[pl.BlockSpec(memory_space=pltpu.SMEM)] * scalars
        + [pl.BlockSpec(memory_space=pltpu.VMEM)] * (len(operands) - scalars),
        out_shape=[jax.ShapeDtypeStruct(shape, dtype) for shape, dtype in outs],
        scratch_shapes=[pltpu.VMEM(shape, dtype) for shape, dtype in scratch],
        compiler_params=pltpu.CompilerParams(vmem_limit_bytes=VMEM_LIMIT),
        cost_estimate=pl.CostEstimate(flops=int(micros * 1.1e9), bytes_accessed=0, transcendentals=0),
        name=name,
    )(*operands)


def attention_first_kernel(*refs):
    blocks, w_ref, rest = refs[:8], refs[-3], refs[8:-3] + refs[-2:]
    rows = blocks[0].shape[2]
    for at, block in enumerate(blocks):
        c, i = divmod(at, 4)
        for kind in range(4):
            for j in range(4):
                w_ref[kind, pl.ds(j * LANES + (2 * i + c) * rows, rows)] = block[kind, j]
    attention_forward_kernel(*rest[:5], w_ref, *rest[5:])


def attention_forward_kernel(
    in_ref, low_ref, other_ref, mark_ref, barred_ref, w_ref, qb, vb, ob, gain, shift,
    q_out, k_out, v_out, e_out, inv_out, o_out, att_out, unit_out, scale_out, mid_out, kmask, vmask,
):
    wq, wk, wv, wo = (w_ref.at[kind] for kind in range(4))
    rows = in_ref.shape[0]
    heads = wq.shape[0] // HEAD_DIM
    zero = jnp.zeros((), LOW)
    low = low_ref[...]
    q_out[...] = (dot_nt(low, wq[...]) + qb[...]).astype(LOW)
    for half, part in enumerate((low, other_ref[...])):
        r = slice(half * rows, (half + 1) * rows)
        keys = dot_nt(part, wk[...]).astype(LOW)
        values = (dot_nt(part, wv[...]) + vb[...]).astype(LOW)
        k_out[r] = keys
        v_out[r] = values
        for h in range(heads):
            keep = lane_half(h % 2)
            cols = slice(h // 2 * LANES, (h // 2 + 1) * LANES)
            kmask[h, r, :LANES] = jnp.where(keep, keys[:, cols], barred_ref[r])
            kmask[h, r, LANES:] = jnp.where(keep, keys[:, cols], zero)
            vmask[h, r] = jnp.where(keep, values[:, cols], jnp.ones((), LOW))
    mark = mark_ref[...]
    first = lane_half(0)
    for p in range(heads // 2):
        cols = slice(p * LANES, (p + 1) * LANES)
        scaled = q_out[:, cols].astype(F32) * EXP2_SCALE
        high = scaled.astype(LOW)
        rest = (scaled - high.astype(F32)).astype(LOW)
        mixed = []
        for h in range(2):
            keep = lane_half(h)
            query = jnp.concatenate((jnp.where(keep, high, mark), jnp.where(keep, rest, zero)), 1)
            scores = dot_nt(query, kmask[2 * p + h])
            exponent = jnp.exp2(scores - jnp.max(scores, -1, keepdims=True)).astype(LOW)
            e_out[2 * p + h] = exponent
            mixed.append(dot_nn(exponent, vmask[2 * p + h]))
        inv = 1.0 / pltpu.roll(jnp.where(first, mixed[1], mixed[0]), HEAD_DIM, 1)
        attended = jnp.where(first, mixed[0], mixed[1]) * inv
        inv_out[:, cols] = inv
        o_out[:, cols] = attended
        att_out[:, cols] = attended.astype(LOW)
    unit, scale = norm(in_ref[...].astype(F32) + dot_nn(att_out[...], wo[...]) + ob[...])
    unit_out[...] = unit
    scale_out[...] = jnp.broadcast_to(scale, scale_out.shape)
    mid_out[...] = unit * gain[...] + shift[...]


def attention_forward(layer_in, low, other, mark, barred, w, blocks=None):
    rows, width = layer_in.shape
    units = w["qb"].shape[1]
    heads = units // HEAD_DIM
    outs = [
        ((rows, units), LOW), ((2 * rows, units), LOW), ((2 * rows, units), LOW), ((heads, rows, 2 * rows), LOW),
        ((rows, units), F32), ((rows, units), F32), ((rows, units), LOW), ((rows, width), F32), ((rows, LANES), F32),
        ((rows, width), F32),
    ]
    scratch = [((heads, 2 * rows, 2 * LANES), LOW), ((heads, 2 * rows, LANES), LOW)]
    tail = (w["qb"], w["vb"], w["ob"], w["g1"], w["s1"])
    first = (layer_in, low, other, mark, barred)
    if blocks is None:
        return call(attention_forward_kernel, "attention_forward", 8, outs, scratch, *first, w["heads"], *tail)
    outs.append(((4, units, width), LOW))
    return call(attention_first_kernel, "attention_first", 8, outs, scratch, *blocks, *first, *tail)


GELU_A = math.sqrt(2.0 / math.pi)
GELU_B = 0.044715


def pieces_of(blocks):
    start = 0
    for block in blocks:
        count = block.shape[1] * block.shape[2]
        yield slice(start, start + count), block[0].reshape(count, -1), block[1].reshape(count, -1)
        start += count


def ffn_forward_kernel(*refs):
    blocks, (mid_ref, upb, db, gain, shift) = refs[:8], refs[8:13]
    low_out, act_out, slope_out, unit_out, scale_out, out_out, next_out = refs[13:]
    middle = mid_ref[...]
    low = middle.astype(LOW)
    low_out[...] = low
    total = middle + db[...]
    for r, up, down in pieces_of(blocks):
        hidden = dot_nt(low, up) + upb[:, r]
        square = hidden * hidden
        bent = jnp.tanh(hidden * (GELU_A + GELU_A * GELU_B * square))
        half = 0.5 + 0.5 * bent
        active = (hidden * half).astype(LOW)
        act_out[:, r] = active
        inner = GELU_A + 3.0 * GELU_A * GELU_B * square
        slope_out[:, r] = (half + 0.5 * hidden * (1.0 - bent * bent) * inner).astype(LOW)
        total = total + dot_nn(active, down)
    unit, scale = norm(total)
    unit_out[...] = unit
    scale_out[...] = jnp.broadcast_to(scale, scale_out.shape)
    layer_out = unit * gain[...] + shift[...]
    out_out[...] = layer_out
    next_out[...] = layer_out.astype(LOW)


def ffn_forward(middle, w):
    rows, width = middle.shape
    units = w["upb"].shape[1]
    outs = [
        ((rows, width), LOW), ((rows, units), LOW), ((rows, units), LOW), ((rows, width), F32), ((rows, LANES), F32),
        ((rows, width), F32), ((rows, width), LOW),
    ]
    return call(
        ffn_forward_kernel, "ffn_forward", 5, outs, [], *w["ffn"], middle, w["upb"], w["db"], w["g2"], w["s2"]
    )


def row_sum(value):
    return jnp.sum(value, 0, keepdims=True)


def ffn_backward_kernel(*refs):
    blocks, (grad_ref, unit_two, scale_two, slope, unit_one, scale_one, w_ref, gain_two, gain_one) = refs[:8], refs[8:17]
    branch_two_out, hidden_out, pre_one_out, branch_one_out, att_out, sums_out = refs[17:]
    grad = grad_ref[...].astype(F32)
    unit = unit_two[...]
    sums_out[0:1] = row_sum(grad * unit)
    sums_out[1:2] = row_sum(grad)
    grad_pre = norm_back(grad, gain_two[...], unit, scale_two[:, :1])
    branch = grad_pre.astype(LOW)
    branch_two_out[...] = branch
    sums_out[2:3] = row_sum(branch.astype(F32))
    grad_middle = grad_pre
    for r, up, down in pieces_of(blocks):
        hidden = (dot_nt(branch, down) * slope[:, r].astype(F32)).astype(LOW)
        hidden_out[:, r] = hidden
        grad_middle = grad_middle + dot_nn(hidden, up)
    unit = unit_one[...]
    sums_out[3:4] = row_sum(grad_middle * unit)
    sums_out[4:5] = row_sum(grad_middle)
    grad_pre = norm_back(grad_middle, gain_one[...], unit, scale_one[:, :1])
    pre_one_out[...] = grad_pre
    branch = grad_pre.astype(LOW)
    branch_one_out[...] = branch
    sums_out[5:6] = row_sum(branch.astype(F32))
    sums_out[6:8] = jnp.zeros((2, grad.shape[1]), F32)
    att_out[...] = dot_nt(branch, w_ref[3]).astype(LOW)


def ffn_backward(grad_out, kept_ffn, kept_attention, w):
    rows, width = grad_out.shape
    units = w["upb"].shape[1]
    outs = [
        ((rows, width), LOW), ((rows, units), LOW), ((rows, width), F32), ((rows, width), LOW),
        ((rows, w["qb"].shape[1]), LOW), ((8, width), F32),
    ]
    return call(
        ffn_backward_kernel, "ffn_backward", 4, outs, [], *w["ffn"],
        grad_out, kept_ffn["unit"], kept_ffn["scale"], kept_ffn["slope"], kept_attention["unit"], kept_attention["scale"],
        w["heads"], w["g2"], w["g1"],
    )


def attention_backward_kernel(
    att_ref, pre_ref, q_ref, k_ref, v_ref, e_ref, inv_ref, o_ref, w_ref,
    in_out, sent_out, dq_out, dk_out, dv_out, vmask,
):
    wq, wk, wv = (w_ref.at[kind] for kind in range(3))
    rows = att_ref.shape[0]
    heads = wq.shape[0] // HEAD_DIM
    zero = jnp.zeros((), LOW)
    first = lane_half(0)
    spare = lax.broadcasted_iota(jnp.int32, (1, LANES), 1) % HEAD_DIM
    minus = jnp.where(spare < 3, -1.0, 0.0).astype(LOW)
    for h in range(heads):
        vmask[h] = jnp.where(lane_half(h % 2), v_ref[:, h // 2 * LANES : (h // 2 + 1) * LANES], minus)
    for p in range(heads // 2):
        cols = slice(p * LANES, (p + 1) * LANES)
        queries, keys = q_ref[:, cols], k_ref[:, cols]
        grad = (att_ref[:, cols].astype(F32) * inv_ref[:, cols]).astype(LOW)
        dots = grad.astype(F32) * o_ref[:, cols]
        dq, dk, dv = [], [], []
        for h in range(2):
            keep = lane_half(h)
            dot = jnp.sum(jnp.where(keep, dots, 0.0), -1, keepdims=True)
            top = dot.astype(LOW)
            left = dot - top.astype(F32)
            mid = left.astype(LOW)
            end = (left - mid.astype(F32)).astype(LOW)
            pieces = jnp.where(spare == 0, top, jnp.where(spare == 1, mid, jnp.where(spare == 2, end, zero)))
            exponent = e_ref[2 * p + h]
            centered = dot_nt(jnp.where(keep, grad, pieces), vmask[2 * p + h])
            grad_scores = (exponent.astype(F32) * centered).astype(LOW)
            dq.append(dot_nn(grad_scores, keys))
            dk.append(dot_tn(grad_scores, queries))
            dv.append(dot_tn(exponent, grad))
        dq_out[:, cols] = (jnp.where(first, dq[0], dq[1]) * INV_SCALE).astype(LOW)
        dk_out[:, cols] = (jnp.where(first, dk[0], dk[1]) * INV_SCALE).astype(LOW)
        dv_out[:, cols] = jnp.where(first, dv[0], dv[1]).astype(LOW)
    dq, dk, dv = dq_out[...], dk_out[...], dv_out[...]
    sent_out[...] = (dot_nn(dk[rows:], wk[...]) + dot_nn(dv[rows:], wv[...])).astype(LOW)
    in_out[...] = pre_ref[...] + dot_nn(dq, wq[...]) + dot_nn(dk[:rows], wk[...]) + dot_nn(dv[:rows], wv[...])


def attention_backward(grad_att, grad_pre, kept, w):
    rows, width = grad_pre.shape
    units = w["qb"].shape[1]
    heads = units // HEAD_DIM
    outs = [
        ((rows, width), F32), ((rows, width), LOW), ((rows, units), LOW), ((2 * rows, units), LOW), ((2 * rows, units), LOW),
    ]
    return call(
        attention_backward_kernel, "attention_backward", 12, outs, [((heads, 2 * rows, LANES), LOW)],
        grad_att, grad_pre, kept["q"], kept["k"], kept["v"], kept["e"], kept["inv"], kept["o"], w["heads"],
    )


def both_layers(firsts, seconds):
    return sum(dot_tn(a[...], b[...]) for a, b in zip(firsts, seconds))


def ffn_grads_kernel(*refs):
    actives, branches, hiddens, middles, attendeds, ones_branches = (refs[2 * i : 2 * i + 2] for i in range(6))
    outs = refs[12:]
    rows, units = actives[0].shape
    step = units // 8
    ur = step // 4
    hr = attendeds[0].shape[1] // 32
    one = jnp.ones((rows, LANES), LOW)
    out_grad = both_layers(attendeds, ones_branches).astype(LOW)
    for at in range(8):
        c, i = divmod(at, 4)
        out = outs[c].at[i]
        cols = slice(at * step, (at + 1) * step)
        down = both_layers([a.at[:, cols] for a in actives], branches).astype(LOW)
        up = both_layers([h.at[:, cols] for h in hiddens], middles).astype(LOW)
        bias = sum(dot_tn(h[:, cols], one) for h in hiddens).astype(LOW)
        for j in range(4):
            out[j, :ur] = down[j * ur : (j + 1) * ur]
            out[j, ur : 2 * ur] = up[j * ur : (j + 1) * ur]
            head = j * LANES + (2 * i + c) * hr
            out[j, 2 * ur : 2 * ur + hr] = out_grad[head : head + hr]
            for g in range(4):
                first = j * ur + g * (ur // 4)
                out[j, 2 * ur + hr :, g * LANES : (g + 1) * LANES] = bias[first : first + ur // 4]


def ffn_grads(pairs):
    rows, units = pairs[0][0].shape
    width = pairs[1][0].shape[1]
    ur, hr = units // 32, pairs[4][0].shape[1] // 32
    out = ((4, 4, 2 * ur + hr + ur // 4, width), LOW)
    return call(ffn_grads_kernel, "ffn_grads", 7, [out, out], [], *[v for pair in pairs for v in pair])


def head_grads_kernel(*refs):
    dqs, dks, dvs, lows, others = (refs[2 * i : 2 * i + 2] for i in range(5))
    outs = refs[10:]
    rows, units = dqs[0].shape
    hr = units // 32
    one = jnp.ones((rows, LANES), LOW)

    def halves(grads):
        own = [g.at[:rows] for g in grads]
        return own, [g.at[rows:] for g in grads]

    dk_own, dk_other = halves(dks)
    dv_own, dv_other = halves(dvs)
    grads = [
        both_layers(dqs, lows),
        both_layers(dk_own + dk_other, lows + others),
        both_layers(dv_own + dv_other, lows + others),
    ]
    grads = [g.astype(LOW) for g in grads]
    biases = [sum(dot_tn(g[...], one) for g in part).astype(LOW) for part in (dqs, dv_own + dv_other)]
    rest = jnp.zeros((hr, outs[0].shape[3] - 2 * LANES), LOW)
    for at in range(8):
        c, i = divmod(at, 4)
        for j in range(4):
            out = outs[c].at[i, j]
            first = j * LANES + (2 * i + c) * hr
            for kind in range(3):
                out[kind * hr : (kind + 1) * hr] = grads[kind][first : first + hr]
            for kind in range(2):
                out[3 * hr :, kind * LANES : (kind + 1) * LANES] = biases[kind][first : first + hr]
            out[3 * hr :, 2 * LANES :] = rest


def head_grads(pairs):
    units = pairs[0][0].shape[1]
    width = pairs[3][0].shape[1]
    out = ((4, 4, 4 * (units // 32), width), LOW)
    return call(head_grads_kernel, "head_grads", 5, [out, out], [], *[v for pair in pairs for v in pair])


def first_row(column):
    return column.T[:1]


def ffn_finish_kernel(ur, hr, eighth_ref, *refs):
    blocks, (down_out, up_out, out_out, bias_out, up_all, bias_all) = refs[:8], refs[8:]
    for at, block in enumerate(blocks):
        c, i = divmod(at, 4)
        slot = eighth_ref[0] ^ (2 * i + c)
        units = pl.ds(pl.multiple_of(slot * ur, ur), ur)
        down_out[units] = block[:ur].astype(F32)
        up_all[units] = block[ur : 2 * ur].astype(F32)
        out_out[pl.ds(pl.multiple_of(slot * hr, hr), hr)] = block[2 * ur : 2 * ur + hr].astype(F32)
        for g in range(4):
            some = pl.ds(pl.multiple_of(slot * ur + g * (ur // 4), ur // 4), ur // 4)
            bias_all[some] = block[2 * ur + hr :, g * LANES : (g + 1) * LANES].astype(F32)
    up_out[...] = up_all[...].T
    bias_out[...] = first_row(bias_all[...])


def ffn_finish(own, ur, hr, eighth):
    own, other = spread(own)
    width = own[0].shape[1]
    outs = [((8 * ur, width), F32), ((width, 8 * ur), F32), ((8 * hr, width), F32), ((1, 8 * ur), F32)]
    scratch = [((8 * ur, width), F32), ((8 * ur, LANES), F32)]
    return call(
        functools.partial(ffn_finish_kernel, ur, hr), "ffn_finish", 2, outs, scratch, eighth, *own, *other, scalars=1
    )


def head_finish_kernel(hr, eighth_ref, *refs):
    blocks, outs, biases, scratch = refs[:8], refs[8:11], refs[11:13], refs[13:]
    for at, block in enumerate(blocks):
        c, i = divmod(at, 4)
        slot = eighth_ref[0] ^ (2 * i + c)
        units = pl.ds(pl.multiple_of(slot * hr, hr), hr)
        for kind in range(3):
            scratch[kind][units] = block[kind * hr : (kind + 1) * hr].astype(F32)
        for kind in range(2):
            scratch[3 + kind][units] = block[3 * hr :, kind * LANES : (kind + 1) * LANES].astype(F32)
    for kind in range(3):
        outs[kind][...] = scratch[kind][...].T
    for kind in range(2):
        biases[kind][...] = first_row(scratch[3 + kind][...])


def head_finish(own, hr, eighth):
    own, other = spread(own)
    width = own[0].shape[1]
    outs = [((width, 8 * hr), F32)] * 3 + [((1, 8 * hr), F32)] * 2
    scratch = [((8 * hr, width), F32)] * 3 + [((8 * hr, LANES), F32)] * 2
    return call(
        functools.partial(head_finish_kernel, hr), "head_finish", 2, outs, scratch, eighth, *own, *other, scalars=1
    )


def per_device(
    inputs, segment_ids, query_weight, query_bias, key_weight, value_weight, value_bias, out_weight, out_bias,
    first_gain, first_shift, up_weight, up_bias, down_weight, down_bias, second_gain, second_shift, cotangent,
):
    rows, width = inputs.shape
    dp, tensor = lax.axis_index("dp"), lax.axis_index("tensor")
    core, eighth = dp % 2, dp % 8
    shard_heads, shard_units = query_weight.shape[1], up_weight.shape[1]
    hr, ur = shard_heads // 8, shard_units // 8

    def columns(weight, count):
        return lax.dynamic_slice_in_dim(weight, eighth * count, count, 1).T

    def own_rows(weight, count):
        return lax.dynamic_slice_in_dim(weight, eighth * count, count, 0)

    heads_piece = jnp.stack([columns(v, hr) for v in (query_weight, key_weight, value_weight)] + [own_rows(out_weight, hr)])
    ffn_piece = jnp.stack((columns(up_weight, ur), own_rows(down_weight, ur)))
    first_in = regroup(inputs)
    heads_piece = join_shards(heads_piece)
    heads_piece, ffn_piece = lax.optimization_barrier((heads_piece, ffn_piece))
    own, others = spread(heads_piece)
    head_blocks = own + others
    own, others = gather_units(ffn_piece)
    ffn_blocks = own + others
    seq = lax.dynamic_slice_in_dim(segment_ids, (tensor // 2) * LEN, LEN)
    seq = jnp.where(core == tensor % 2, seq, swap_dp(seq, 1))
    labels_own = lax.dynamic_slice_in_dim(seq, core * rows, rows)
    labels_all = jnp.concatenate((labels_own, lax.dynamic_slice_in_dim(seq, (1 - core) * rows, rows)))
    code = jnp.arange(LANES) % HEAD_DIM - 1
    mark = (labels_own[:, None] == code).astype(LOW)
    barred = jnp.where(labels_all[:, None] == code, 0.0, BARRED).astype(LOW)
    flat = jnp.concatenate((relative_bias(query_bias), relative_bias(value_bias), relative_bias(up_bias)))
    flat = jnp.stack((flat, swap_tensor(flat, 1)))
    flat = jnp.concatenate((flat, swap_tensor(flat, 2)))
    w = {
        "ffn": ffn_blocks,
        "qb": flat[:, :shard_heads].reshape(1, -1), "vb": flat[:, shard_heads : 2 * shard_heads].reshape(1, -1),
        "upb": flat[:, 2 * shard_heads :].reshape(4, 4, 2, ur).transpose(2, 1, 0, 3).reshape(1, -1),
        "ob": out_bias[None], "g1": first_gain[None], "s1": first_shift[None], "db": down_bias[None],
        "g2": second_gain[None], "s2": second_shift[None],
    }

    kept = []
    layer_in, low = first_in, first_in
    for position in range(2):
        other = swap_dp(low, 1)
        made = attention_forward(layer_in, low, other, mark, barred, w, None if position else head_blocks)
        q, k, v, e, inv, o, attended, unit_one, scale_one, middle = made[:10]
        if position == 0:
            w["heads"] = made[10]
        middle_low, active, slope, unit_two, scale_two, layer_out, next_low = ffn_forward(middle, w)
        attention = {"q": q, "k": k, "v": v, "e": e, "inv": inv, "o": o, "unit": unit_one, "scale": scale_one}
        ffn = {"slope": slope, "unit": unit_two, "scale": scale_two}
        kept.append((attention, ffn, low, other, attended, middle_low, active))
        layer_in, low = layer_out, next_low
    result = regroup(low)

    grad_flow = regroup(cotangent)
    ffn_pairs, head_pairs, sums = [], [], []
    for position in (1, 0):
        attention, ffn, low, other, attended, middle_low, active = kept[position]
        branch_two, grad_hidden, grad_pre, branch_one, grad_att, six = ffn_backward(grad_flow, ffn, attention, w)
        sums.append(six)
        ffn_pairs.append((active, branch_two, grad_hidden, middle_low, attended, branch_one))
        if position == 0:
            ffn_parts = reduce_core(*ffn_grads(list(zip(*ffn_pairs))))
            grad_att, *ffn_parts = lax.optimization_barrier((grad_att, *ffn_parts))
        grad_in, sent, dq, dk, dv = attention_backward(grad_att, grad_pre, attention, w)
        grad_flow = grad_in + swap_dp(sent, 1).astype(F32)
        head_pairs.append((dq, dk, dv, low, other))
    head_parts = reduce_core(*head_grads(list(zip(*head_pairs))))
    ffn_own = reduce_shards(reduce_plane(ffn_parts))
    head_own = reduce_shards(reduce_plane(head_parts))
    at = jnp.reshape(eighth, (1,)).astype(jnp.int32)
    down_grad, up_grad, out_grad, up_bias_grad = ffn_finish(ffn_own, ur, hr, at)
    q_grad, k_grad, v_grad, q_bias_grad, v_bias_grad = head_finish(head_own, hr, at)
    shared = sum_everywhere(sums[0] + sums[1])
    input_grad = regroup(grad_flow.astype(LOW)).astype(F32)
    return (
        result, input_grad, q_grad, q_bias_grad[0], k_grad, v_grad, v_bias_grad[0], out_grad, shared[5], shared[3], shared[4],
        up_grad, up_bias_grad[0], down_grad, shared[2], shared[0], shared[1],
    )


def solution(mesh):
    split = P(("dp", "tensor"), None)
    columns, rows, part = P(None, "tensor"), P("tensor", None), P("tensor")
    return jax.shard_map(
        per_device,
        mesh=mesh,
        in_specs=(
            split, P("dp"), columns, part, columns, columns, part, rows, P(), P(), P(), columns, part, rows, P(), P(),
            P(), split,
        ),
        out_specs=(
            split, split, columns, part, columns, columns, part, rows, P(), P(), P(), columns, part, rows, P(), P(), P(),
        ),
        check_vma=False,
    )
```

```python
import functools
import math

import jax
import jax.numpy as jnp
from jax import lax
from jax.experimental import pallas as pl
from jax.experimental.pallas import tpu as pltpu
from jax.sharding import PartitionSpec as P

HEAD_DIM = 64
LEN = 1024
EPS = 1e-05
LANES = 128
LOW = jnp.bfloat16
F32 = jnp.float32
EXP2_SCALE = math.log2(math.e) / math.sqrt(HEAD_DIM)
INV_SCALE = 1.0 / math.sqrt(HEAD_DIM)
BARRED = -1e9


def swap_dp(value, bits):
    count = lax.axis_size("dp")
    return lax.ppermute(value, "dp", [(i, i ^ bits) for i in range(count)])


def swap_tensor(value, step):
    count = lax.axis_size("tensor")
    return lax.ppermute(value, "tensor", [(i, i ^ step) for i in range(count)])


def regroup(block):
    dp, tensor = lax.axis_size("dp"), lax.axis_size("tensor")
    pairs = [
        ((2 * k + c) * tensor + 2 * a + b, (2 * k + b) * tensor + 2 * a + c)
        for k in range(dp // 2)
        for c in range(2)
        for a in range(tensor // 2)
        for b in range(2)
        if b != c
    ]
    moved = lax.ppermute(block, ("dp", "tensor"), pairs)
    stays = (lax.axis_index("dp") % 2) == (lax.axis_index("tensor") % 2)
    return jnp.where(stays, block, moved)


def join_shards(piece):
    pieces = jnp.stack((piece, swap_tensor(piece, 2)))
    other = swap_tensor(pieces, 1)
    return jnp.stack((pieces[0], other[0], pieces[1], other[1]))


def spread_plane(block):
    return [block] + [swap_dp(block, bits) for bits in (2, 4, 6)]


def spread(block):
    own = spread_plane(block)
    return own + [swap_dp(block, 1) for block in own]


def sum_parts(parts):
    total = parts[0].astype(F32)
    for part in parts[1:]:
        total = total + part.astype(F32)
    return total


def pair_halves(keep, send):
    other = swap_dp(send, 1)

    def pair(first, second, shards):
        return jnp.stack([sum_parts((keep[i, shards], other[i, shards])).astype(LOW) for i in (first, second)])

    near, far = slice(0, 2), slice(2, 4)
    return pair(0, 2, near), pair(1, 3, near), pair(0, 1, far), pair(2, 3, far)


def add_halves(kept, got):
    return [sum_parts((kept[i], got[i])).astype(LOW) for i in range(2)]


def add_shards(near, near_got, far, far_got):
    return [sum_parts((a[j], b[j])).astype(LOW) for a, b in ((near, near_got), (far, far_got)) for j in range(2)]


def reduce_shards(parts):
    total = sum_parts([parts[0]] + [swap_tensor(parts[j], j) for j in (1, 2, 3)])
    bits = 8
    while bits < lax.axis_size("dp"):
        total = total + swap_dp(total.astype(LOW), bits).astype(F32)
        bits *= 2
    return total.astype(LOW)


def flip(value, axis, wanted):
    return jnp.where(wanted, jnp.flip(value, axis), value)


def relative_blocks(blocks):
    dp = lax.axis_index("dp")
    return flip(flip(flip(blocks, 3, (dp & 1) != 0), 2, (dp & 2) != 0), 1, (dp & 4) != 0)


def dot_nt(a, b):
    return lax.dot_general(a, b, (((1,), (1,)), ((), ())), preferred_element_type=F32)


def dot_tn(a, b):
    return lax.dot_general(a, b, (((0,), (0,)), ((), ())), preferred_element_type=F32)


def dot_nn(a, b):
    return jnp.dot(a, b, preferred_element_type=F32)


def norm(value):
    center = value - jnp.mean(value, -1, keepdims=True)
    scale = lax.rsqrt(jnp.mean(center * center, -1, keepdims=True) + EPS)
    return center * scale, scale


def norm_back(grad, gain, unit, scale):
    scaled = grad * gain
    mean_a = jnp.mean(scaled, -1, keepdims=True)
    mean_b = jnp.mean(scaled * unit, -1, keepdims=True)
    return (scaled - mean_a - unit * mean_b) * scale


def lane_half(which):
    first = lax.broadcasted_iota(jnp.int32, (1, LANES), 1) < HEAD_DIM
    return first if which == 0 else jnp.logical_not(first)


VMEM_LIMIT = 10


def call(kernel, name, micros, outs, scratch, *operands, scalars=0, far=0, vmem=VMEM_LIMIT):
    spaces = [pltpu.SMEM] * scalars + [pl.ANY] * far + [pltpu.VMEM] * (len(operands) - scalars - far)
    return pl.pallas_call(
        kernel,
        in_specs=[pl.BlockSpec(memory_space=space) for space in spaces],
        out_specs=[pl.BlockSpec(memory_space=pltpu.VMEM)] * len(outs),
        out_shape=[jax.ShapeDtypeStruct(shape, dtype) for shape, dtype in outs],
        scratch_shapes=[pltpu.VMEM(*s) if isinstance(s, tuple) else s for s in scratch],
        compiler_params=pltpu.CompilerParams(vmem_limit_bytes=vmem * 2**20),
        cost_estimate=pl.CostEstimate(flops=int(micros * 1.1e9), bytes_accessed=0, transcendentals=0),
        name=name,
    )(*operands)


def attention_first_kernel(*refs):
    blocks, rest, w_out, scratch, sems = refs[:8], refs[8:-4], refs[-4], refs[-3:-1], refs[-1]
    copies = []
    for at, block in enumerate(blocks):
        c, i = divmod(at, 4)
        rows = block.shape[1] // 4
        for kind in range(4):
            source = block.at[:, kind * rows : (kind + 1) * rows]
            copies.append(pltpu.make_async_copy(source, w_out.at[kind, :, 2 * i + c], sems.at[at, kind]))
    for copy in copies:
        copy.start()
    for copy in copies:
        copy.wait()
    attention_forward_kernel(*rest[:5], w_out, *rest[5:], *scratch)


def attention_forward_kernel(
    in_ref, low_ref, other_ref, mark_ref, barred_ref, w_ref, qb, vb, ob, gain, shift,
    q_out, k_out, v_out, e_out, inv_out, o_out, att_out, unit_out, scale_out, mid_out, kmask, vmask,
):
    rows = in_ref.shape[0]
    wq, wk, wv, wo = (w_ref[kind].reshape(-1, w_ref.shape[-1]) for kind in range(4))
    heads = wq.shape[0] // HEAD_DIM
    zero = jnp.zeros((), LOW)
    low = low_ref[...]
    q_out[...] = (dot_nt(low, wq) + qb[...]).astype(LOW)
    for half, part in enumerate((low, other_ref[...])):
        r = slice(half * rows, (half + 1) * rows)
        k_out[r] = dot_nt(part, wk).astype(LOW)
        v_out[r] = (dot_nt(part, wv) + vb[...]).astype(LOW)
    mark = mark_ref[...]
    first = lane_half(0)
    for p in range(heads // 2):
        cols = slice(p * LANES, (p + 1) * LANES)
        keys, values = k_out[:, cols], v_out[:, cols]
        scaled = q_out[:, cols].astype(F32) * EXP2_SCALE
        high = scaled.astype(LOW)
        rest = (scaled - high.astype(F32)).astype(LOW)
        mixed = []
        for h in range(2):
            keep = lane_half(h)
            query = jnp.concatenate((jnp.where(keep, high, mark), jnp.where(keep, rest, zero)), 1)
            slot = (2 * p + h) % 4
            kmask[slot, :, :LANES] = jnp.where(keep, keys, barred_ref[...])
            kmask[slot, :, LANES:] = jnp.where(keep, keys, zero)
            vmask[slot] = jnp.where(keep, values, jnp.ones((), LOW))
            scores = dot_nt(query, kmask[slot])
            exponent = jnp.exp2(scores - jnp.max(scores, -1, keepdims=True)).astype(LOW)
            e_out[2 * p + h] = exponent
            mixed.append(dot_nn(exponent, vmask[slot]))
        inv = 1.0 / pltpu.roll(jnp.where(first, mixed[1], mixed[0]), HEAD_DIM, 1)
        attended = jnp.where(first, mixed[0], mixed[1]) * inv
        inv_out[:, cols] = inv
        o_out[:, cols] = attended
        att_out[:, cols] = attended.astype(LOW)
    unit, scale = norm(in_ref[...].astype(F32) + dot_nn(att_out[...], wo) + ob[...])
    unit_out[...] = unit
    scale_out[...] = jnp.broadcast_to(scale, scale_out.shape)
    mid_out[...] = unit * gain[...] + shift[...]


def attention_forward(layer_in, low, other, mark, barred, w, blocks=None):
    rows, width = layer_in.shape
    units = w["qb"].shape[1]
    heads = units // HEAD_DIM
    outs = [
        ((rows, units), LOW), ((2 * rows, units), LOW), ((2 * rows, units), LOW), ((heads, rows, 2 * rows), LOW),
        ((rows, units), F32), ((rows, units), F32), ((rows, units), LOW), ((rows, width), F32), ((rows, LANES), F32),
        ((rows, width), F32),
    ]
    scratch = [((4, 2 * rows, 2 * LANES), LOW), ((4, 2 * rows, LANES), LOW)]
    tail = (w["qb"], w["vb"], w["ob"], w["g1"], w["s1"])
    first = (layer_in, low, other, mark, barred)
    if blocks is None:
        return call(attention_forward_kernel, "attention_forward", 8, outs, scratch, *first, w["heads"], *tail)
    scratch.append(pltpu.SemaphoreType.DMA((8, 4)))
    outs.append(((4, 4, 8, units // 32, width), LOW))
    return call(attention_first_kernel, "attention_first", 9, outs, scratch, *blocks, *first, *tail, far=8)


GELU_A = math.sqrt(2.0 / math.pi)
GELU_B = 0.044715


def ffn_first_kernel(*refs):
    blocks, rest, w_out, sems = refs[:8], refs[8:-2], refs[-2], refs[-1]
    copies = []
    for at, block in enumerate(blocks):
        rows = block.shape[1] // 2
        for kind in range(2):
            source = block.at[:, kind * rows : (kind + 1) * rows]
            copies.append(pltpu.make_async_copy(source, w_out.at[kind, at], sems.at[at, kind]))
    for copy in copies:
        copy.start()
    for copy in copies:
        copy.wait()
    ffn_forward_kernel(rest[0], w_out, *rest[1:])


def unit_blocks(w_ref):
    count = w_ref.shape[2] * w_ref.shape[3] * 2
    for at in range(4):
        up, down = (w_ref[kind, 2 * at : 2 * at + 2].reshape(count, -1) for kind in range(2))
        yield slice(at * count, (at + 1) * count), up, down


def ffn_forward_kernel(
    mid_ref, w_ref, upb, db, gain, shift, low_out, act_out, slope_out, unit_out, scale_out, out_out, next_out
):
    middle = mid_ref[...]
    low = middle.astype(LOW)
    low_out[...] = low
    total = middle + db[...]
    for r, up, down in unit_blocks(w_ref):
        hidden = dot_nt(low, up) + upb[:, r]
        square = hidden * hidden
        bent = jnp.tanh(hidden * (GELU_A + GELU_A * GELU_B * square))
        half = 0.5 + 0.5 * bent
        active = (hidden * half).astype(LOW)
        act_out[:, r] = active
        inner = GELU_A + 3.0 * GELU_A * GELU_B * square
        slope_out[:, r] = (half + 0.5 * hidden * (1.0 - bent * bent) * inner).astype(LOW)
        total = total + dot_nn(active, down)
    unit, scale = norm(total)
    unit_out[...] = unit
    scale_out[...] = jnp.broadcast_to(scale, scale_out.shape)
    layer_out = unit * gain[...] + shift[...]
    out_out[...] = layer_out
    next_out[...] = layer_out.astype(LOW)


def ffn_forward(middle, w, blocks=None):
    rows, width = middle.shape
    units = w["upb"].shape[1]
    outs = [
        ((rows, width), LOW), ((rows, units), LOW), ((rows, units), LOW), ((rows, width), F32), ((rows, LANES), F32),
        ((rows, width), F32), ((rows, width), LOW),
    ]
    tail = (w["upb"], w["db"], w["g2"], w["s2"])
    if blocks is None:
        return call(ffn_forward_kernel, "ffn_forward", 5, outs, [], middle, w["ffn"], *tail)
    outs.append(((2, 8, 4, units // 32, width), LOW))
    scratch = [pltpu.SemaphoreType.DMA((8, 2))]
    return call(ffn_first_kernel, "ffn_first", 6, outs, scratch, *blocks, middle, *tail, far=8)


def row_sum(value):
    return jnp.sum(value, 0, keepdims=True)


def ffn_backward_kernel(
    w_ref, grad_ref, unit_two, scale_two, slope, unit_one, scale_one, heads_ref, gain_two, gain_one,
    branch_two_out, hidden_out, pre_one_out, branch_one_out, att_out, sums_out,
):
    grad = grad_ref[...].astype(F32)
    unit = unit_two[...]
    sums_out[0:1] = row_sum(grad * unit)
    sums_out[1:2] = row_sum(grad)
    grad_pre = norm_back(grad, gain_two[...], unit, scale_two[:, :1])
    branch = grad_pre.astype(LOW)
    branch_two_out[...] = branch
    sums_out[2:3] = row_sum(branch.astype(F32))
    grad_middle = grad_pre
    for r, up, down in unit_blocks(w_ref):
        hidden = (dot_nt(branch, down) * slope[:, r].astype(F32)).astype(LOW)
        hidden_out[:, r] = hidden
        grad_middle = grad_middle + dot_nn(hidden, up)
    unit = unit_one[...]
    sums_out[3:4] = row_sum(grad_middle * unit)
    sums_out[4:5] = row_sum(grad_middle)
    grad_pre = norm_back(grad_middle, gain_one[...], unit, scale_one[:, :1])
    pre_one_out[...] = grad_pre
    branch = grad_pre.astype(LOW)
    branch_one_out[...] = branch
    sums_out[5:6] = row_sum(branch.astype(F32))
    sums_out[6:8] = jnp.zeros((2, grad.shape[1]), F32)
    att_out[...] = dot_nt(branch, heads_ref[3].reshape(-1, grad.shape[1])).astype(LOW)


def ffn_backward(grad_out, kept_ffn, kept_attention, w):
    rows, width = grad_out.shape
    units = w["upb"].shape[1]
    outs = [
        ((rows, width), LOW), ((rows, units), LOW), ((rows, width), F32), ((rows, width), LOW),
        ((rows, w["qb"].shape[1]), LOW), ((8, width), F32),
    ]
    return call(
        ffn_backward_kernel, "ffn_backward", 5, outs, [], w["ffn"],
        grad_out, kept_ffn["unit"], kept_ffn["scale"], kept_ffn["slope"], kept_attention["unit"], kept_attention["scale"],
        w["heads"], w["g2"], w["g1"],
    )


def attention_backward_kernel(
    att_ref, pre_ref, q_ref, k_ref, v_ref, e_ref, inv_ref, o_ref, w_ref,
    in_out, sent_out, dq_out, dk_out, dv_out, vmask,
):
    wq, wk, wv = (w_ref[kind].reshape(-1, w_ref.shape[-1]) for kind in range(3))
    rows = att_ref.shape[0]
    heads = wq.shape[0] // HEAD_DIM
    zero = jnp.zeros((), LOW)
    first = lane_half(0)
    spare = lax.broadcasted_iota(jnp.int32, (1, LANES), 1) % HEAD_DIM
    minus = jnp.where(spare < 3, -1.0, 0.0).astype(LOW)
    for p in range(heads // 2):
        cols = slice(p * LANES, (p + 1) * LANES)
        queries, keys, values = q_ref[:, cols], k_ref[:, cols], v_ref[:, cols]
        grad = (att_ref[:, cols].astype(F32) * inv_ref[:, cols]).astype(LOW)
        dots = grad.astype(F32) * o_ref[:, cols]
        dq, dk, dv = [], [], []
        for h in range(2):
            keep = lane_half(h)
            dot = jnp.sum(jnp.where(keep, dots, 0.0), -1, keepdims=True)
            top = dot.astype(LOW)
            left = dot - top.astype(F32)
            mid = left.astype(LOW)
            end = (left - mid.astype(F32)).astype(LOW)
            pieces = jnp.where(spare == 0, top, jnp.where(spare == 1, mid, jnp.where(spare == 2, end, zero)))
            exponent = e_ref[2 * p + h]
            slot = (2 * p + h) % 4
            vmask[slot] = jnp.where(keep, values, minus)
            centered = dot_nt(jnp.where(keep, grad, pieces), vmask[slot])
            grad_scores = (exponent.astype(F32) * centered).astype(LOW)
            dq.append(dot_nn(grad_scores, keys))
            dk.append(dot_tn(grad_scores, queries))
            dv.append(dot_tn(exponent, grad))
        dq_out[:, cols] = (jnp.where(first, dq[0], dq[1]) * INV_SCALE).astype(LOW)
        dk_out[:, cols] = (jnp.where(first, dk[0], dk[1]) * INV_SCALE).astype(LOW)
        dv_out[:, cols] = jnp.where(first, dv[0], dv[1]).astype(LOW)
    dq, dk, dv = dq_out[...], dk_out[...], dv_out[...]
    sent_out[...] = (dot_nn(dk[rows:], wk) + dot_nn(dv[rows:], wv)).astype(LOW)
    in_out[...] = pre_ref[...] + dot_nn(dq, wq) + dot_nn(dk[:rows], wk) + dot_nn(dv[:rows], wv)


def attention_backward(grad_att, grad_pre, kept, w):
    rows, width = grad_pre.shape
    units = w["qb"].shape[1]
    heads = units // HEAD_DIM
    outs = [
        ((rows, width), F32), ((rows, width), LOW), ((rows, units), LOW), ((2 * rows, units), LOW), ((2 * rows, units), LOW),
    ]
    return call(
        attention_backward_kernel, "attention_backward", 12, outs,
        [((4, 2 * rows, LANES), LOW)],
        grad_att, grad_pre, kept["q"], kept["k"], kept["v"], kept["e"], kept["inv"], kept["o"], w["heads"],
    )


def both_layers(firsts, seconds):
    return sum(dot_tn(a[...], b[...]) for a, b in zip(firsts, seconds))


def ffn_grads_kernel(*refs):
    actives, branches, hiddens, middles, attendeds, ones_branches = (refs[2 * i : 2 * i + 2] for i in range(6))
    outs = refs[12:]
    rows, units = actives[0].shape
    step = units // 8
    ur = step // 4
    hr = attendeds[0].shape[1] // 32
    one = jnp.ones((rows, LANES), LOW)
    out_grad = both_layers(attendeds, ones_branches).astype(LOW)
    for at in range(8):
        c, i = divmod(at, 4)
        out = outs[c].at[i]
        cols = slice(at * step, (at + 1) * step)
        down = both_layers([a.at[:, cols] for a in actives], branches).astype(LOW)
        up = both_layers([h.at[:, cols] for h in hiddens], middles).astype(LOW)
        bias = sum(dot_tn(h[:, cols], one) for h in hiddens).astype(LOW)
        for j in range(4):
            out[j, :ur] = down[j * ur : (j + 1) * ur]
            out[j, ur : 2 * ur] = up[j * ur : (j + 1) * ur]
            head = j * LANES + (2 * i + c) * hr
            out[j, 2 * ur : 2 * ur + hr] = out_grad[head : head + hr]
            for g in range(4):
                first = j * ur + g * (ur // 4)
                out[j, 2 * ur + hr :, g * LANES : (g + 1) * LANES] = bias[first : first + ur // 4]


def ffn_grads(pairs):
    rows, units = pairs[0][0].shape
    width = pairs[1][0].shape[1]
    ur, hr = units // 32, pairs[4][0].shape[1] // 32
    out = ((4, 4, 2 * ur + hr + ur // 4, width), LOW)
    return call(ffn_grads_kernel, "ffn_grads", 7, [out, out], [], *[v for pair in pairs for v in pair])


def head_grads_kernel(eighth_ref, *refs):
    dqs, dks, dvs, lows, others, sums = (refs[2 * i : 2 * i + 2] for i in range(6))
    *outs, shared = refs[12:]
    shared[...] = sums[0][...] + sums[1][...]
    upper = lax.broadcasted_iota(jnp.int32, (16, 1), 0) < 8
    rows, units = dqs[0].shape
    hr = units // 32
    one = jnp.ones((rows, LANES), LOW)

    def halves(grads):
        own = [g.at[:rows] for g in grads]
        return own, [g.at[rows:] for g in grads]

    dk_own, dk_other = halves(dks)
    dv_own, dv_other = halves(dvs)
    grads = [
        both_layers(dqs, lows),
        both_layers(dk_own + dk_other, lows + others),
        both_layers(dv_own + dv_other, lows + others),
    ]
    grads = [g.astype(LOW) for g in grads]
    biases = [sum(dot_tn(g[...], one) for g in part).astype(LOW) for part in (dqs, dv_own + dv_other)]
    for at in range(8):
        c, i = divmod(at, 4)
        line = shared[pl.ds(eighth_ref[0] ^ (2 * i + c), 1)]
        line = jnp.where(upper, line[:, : 2 * LANES], line[:, 2 * LANES :]).astype(LOW)
        for j in range(4):
            out = outs[c].at[i, j]
            first = j * LANES + (2 * i + c) * hr
            for kind in range(3):
                out[kind * hr : (kind + 1) * hr] = grads[kind][first : first + hr]
            for kind in range(2):
                out[3 * hr :, kind * LANES : (kind + 1) * LANES] = biases[kind][first : first + hr]
            out[3 * hr :, 2 * LANES :] = line


def head_grads(pairs, eighth):
    units = pairs[0][0].shape[1]
    width = pairs[3][0].shape[1]
    out = ((4, 4, 4 * (units // 32), width), LOW)
    return call(head_grads_kernel, "head_grads", 5, [out, out], [((8, width), F32)], eighth, *[v for pair in pairs for v in pair], scalars=1)


def first_row(column):
    return column.T[:1]


def finish_kernel(ur, hr, eighth_ref, *refs):
    blocks, (down_out, up_out, out_out, up_bias) = refs[:8], refs[8:12]
    outs, biases, shared, (up_all, up_bias_all, *scratch) = refs[12:15], refs[15:17], refs[17], refs[18:]
    head = 2 * ur + hr + ur // 4
    for at, block in enumerate(blocks):
        c, i = divmod(at, 4)
        slot = eighth_ref[0] ^ (2 * i + c)
        units = pl.ds(pl.multiple_of(slot * ur, ur), ur)
        down_out[units] = block[:ur].astype(F32)
        up_all[units] = block[ur : 2 * ur].astype(F32)
        out_out[pl.ds(pl.multiple_of(slot * hr, hr), hr)] = block[2 * ur : 2 * ur + hr].astype(F32)
        for g in range(4):
            some = pl.ds(pl.multiple_of(slot * ur + g * (ur // 4), ur // 4), ur // 4)
            up_bias_all[some] = block[2 * ur + hr : head, g * LANES : (g + 1) * LANES].astype(F32)
        units = pl.ds(pl.multiple_of(slot * hr, hr), hr)
        for kind in range(3):
            scratch[kind][units] = block[head + kind * hr : head + (kind + 1) * hr].astype(F32)
        for kind in range(2):
            scratch[3 + kind][units] = block[head + 3 * hr :, kind * LANES : (kind + 1) * LANES].astype(F32)
        line = block[head + 3 * hr :, 2 * LANES :].astype(F32)
        shared[pl.ds(slot, 1)] = jnp.concatenate((line[:1], line[8:9]), 1)
    up_out[...] = up_all[...].T
    up_bias[...] = first_row(up_bias_all[...])
    for kind in range(3):
        outs[kind][...] = scratch[kind][...].T
    for kind in range(2):
        biases[kind][...] = first_row(scratch[3 + kind][...])


def finish(own, ur, hr, eighth):
    blocks = spread(own)
    width = own.shape[1]
    outs = [((8 * ur, width), F32), ((width, 8 * ur), F32), ((8 * hr, width), F32), ((1, 8 * ur), F32)]
    outs += [((width, 8 * hr), F32)] * 3 + [((1, 8 * hr), F32)] * 2 + [((8, width), F32)]
    scratch = [((8 * ur, width), F32), ((8 * ur, LANES), F32)]
    scratch += [((8 * hr, width), F32)] * 3 + [((8 * hr, LANES), F32)] * 2
    return call(functools.partial(finish_kernel, ur, hr), "finish", 3, outs, scratch, eighth, *blocks, scalars=1)


def per_device(
    inputs, segment_ids, query_weight, query_bias, key_weight, value_weight, value_bias, out_weight, out_bias,
    first_gain, first_shift, up_weight, up_bias, down_weight, down_bias, second_gain, second_shift, cotangent,
):
    rows, width = inputs.shape
    dp, tensor = lax.axis_index("dp"), lax.axis_index("tensor")
    core, eighth = dp % 2, dp % 8
    shard_heads, shard_units = query_weight.shape[1], up_weight.shape[1]
    hr, ur = shard_heads // 8, shard_units // 8

    def columns(weight, count):
        return lax.dynamic_slice_in_dim(weight, eighth * count, count, 1).T

    def own_rows(weight, count):
        return lax.dynamic_slice_in_dim(weight, eighth * count, count, 0)

    first_in = regroup(inputs)
    flat = jnp.concatenate((query_bias, value_bias, up_bias))
    top = lax.reduce_precision(flat, 8, 7)
    mid = lax.reduce_precision(flat - top, 8, 7)
    flat = jnp.concatenate((top, mid, flat - top - mid)).astype(LOW)
    count = flat.shape[0]
    flat = jnp.pad(flat, (0, -count % (16 * width))).reshape(-1, width)
    heads_piece = jnp.concatenate(
        [columns(v, hr) for v in (query_weight, key_weight, value_weight)] + [own_rows(out_weight, hr), flat]
    )
    ffn_piece = jnp.concatenate((columns(up_weight, ur), own_rows(down_weight, ur)))
    shards = jnp.stack([heads_piece] + [swap_tensor(heads_piece, step) for step in (1, 2, 3)])
    heads_own = spread_plane(shards[:, : 4 * hr])
    ffn_own = spread_plane(join_shards(ffn_piece))
    heads_own = lax.optimization_barrier(heads_own)
    head_blocks = heads_own + [swap_dp(block, 1) for block in heads_own]
    flat = shards[:, 4 * hr :].reshape(4, -1)[:, :count].astype(F32)
    flat = jnp.sum(flat.reshape(4, 3, -1), 1)
    seq = lax.dynamic_slice_in_dim(segment_ids, (tensor // 2) * LEN, LEN)
    seq = jnp.where(core == tensor % 2, seq, swap_dp(seq, 1))
    labels_own = lax.dynamic_slice_in_dim(seq, core * rows, rows)
    labels_all = jnp.concatenate((labels_own, lax.dynamic_slice_in_dim(seq, (1 - core) * rows, rows)))
    code = jnp.arange(LANES) % HEAD_DIM - 1
    mark = (labels_own[:, None] == code).astype(LOW)
    barred = jnp.where(labels_all[:, None] == code, 0.0, BARRED).astype(LOW)

    def bias(start, count):
        return relative_blocks(flat[:, start : start + count].reshape(4, 2, 2, 2, -1))

    w = {
        "qb": bias(0, shard_heads).reshape(1, -1), "vb": bias(shard_heads, shard_heads).reshape(1, -1),
        "upb": bias(2 * shard_heads, shard_units).reshape(4, 4, 2, ur).transpose(2, 1, 0, 3).reshape(1, -1),
        "ob": out_bias[None], "g1": first_gain[None], "s1": first_shift[None], "db": down_bias[None],
        "g2": second_gain[None], "s2": second_shift[None],
    }

    kept = []
    layer_in, low = first_in, first_in
    for position in range(2):
        other = swap_dp(low, 1)
        made = attention_forward(layer_in, low, other, mark, barred, w, None if position else head_blocks)
        q, k, v, e, inv, o, attended, unit_one, scale_one, middle = made[:10]
        if position == 0:
            w["heads"] = made[10]
            middle, cotangent, *ffn_own = lax.optimization_barrier((middle, cotangent, *ffn_own))
            ffn_blocks = ffn_own + [swap_dp(block, 1) for block in ffn_own]
        made = ffn_forward(middle, w, None if position else ffn_blocks)
        middle_low, active, slope, unit_two, scale_two, layer_out, next_low = made[:7]
        if position == 0:
            w["ffn"] = made[7]
        attention = {"q": q, "k": k, "v": v, "e": e, "inv": inv, "o": o, "unit": unit_one, "scale": scale_one}
        ffn = {"slope": slope, "unit": unit_two, "scale": scale_two}
        kept.append((attention, ffn, low, other, attended, middle_low, active))
        layer_in, low = layer_out, next_low
    result = regroup(low)

    grad_flow = regroup(cotangent)
    ffn_pairs, head_pairs = [], []
    for position in (1, 0):
        attention, ffn, low, other, attended, middle_low, active = kept[position]
        branch_two, grad_hidden, grad_pre, branch_one, grad_att, six = ffn_backward(grad_flow, ffn, attention, w)
        ffn_pairs.append((active, branch_two, grad_hidden, middle_low, attended, branch_one))
        if position == 0:
            near, near_sent, far, far_sent = pair_halves(*ffn_grads(list(zip(*ffn_pairs))))
            grad_att, near_sent, far_sent = lax.optimization_barrier((grad_att, near_sent, far_sent))
            near_got, far_got = swap_dp(near_sent, 2), swap_dp(far_sent, 4)
        grad_in, sent, dq, dk, dv = attention_backward(grad_att, grad_pre, attention, w)
        if position == 1:
            grad_in, result = lax.optimization_barrier((grad_in, result))
        if position == 0:
            dq, sent, near_got, far_got = lax.optimization_barrier((dq, sent, near_got, far_got))
            (near, near_sent), (far, far_sent) = add_halves(near, near_got), add_halves(far, far_got)
            dq, near_sent, far_sent = lax.optimization_barrier((dq, near_sent, far_sent))
            near_got, far_got = swap_dp(near_sent, 4), swap_dp(far_sent, 2)
        grad_flow = grad_in + swap_dp(sent, 1).astype(F32)
        head_pairs.append((dq, dk, dv, low, other, six))
    at = jnp.reshape(eighth, (1,)).astype(jnp.int32)
    keep, send = head_grads(list(zip(*head_pairs)), at)
    near_got, far_got, keep, send = lax.optimization_barrier((near_got, far_got, keep, send))
    ffn_parts = add_shards(near, near_got, far, far_got)
    near, near_sent, far, far_sent = pair_halves(keep, send)
    near_got, far_got = swap_dp(near_sent, 2), swap_dp(far_sent, 4)
    ffn_own = reduce_shards(ffn_parts)
    (near, near_sent), (far, far_sent) = add_halves(near, near_got), add_halves(far, far_got)
    near_got, far_got = swap_dp(near_sent, 4), swap_dp(far_sent, 2)
    head_own = reduce_shards(add_shards(near, near_got, far, far_got))
    own = jnp.concatenate((ffn_own, head_own))
    own, grad_low = lax.optimization_barrier((own, grad_flow.astype(LOW)))
    input_grad = regroup(grad_low).astype(F32)
    (
        down_grad, up_grad, out_grad, up_bias_grad, q_grad, k_grad, v_grad, q_bias_grad, v_bias_grad, shared,
    ) = finish(own, ur, hr, at)
    return (
        result, input_grad, q_grad, q_bias_grad[0], k_grad, v_grad, v_bias_grad[0], out_grad, shared[5], shared[3], shared[4],
        up_grad, up_bias_grad[0], down_grad, shared[2], shared[0], shared[1],
    )


def solution(mesh):
    split = P(("dp", "tensor"), None)
    columns, rows, part = P(None, "tensor"), P("tensor", None), P("tensor")
    return jax.shard_map(
        per_device,
        mesh=mesh,
        in_specs=(
            split, P("dp"), columns, part, columns, columns, part, rows, P(), P(), P(), columns, part, rows, P(), P(),
            P(), split,
        ),
        out_specs=(
            split, split, columns, part, columns, columns, part, rows, P(), P(), P(), columns, part, rows, P(), P(), P(),
        ),
        check_vma=False,
    )
```

```python
import functools
import math

import jax
import jax.numpy as jnp
from jax import lax
from jax.experimental import pallas as pl
from jax.experimental.pallas import tpu as pltpu
from jax.sharding import PartitionSpec as P

HEAD_DIM = 64
LEN = 1024
EPS = 1e-05
LANES = 128
LOW = jnp.bfloat16
F32 = jnp.float32
EXP2_SCALE = math.log2(math.e) / math.sqrt(HEAD_DIM)
INV_SCALE = 1.0 / math.sqrt(HEAD_DIM)
BARRED = -1e9


def swap_dp(value, bits):
    count = lax.axis_size("dp")
    return lax.ppermute(value, "dp", [(i, i ^ bits) for i in range(count)])


def swap_tensor(value, step):
    count = lax.axis_size("tensor")
    return lax.ppermute(value, "tensor", [(i, i ^ step) for i in range(count)])


def regroup(block):
    dp, tensor = lax.axis_size("dp"), lax.axis_size("tensor")
    pairs = [
        ((2 * k + c) * tensor + 2 * a + b, (2 * k + b) * tensor + 2 * a + c)
        for k in range(dp // 2)
        for c in range(2)
        for a in range(tensor // 2)
        for b in range(2)
        if b != c
    ]
    moved = lax.ppermute(block, ("dp", "tensor"), pairs)
    stays = (lax.axis_index("dp") % 2) == (lax.axis_index("tensor") % 2)
    return jnp.where(stays, block, moved)


def join_shards(piece):
    pieces = jnp.stack((piece, swap_tensor(piece, 2)))
    other = swap_tensor(pieces, 1)
    return jnp.stack((pieces[0], other[0], pieces[1], other[1]))


def spread_plane(block):
    return [block] + [swap_dp(block, bits) for bits in (2, 4, 6)]


def spread(block):
    own = spread_plane(block)
    return own + [swap_dp(block, 1) for block in own]


def sum_parts(parts):
    total = parts[0].astype(F32)
    for part in parts[1:]:
        total = total + part.astype(F32)
    return total


def pair_halves(keep, other):
    def pair(first, second, shards):
        return jnp.stack([sum_parts((keep[i, shards], other[i, shards])).astype(LOW) for i in (first, second)])

    near, far = slice(0, 2), slice(2, 4)
    return pair(0, 2, near), pair(1, 3, near), pair(0, 1, far), pair(2, 3, far)


def add_halves(kept, got):
    return [sum_parts((kept[i], got[i])).astype(LOW) for i in range(2)]


def add_shards(near, near_got, far, far_got):
    return [sum_parts((a[j], b[j])).astype(LOW) for a, b in ((near, near_got), (far, far_got)) for j in range(2)]


def swap_shards(parts):
    return [parts[0]] + [swap_tensor(parts[j], j) for j in (1, 2, 3)]


def sum_shards(parts):
    total = sum_parts(parts)
    bits = 8
    while bits < lax.axis_size("dp"):
        total = total + swap_dp(total.astype(LOW), bits).astype(F32)
        bits *= 2
    return total.astype(LOW)


def flip(value, axis, wanted):
    return jnp.where(wanted, jnp.flip(value, axis), value)


def relative_blocks(blocks):
    dp = lax.axis_index("dp")
    return flip(flip(flip(blocks, 3, (dp & 1) != 0), 2, (dp & 2) != 0), 1, (dp & 4) != 0)


def dot_nt(a, b):
    return lax.dot_general(a, b, (((1,), (1,)), ((), ())), preferred_element_type=F32)


def dot_tn(a, b):
    return lax.dot_general(a, b, (((0,), (0,)), ((), ())), preferred_element_type=F32)


def dot_nn(a, b):
    return jnp.dot(a, b, preferred_element_type=F32)


def norm(value):
    center = value - jnp.mean(value, -1, keepdims=True)
    scale = lax.rsqrt(jnp.mean(center * center, -1, keepdims=True) + EPS)
    return center * scale, scale


def norm_back(grad, gain, unit, scale):
    scaled = grad * gain
    mean_a = jnp.mean(scaled, -1, keepdims=True)
    mean_b = jnp.mean(scaled * unit, -1, keepdims=True)
    return (scaled - mean_a - unit * mean_b) * scale


def lane_half(which):
    first = lax.broadcasted_iota(jnp.int32, (1, LANES), 1) < HEAD_DIM
    return first if which == 0 else jnp.logical_not(first)


VMEM_MIB = {
    "attention_first": 10, "attention_forward": 10, "ffn_first": 5, "ffn_forward": 5, "ffn_backward": 4, "ffn_grads": 3,
    "attention_backward": 6, "last_backward": 10, "finish": 7,
}


def call(kernel, name, micros, outs, scratch, *operands, scalars=0, far=0):
    spaces = [pltpu.SMEM] * scalars + [pl.ANY] * far + [pltpu.VMEM] * (len(operands) - scalars - far)
    return pl.pallas_call(
        kernel,
        in_specs=[pl.BlockSpec(memory_space=space) for space in spaces],
        out_specs=[pl.BlockSpec(memory_space=pltpu.VMEM)] * len(outs),
        out_shape=[jax.ShapeDtypeStruct(shape, dtype) for shape, dtype in outs],
        scratch_shapes=[pltpu.VMEM(*s) if isinstance(s, tuple) else s for s in scratch],
        compiler_params=pltpu.CompilerParams(vmem_limit_bytes=VMEM_MIB[name] * 2**20),
        cost_estimate=pl.CostEstimate(flops=int(micros * 1.1e9), bytes_accessed=0, transcendentals=0),
        name=name,
    )(*operands)


def attention_first_kernel(*refs):
    blocks, rest, w_out, scratch, sems = refs[:8], refs[8:-4], refs[-4], refs[-3:-1], refs[-1]
    copies = []
    for at, block in enumerate(blocks):
        c, i = divmod(at, 4)
        rows = block.shape[1] // 4
        for kind in range(4):
            source = block.at[:, kind * rows : (kind + 1) * rows]
            copies.append(pltpu.make_async_copy(source, w_out.at[kind, :, 2 * i + c], sems.at[at, kind]))
    for copy in copies:
        copy.start()
    for copy in copies:
        copy.wait()
    attention_forward_kernel(*rest[:5], w_out, *rest[5:], *scratch)


def attention_forward_kernel(
    in_ref, low_ref, other_ref, mark_ref, barred_ref, w_ref, qb, vb, ob, gain, shift,
    q_out, k_out, v_out, e_out, inv_out, o_out, att_out, unit_out, scale_out, mid_out, kmask, vmask,
):
    rows = in_ref.shape[0]
    wq, wk, wv, wo = (w_ref[kind].reshape(-1, w_ref.shape[-1]) for kind in range(4))
    heads = wq.shape[0] // HEAD_DIM
    zero = jnp.zeros((), LOW)
    low = low_ref[...]
    q_out[...] = (dot_nt(low, wq) + qb[...]).astype(LOW)
    for half, part in enumerate((low, other_ref[...])):
        r = slice(half * rows, (half + 1) * rows)
        k_out[r] = dot_nt(part, wk).astype(LOW)
        v_out[r] = (dot_nt(part, wv) + vb[...]).astype(LOW)
    mark = mark_ref[...]
    first = lane_half(0)
    for p in range(heads // 2):
        cols = slice(p * LANES, (p + 1) * LANES)
        keys, values = k_out[:, cols], v_out[:, cols]
        scaled = q_out[:, cols].astype(F32) * EXP2_SCALE
        high = scaled.astype(LOW)
        rest = (scaled - high.astype(F32)).astype(LOW)
        mixed = []
        for h in range(2):
            keep = lane_half(h)
            query = jnp.concatenate((jnp.where(keep, high, mark), jnp.where(keep, rest, zero)), 1)
            slot = (2 * p + h) % 4
            kmask[slot, :, :LANES] = jnp.where(keep, keys, barred_ref[...])
            kmask[slot, :, LANES:] = jnp.where(keep, keys, zero)
            vmask[slot] = jnp.where(keep, values, jnp.ones((), LOW))
            scores = dot_nt(query, kmask[slot])
            exponent = jnp.exp2(scores - jnp.max(scores, -1, keepdims=True)).astype(LOW)
            e_out[2 * p + h] = exponent
            mixed.append(dot_nn(exponent, vmask[slot]))
        inv = 1.0 / pltpu.roll(jnp.where(first, mixed[1], mixed[0]), HEAD_DIM, 1)
        attended = jnp.where(first, mixed[0], mixed[1]) * inv
        inv_out[:, cols] = inv
        o_out[:, cols] = attended
        att_out[:, cols] = attended.astype(LOW)
    unit, scale = norm(in_ref[...].astype(F32) + dot_nn(att_out[...], wo) + ob[...])
    unit_out[...] = unit
    scale_out[...] = jnp.broadcast_to(scale, scale_out.shape)
    mid_out[...] = unit * gain[...] + shift[...]


def attention_forward(layer_in, low, other, mark, barred, w, blocks=None):
    rows, width = layer_in.shape
    units = w["qb"].shape[1]
    heads = units // HEAD_DIM
    outs = [
        ((rows, units), LOW), ((2 * rows, units), LOW), ((2 * rows, units), LOW), ((heads, rows, 2 * rows), LOW),
        ((rows, units), F32), ((rows, units), F32), ((rows, units), LOW), ((rows, width), F32), ((rows, LANES), F32),
        ((rows, width), F32),
    ]
    scratch = [((4, 2 * rows, 2 * LANES), LOW), ((4, 2 * rows, LANES), LOW)]
    tail = (w["qb"], w["vb"], w["ob"], w["g1"], w["s1"])
    first = (layer_in, low, other, mark, barred)
    if blocks is None:
        return call(attention_forward_kernel, "attention_forward", 8, outs, scratch, *first, w["heads"], *tail)
    scratch.append(pltpu.SemaphoreType.DMA((8, 4)))
    outs.append(((4, 4, 8, units // 32, width), LOW))
    return call(attention_first_kernel, "attention_first", 9, outs, scratch, *blocks, *first, *tail, far=8)


GELU_A = math.sqrt(2.0 / math.pi)
GELU_B = 0.044715


def ffn_first_kernel(*refs):
    blocks, rest, w_out, sems = refs[:8], refs[8:-2], refs[-2], refs[-1]
    copies = []
    for at, block in enumerate(blocks):
        rows = block.shape[1] // 2
        for kind in range(2):
            source = block.at[:, kind * rows : (kind + 1) * rows]
            copies.append(pltpu.make_async_copy(source, w_out.at[kind, at], sems.at[at, kind]))
    for copy in copies:
        copy.start()
    for copy in copies:
        copy.wait()
    ffn_forward_kernel(rest[0], w_out, *rest[1:])


def unit_blocks(w_ref):
    count = w_ref.shape[2] * w_ref.shape[3] * 2
    for at in range(4):
        up, down = (w_ref[kind, 2 * at : 2 * at + 2].reshape(count, -1) for kind in range(2))
        yield slice(at * count, (at + 1) * count), up, down


def ffn_forward_kernel(
    mid_ref, w_ref, upb, db, gain, shift, low_out, act_out, slope_out, unit_out, scale_out, out_out, next_out
):
    middle = mid_ref[...]
    low = middle.astype(LOW)
    low_out[...] = low
    total = middle + db[...]
    for r, up, down in unit_blocks(w_ref):
        hidden = dot_nt(low, up) + upb[:, r]
        square = hidden * hidden
        bent = jnp.tanh(hidden * (GELU_A + GELU_A * GELU_B * square))
        half = 0.5 + 0.5 * bent
        active = (hidden * half).astype(LOW)
        act_out[:, r] = active
        inner = GELU_A + 3.0 * GELU_A * GELU_B * square
        slope_out[:, r] = (half + 0.5 * hidden * (1.0 - bent * bent) * inner).astype(LOW)
        total = total + dot_nn(active, down)
    unit, scale = norm(total)
    unit_out[...] = unit
    scale_out[...] = jnp.broadcast_to(scale, scale_out.shape)
    layer_out = unit * gain[...] + shift[...]
    out_out[...] = layer_out
    next_out[...] = layer_out.astype(LOW)


def ffn_forward(middle, w, blocks=None):
    rows, width = middle.shape
    units = w["upb"].shape[1]
    outs = [
        ((rows, width), LOW), ((rows, units), LOW), ((rows, units), LOW), ((rows, width), F32), ((rows, LANES), F32),
        ((rows, width), F32), ((rows, width), LOW),
    ]
    tail = (w["upb"], w["db"], w["g2"], w["s2"])
    if blocks is None:
        return call(ffn_forward_kernel, "ffn_forward", 5, outs, [], middle, w["ffn"], *tail)
    outs.append(((2, 8, 4, units // 32, width), LOW))
    scratch = [pltpu.SemaphoreType.DMA((8, 2))]
    return call(ffn_first_kernel, "ffn_first", 6, outs, scratch, *blocks, middle, *tail, far=8)


def row_sum(value):
    return jnp.sum(value, 0, keepdims=True)


def ffn_backward_kernel(
    w_ref, grad_ref, unit_two, scale_two, slope, unit_one, scale_one, heads_ref, gain_two, gain_one,
    branch_two_out, hidden_out, pre_one_out, branch_one_out, att_out, sums_out,
):
    grad = grad_ref[...].astype(F32)
    unit = unit_two[...]
    sums_out[0:1] = row_sum(grad * unit)
    sums_out[1:2] = row_sum(grad)
    grad_pre = norm_back(grad, gain_two[...], unit, scale_two[:, :1])
    branch = grad_pre.astype(LOW)
    branch_two_out[...] = branch
    sums_out[2:3] = row_sum(branch.astype(F32))
    grad_middle = grad_pre
    for r, up, down in unit_blocks(w_ref):
        hidden = (dot_nt(branch, down) * slope[:, r].astype(F32)).astype(LOW)
        hidden_out[:, r] = hidden
        grad_middle = grad_middle + dot_nn(hidden, up)
    unit = unit_one[...]
    sums_out[3:4] = row_sum(grad_middle * unit)
    sums_out[4:5] = row_sum(grad_middle)
    grad_pre = norm_back(grad_middle, gain_one[...], unit, scale_one[:, :1])
    pre_one_out[...] = grad_pre
    branch = grad_pre.astype(LOW)
    branch_one_out[...] = branch
    sums_out[5:6] = row_sum(branch.astype(F32))
    sums_out[6:8] = jnp.zeros((2, grad.shape[1]), F32)
    att_out[...] = dot_nt(branch, heads_ref[3].reshape(-1, grad.shape[1])).astype(LOW)


def ffn_backward(grad_out, kept_ffn, kept_attention, w):
    rows, width = grad_out.shape
    units = w["upb"].shape[1]
    outs = [
        ((rows, width), LOW), ((rows, units), LOW), ((rows, width), F32), ((rows, width), LOW),
        ((rows, w["qb"].shape[1]), LOW), ((8, width), F32),
    ]
    return call(
        ffn_backward_kernel, "ffn_backward", 5, outs, [], w["ffn"],
        grad_out, kept_ffn["unit"], kept_ffn["scale"], kept_ffn["slope"], kept_attention["unit"], kept_attention["scale"],
        w["heads"], w["g2"], w["g1"],
    )


def attention_backward_kernel(
    att_ref, pre_ref, q_ref, k_ref, v_ref, e_ref, inv_ref, o_ref, w_ref,
    in_out, sent_out, dq_out, dk_out, dv_out, vmask,
):
    wq, wk, wv = (w_ref[kind].reshape(-1, w_ref.shape[-1]) for kind in range(3))
    rows = att_ref.shape[0]
    heads = wq.shape[0] // HEAD_DIM
    zero = jnp.zeros((), LOW)
    first = lane_half(0)
    spare = lax.broadcasted_iota(jnp.int32, (1, LANES), 1) % HEAD_DIM
    minus = jnp.where(spare < 3, -1.0, 0.0).astype(LOW)
    for p in range(heads // 2):
        cols = slice(p * LANES, (p + 1) * LANES)
        queries, keys, values = q_ref[:, cols], k_ref[:, cols], v_ref[:, cols]
        grad = (att_ref[:, cols].astype(F32) * inv_ref[:, cols]).astype(LOW)
        dots = grad.astype(F32) * o_ref[:, cols]
        dq, dk, dv = [], [], []
        for h in range(2):
            keep = lane_half(h)
            dot = jnp.sum(jnp.where(keep, dots, 0.0), -1, keepdims=True)
            top = dot.astype(LOW)
            left = dot - top.astype(F32)
            mid = left.astype(LOW)
            end = (left - mid.astype(F32)).astype(LOW)
            pieces = jnp.where(spare == 0, top, jnp.where(spare == 1, mid, jnp.where(spare == 2, end, zero)))
            exponent = e_ref[2 * p + h]
            slot = (2 * p + h) % 4
            vmask[slot] = jnp.where(keep, values, minus)
            centered = dot_nt(jnp.where(keep, grad, pieces), vmask[slot])
            grad_scores = (exponent.astype(F32) * centered).astype(LOW)
            dq.append(dot_nn(grad_scores, keys))
            dk.append(dot_tn(grad_scores, queries))
            dv.append(dot_tn(exponent, grad))
        dq_out[:, cols] = (jnp.where(first, dq[0], dq[1]) * INV_SCALE).astype(LOW)
        dk_out[:, cols] = (jnp.where(first, dk[0], dk[1]) * INV_SCALE).astype(LOW)
        dv_out[:, cols] = jnp.where(first, dv[0], dv[1]).astype(LOW)
    dq, dk, dv = dq_out[...], dk_out[...], dv_out[...]
    sent_out[...] = (dot_nn(dk[rows:], wk) + dot_nn(dv[rows:], wv)).astype(LOW)
    in_out[...] = pre_ref[...] + dot_nn(dq, wq) + dot_nn(dk[:rows], wk) + dot_nn(dv[:rows], wv)


def attention_backward(grad_att, grad_pre, kept, w):
    rows, width = grad_pre.shape
    units = w["qb"].shape[1]
    heads = units // HEAD_DIM
    outs = [
        ((rows, width), F32), ((rows, width), LOW), ((rows, units), LOW), ((2 * rows, units), LOW), ((2 * rows, units), LOW),
    ]
    return call(
        attention_backward_kernel, "attention_backward", 12, outs,
        [((4, 2 * rows, LANES), LOW)],
        grad_att, grad_pre, kept["q"], kept["k"], kept["v"], kept["e"], kept["inv"], kept["o"], w["heads"],
    )


def both_layers(firsts, seconds):
    return sum(dot_tn(a[...], b[...]) for a, b in zip(firsts, seconds))


def ffn_grads_kernel(c, *refs):
    actives, branches, hiddens, middles, attendeds, ones_branches = (refs[2 * i : 2 * i + 2] for i in range(6))
    out, bias_out = refs[12:]
    rows, units = actives[0].shape
    step = units // 8
    ur = step // 4
    hr = attendeds[0].shape[1] // 32
    one = jnp.ones((rows, LANES), LOW)
    out_grad = both_layers(attendeds, ones_branches).astype(LOW)
    for i in range(4):
        at = 4 * c + i
        cols = slice(at * step, (at + 1) * step)
        down = both_layers([a.at[:, cols] for a in actives], branches).astype(LOW)
        up = both_layers([h.at[:, cols] for h in hiddens], middles).astype(LOW)
        bias_out[i * step : (i + 1) * step] = sum(dot_tn(h[:, cols], one) for h in hiddens).astype(LOW)
        for j in range(4):
            out[i, j, :ur] = down[j * ur : (j + 1) * ur]
            out[i, j, ur : 2 * ur] = up[j * ur : (j + 1) * ur]
            head = j * LANES + (2 * i + c) * hr
            out[i, j, 2 * ur :] = out_grad[head : head + hr]


def ffn_grads(pairs, c):
    rows, units = pairs[0][0].shape
    width = pairs[1][0].shape[1]
    ur, hr = units // 32, pairs[4][0].shape[1] // 32
    outs = [((4, 4, 2 * ur + hr, width), LOW), ((units // 2, LANES), LOW)]
    return call(functools.partial(ffn_grads_kernel, c), "ffn_grads", 3, outs, [], *[v for pair in pairs for v in pair])


def head_grads_kernel(eighth_ref, *refs):
    dqs, dks, dvs, lows, others, sums = (refs[2 * i : 2 * i + 2] for i in range(6))
    up_biases, (keep, send, shared) = refs[12:14], refs[14:]
    lane = lax.broadcasted_iota(jnp.int32, (1, LANES), 1) // (LANES // 4)
    shared[...] = sums[0][...] + sums[1][...]
    upper = lax.broadcasted_iota(jnp.int32, (16, 1), 0) < 8
    rows, units = dqs[0].shape
    hr = units // 32
    one = jnp.ones((rows, LANES), LOW)

    def halves(grads):
        own = [g.at[:rows] for g in grads]
        return own, [g.at[rows:] for g in grads]

    dk_own, dk_other = halves(dks)
    dv_own, dv_other = halves(dvs)
    grads = [
        both_layers(dqs, lows),
        both_layers(dk_own + dk_other, lows + others),
        both_layers(dv_own + dv_other, lows + others),
    ]
    grads = [g.astype(LOW) for g in grads]
    biases = [sum(dot_tn(g[...], one) for g in part).astype(LOW) for part in (dqs, dv_own + dv_other)]
    for at in range(8):
        c, i = divmod(at, 4)
        line = shared[pl.ds(eighth_ref[0] ^ (2 * i + c), 1)]
        line = jnp.where(upper, line[:, : 2 * LANES], line[:, 2 * LANES :]).astype(LOW)
        for j in range(4):
            out = keep.at[i, j] if c == 0 else send.at[4 * i + j]
            first = j * LANES + (2 * i + c) * hr
            for kind in range(3):
                out[kind * hr : (kind + 1) * hr] = grads[kind][first : first + hr]
            q, v = (bias[first : first + hr] for bias in biases)
            up_bias = up_biases[c]
            first = (4 * i + j) * (up_bias.shape[0] // 16)
            u = [up_bias[first + g * hr : first + (g + 1) * hr] for g in range(4)]
            out[3 * hr :, :LANES] = jnp.where(lane < 1, q, jnp.where(lane < 2, v, jnp.where(lane < 3, u[0], u[1])))
            out[3 * hr :, LANES : 2 * LANES] = jnp.where(lane < 1, u[2], u[3])
            out[3 * hr :, 2 * LANES :] = line


def last_backward_kernel(eighth_ref, *refs):
    given, (dq_two, dk_two, dv_two), lows, others, sums = refs[:9], refs[9:12], refs[12:14], refs[14:16], refs[16:18]
    up_biases, (in_out, keep, send, dq, dk, dv, sent_out, vmask, shared) = refs[18:20], refs[20:]
    attention_backward_kernel(*given, in_out, sent_out, dq, dk, dv, vmask)
    head_grads_kernel(eighth_ref, dq_two, dq, dk_two, dk, dv_two, dv, *lows, *others, *sums, *up_biases, keep, send, shared)
    send[16:] = sent_out[...].reshape(-1, *send.shape[1:])


def last_backward(grad_att, grad_pre, kept, w, pairs, eighth):
    rows, width = grad_pre.shape
    units = w["qb"].shape[1]
    block = 4 * (units // 32)
    outs = [((rows, width), F32), ((4, 4, block, width), LOW), ((16 + rows // block, block, width), LOW)]
    scratch = [((rows, units), LOW), ((2 * rows, units), LOW), ((2 * rows, units), LOW), ((rows, width), LOW)]
    scratch += [((4, 2 * rows, LANES), LOW), ((8, width), F32)]
    return call(
        last_backward_kernel, "last_backward", 16, outs, scratch, eighth, grad_att, grad_pre,
        kept["q"], kept["k"], kept["v"], kept["e"], kept["inv"], kept["o"], w["heads"], *pairs, scalars=1,
    )


def first_row(column):
    return column.T[:1]


def finish_kernel(ur, hr, eighth_ref, *refs):
    blocks, (down_out, up_out, out_out, up_bias) = refs[:8], refs[8:12]
    outs, biases, shared, (up_all, up_bias_all, *scratch) = refs[12:15], refs[15:17], refs[17], refs[18:]
    head = 2 * ur + hr
    for at, block in enumerate(blocks):
        c, i = divmod(at, 4)
        slot = eighth_ref[0] ^ (2 * i + c)
        units = pl.ds(pl.multiple_of(slot * ur, ur), ur)
        down_out[units] = block[:ur].astype(F32)
        up_all[units] = block[ur : 2 * ur].astype(F32)
        out_out[pl.ds(pl.multiple_of(slot * hr, hr), hr)] = block[2 * ur : 2 * ur + hr].astype(F32)
        columns = [
            jnp.broadcast_to(block[head + 3 * hr :, at : at + 1].astype(F32), (hr, LANES))
            for at in range(0, 6 * (LANES // 4), LANES // 4)
        ]
        for g in range(4):
            some = pl.ds(pl.multiple_of(slot * ur + g * hr, hr), hr)
            up_bias_all[some] = columns[2 + g]
        units = pl.ds(pl.multiple_of(slot * hr, hr), hr)
        for kind in range(3):
            scratch[kind][units] = block[head + kind * hr : head + (kind + 1) * hr].astype(F32)
        for kind in range(2):
            scratch[3 + kind][units] = columns[kind]
        line = block[head + 3 * hr :, 2 * LANES :].astype(F32)
        shared[pl.ds(slot, 1)] = jnp.concatenate((line[:1], line[8:9]), 1)
    up_out[...] = up_all[...].T
    up_bias[...] = first_row(up_bias_all[...])
    for kind in range(3):
        outs[kind][...] = scratch[kind][...].T
    for kind in range(2):
        biases[kind][...] = first_row(scratch[3 + kind][...])


def finish(own, ur, hr, eighth):
    blocks = spread(own)
    width = own.shape[1]
    outs = [((8 * ur, width), F32), ((width, 8 * ur), F32), ((8 * hr, width), F32), ((1, 8 * ur), F32)]
    outs += [((width, 8 * hr), F32)] * 3 + [((1, 8 * hr), F32)] * 2 + [((8, width), F32)]
    scratch = [((8 * ur, width), F32), ((8 * ur, LANES), F32)]
    scratch += [((8 * hr, width), F32)] * 3 + [((8 * hr, LANES), F32)] * 2
    return call(functools.partial(finish_kernel, ur, hr), "finish", 3, outs, scratch, eighth, *blocks, scalars=1)


def per_device(
    inputs, segment_ids, query_weight, query_bias, key_weight, value_weight, value_bias, out_weight, out_bias,
    first_gain, first_shift, up_weight, up_bias, down_weight, down_bias, second_gain, second_shift, cotangent,
):
    rows, width = inputs.shape
    dp, tensor = lax.axis_index("dp"), lax.axis_index("tensor")
    core, eighth = dp % 2, dp % 8
    shard_heads, shard_units = query_weight.shape[1], up_weight.shape[1]
    hr, ur = shard_heads // 8, shard_units // 8

    def columns(weight, count):
        return lax.dynamic_slice_in_dim(weight, eighth * count, count, 1).T

    def own_rows(weight, count):
        return lax.dynamic_slice_in_dim(weight, eighth * count, count, 0)

    first_in = regroup(inputs)
    flat = jnp.concatenate((query_bias, value_bias, up_bias))
    top = lax.reduce_precision(flat, 8, 7)
    mid = lax.reduce_precision(flat - top, 8, 7)
    flat = jnp.concatenate((top, mid, flat - top - mid)).astype(LOW)
    count = flat.shape[0]
    flat = jnp.pad(flat, (0, -count % (16 * width))).reshape(-1, width)
    heads_piece = jnp.concatenate(
        [columns(v, hr) for v in (query_weight, key_weight, value_weight)] + [own_rows(out_weight, hr), flat]
    )
    ffn_piece = jnp.concatenate((columns(up_weight, ur), own_rows(down_weight, ur)))
    shards = jnp.stack([heads_piece] + [swap_tensor(heads_piece, step) for step in (1, 2, 3)])
    heads_own = spread_plane(shards[:, : 4 * hr])
    ffn_own = spread_plane(join_shards(ffn_piece))
    first_in, *heads_own = lax.optimization_barrier((first_in, *heads_own))
    head_blocks = heads_own + [swap_dp(block, 1) for block in heads_own]
    flat = shards[:, 4 * hr :].reshape(4, -1)[:, :count].astype(F32)
    flat = jnp.sum(flat.reshape(4, 3, -1), 1)
    seq = lax.dynamic_slice_in_dim(segment_ids, (tensor // 2) * LEN, LEN)
    seq = jnp.where(core == tensor % 2, seq, swap_dp(seq, 1))
    labels_own = lax.dynamic_slice_in_dim(seq, core * rows, rows)
    labels_all = jnp.concatenate((labels_own, lax.dynamic_slice_in_dim(seq, (1 - core) * rows, rows)))
    code = jnp.arange(LANES) % HEAD_DIM - 1
    mark = (labels_own[:, None] == code).astype(LOW)
    barred = jnp.where(labels_all[:, None] == code, 0.0, BARRED).astype(LOW)

    def bias(start, count):
        return relative_blocks(flat[:, start : start + count].reshape(4, 2, 2, 2, -1))

    w = {
        "qb": bias(0, shard_heads).reshape(1, -1), "vb": bias(shard_heads, shard_heads).reshape(1, -1),
        "upb": bias(2 * shard_heads, shard_units).reshape(4, 4, 2, ur).transpose(2, 1, 0, 3).reshape(1, -1),
        "ob": out_bias[None], "g1": first_gain[None], "s1": first_shift[None], "db": down_bias[None],
        "g2": second_gain[None], "s2": second_shift[None],
    }

    kept = []
    layer_in, low = first_in, first_in
    for position in range(2):
        other = swap_dp(low, 1)
        made = attention_forward(layer_in, low, other, mark, barred, w, None if position else head_blocks)
        q, k, v, e, inv, o, attended, unit_one, scale_one, middle = made[:10]
        if position == 0:
            w["heads"] = made[10]
            middle, cotangent, *ffn_own = lax.optimization_barrier((middle, cotangent, *ffn_own))
            ffn_blocks = ffn_own + [swap_dp(block, 1) for block in ffn_own]
        made = ffn_forward(middle, w, None if position else ffn_blocks)
        middle_low, active, slope, unit_two, scale_two, layer_out, next_low = made[:7]
        if position == 0:
            w["ffn"] = made[7]
        attention = {"q": q, "k": k, "v": v, "e": e, "inv": inv, "o": o, "unit": unit_one, "scale": scale_one, "att": attended}
        ffn = {"slope": slope, "unit": unit_two, "scale": scale_two}
        kept.append((attention, ffn, low, other, middle_low, active))
        layer_in, low = layer_out, next_low
    result = regroup(low)

    grad_flow = regroup(cotangent)
    at = jnp.reshape(eighth, (1,)).astype(jnp.int32)
    attention_two, ffn, low_two, other_two, middle_low, active = kept[1]
    branch_two, grad_hidden, grad_pre, branch_one, grad_att, six_two = ffn_backward(grad_flow, ffn, attention_two, w)
    pairs_two = (active, branch_two, grad_hidden, middle_low, attention_two["att"], branch_one)
    grad_in, sent, dq, dk, dv = attention_backward(grad_att, grad_pre, attention_two, w)
    grad_in, result = lax.optimization_barrier((grad_in, result))
    grad_flow = grad_in + swap_dp(sent, 1).astype(F32)

    attention, ffn, low, low_other, middle_low, active = kept[0]
    branch_two, grad_hidden, grad_pre, branch_one, grad_att, six = ffn_backward(grad_flow, ffn, attention, w)
    pairs_one = (active, branch_two, grad_hidden, middle_low, attention["att"], branch_one)
    ffn_pairs = list(zip(pairs_two, pairs_one))
    send, other_columns = ffn_grads(ffn_pairs, 1)
    other = swap_dp(send, 1)
    keep, own_columns = ffn_grads(ffn_pairs, 0)
    near, near_sent, far, far_sent = pair_halves(keep, other)
    grad_att, near_sent, far_sent = lax.optimization_barrier((grad_att, near_sent, far_sent))
    near_got, far_got = swap_dp(near_sent, 2), swap_dp(far_sent, 4)
    grad_in, keep, send = last_backward(
        grad_att, grad_pre, attention, w,
        (dq, dk, dv, low_two, low, other_two, low_other, six_two, six, own_columns, other_columns), at,
    )
    keep, send, near_got, far_got = lax.optimization_barrier((keep, send, near_got, far_got))
    (near, near_sent), (far, far_sent) = add_halves(near, near_got), add_halves(far, far_got)
    near_sent, far_sent, send = lax.optimization_barrier((near_sent, far_sent, send))
    near_got, far_got = swap_dp(near_sent, 4), swap_dp(far_sent, 2)
    other = swap_dp(send, 1)
    grad_low = (grad_in + other[16:].reshape(rows, width).astype(F32)).astype(LOW)
    near_head, near_sent, far_head, far_sent = pair_halves(keep, other[:16].reshape(keep.shape))
    near_head_got, far_head_got = lax.optimization_barrier((swap_dp(near_sent, 2), swap_dp(far_sent, 4)))
    (near_head, near_sent), (far_head, far_sent) = add_halves(near_head, near_head_got), add_halves(far_head, far_head_got)
    near_head_got, far_head_got = swap_dp(near_sent, 4), swap_dp(far_sent, 2)
    ffn_parts = swap_shards(add_shards(near, near_got, far, far_got))
    ffn_parts = lax.optimization_barrier((*ffn_parts, near_head_got, far_head_got))[:4]
    ffn_own = sum_shards(ffn_parts)
    head_own = sum_shards(swap_shards(add_shards(near_head, near_head_got, far_head, far_head_got)))
    own = jnp.concatenate((ffn_own, head_own))
    own, grad_low = lax.optimization_barrier((own, grad_low))
    input_grad = regroup(grad_low).astype(F32)
    (
        down_grad, up_grad, out_grad, up_bias_grad, q_grad, k_grad, v_grad, q_bias_grad, v_bias_grad, shared,
    ) = finish(own, ur, hr, at)
    return (
        result, input_grad, q_grad, q_bias_grad[0], k_grad, v_grad, v_bias_grad[0], out_grad, shared[5], shared[3], shared[4],
        up_grad, up_bias_grad[0], down_grad, shared[2], shared[0], shared[1],
    )


def solution(mesh):
    split = P(("dp", "tensor"), None)
    columns, rows, part = P(None, "tensor"), P("tensor", None), P("tensor")
    return jax.shard_map(
        per_device,
        mesh=mesh,
        in_specs=(
            split, P("dp"), columns, part, columns, columns, part, rows, P(), P(), P(), columns, part, rows, P(), P(),
            P(), split,
        ),
        out_specs=(
            split, split, columns, part, columns, columns, part, rows, P(), P(), P(), columns, part, rows, P(), P(), P(),
        ),
        check_vma=False,
    )
```

```python
import functools
import math

import jax
import jax.numpy as jnp
from jax import lax
from jax.experimental import pallas as pl
from jax.experimental.pallas import tpu as pltpu
from jax.sharding import PartitionSpec as P

HEAD_DIM = 64
LEN = 1024
EPS = 1e-05
LANES = 128
LOW = jnp.bfloat16
F32 = jnp.float32
EXP2_SCALE = math.log2(math.e) / math.sqrt(HEAD_DIM)
INV_SCALE = 1.0 / math.sqrt(HEAD_DIM)
BARRED = -1e9


def swap_dp(value, bits):
    count = lax.axis_size("dp")
    return lax.ppermute(value, "dp", [(i, i ^ bits) for i in range(count)])


def swap_tensor(value, step):
    count = lax.axis_size("tensor")
    return lax.ppermute(value, "tensor", [(i, i ^ step) for i in range(count)])


def regroup(block):
    dp, tensor = lax.axis_size("dp"), lax.axis_size("tensor")
    pairs = [
        ((2 * k + c) * tensor + 2 * a + b, (2 * k + b) * tensor + 2 * a + c)
        for k in range(dp // 2)
        for c in range(2)
        for a in range(tensor // 2)
        for b in range(2)
        if b != c
    ]
    moved = lax.ppermute(block, ("dp", "tensor"), pairs)
    stays = (lax.axis_index("dp") % 2) == (lax.axis_index("tensor") % 2)
    return jnp.where(stays, block, moved)


def join_shards(piece):
    pieces = jnp.stack((piece, swap_tensor(piece, 2)))
    other = swap_tensor(pieces, 1)
    return jnp.stack((pieces[0], other[0], pieces[1], other[1]))


def spread_plane(block):
    return [block] + [swap_dp(block, bits) for bits in (2, 4, 6)]


def sum_parts(parts):
    total = parts[0].astype(F32)
    for part in parts[1:]:
        total = total + part.astype(F32)
    return total


def pair_halves(keep, other):
    def pair(first, second, shards):
        return jnp.stack([sum_parts((keep[i, shards], other[i, shards])).astype(LOW) for i in (first, second)])

    near, far = slice(0, 2), slice(2, 4)
    return pair(0, 2, near), pair(1, 3, near), pair(0, 1, far), pair(2, 3, far)


def add_halves(kept, got):
    return [sum_parts((kept[i], got[i])).astype(LOW) for i in range(2)]


def add_shards(near, near_got, far, far_got):
    return [sum_parts((a[j], b[j])).astype(LOW) for a, b in ((near, near_got), (far, far_got)) for j in range(2)]


def swap_shards(parts):
    return [parts[0]] + [swap_tensor(parts[j], j) for j in (1, 2, 3)]


def sum_shards(parts):
    total = sum_parts(parts)
    bits = 8
    while bits < lax.axis_size("dp"):
        total = total + swap_dp(total.astype(LOW), bits).astype(F32)
        bits *= 2
    return total.astype(LOW)


def flip(value, axis, wanted):
    return jnp.where(wanted, jnp.flip(value, axis), value)


def relative_blocks(blocks):
    dp = lax.axis_index("dp")
    return flip(flip(flip(blocks, 3, (dp & 1) != 0), 2, (dp & 2) != 0), 1, (dp & 4) != 0)


def dot_nt(a, b):
    return lax.dot_general(a, b, (((1,), (1,)), ((), ())), preferred_element_type=F32)


def dot_tn(a, b):
    return lax.dot_general(a, b, (((0,), (0,)), ((), ())), preferred_element_type=F32)


def dot_nn(a, b):
    return jnp.dot(a, b, preferred_element_type=F32)


def norm(value):
    center = value - jnp.mean(value, -1, keepdims=True)
    scale = lax.rsqrt(jnp.mean(center * center, -1, keepdims=True) + EPS)
    return center * scale, scale


def norm_back(grad, gain, unit, scale):
    scaled = grad * gain
    mean_a = jnp.mean(scaled, -1, keepdims=True)
    mean_b = jnp.mean(scaled * unit, -1, keepdims=True)
    return (scaled - mean_a - unit * mean_b) * scale


def lane_half(which):
    first = lax.broadcasted_iota(jnp.int32, (1, LANES), 1) < HEAD_DIM
    return first if which == 0 else jnp.logical_not(first)


VMEM_MIB = {
    "attention_first": 10, "attention_forward": 10, "ffn_first": 5, "ffn_forward": 5, "ffn_backward": 4, "ffn_grads": 3,
    "attention_backward": 6, "last_backward": 10, "finish": 7,
}


def call(kernel, name, micros, outs, scratch, *operands, scalars=0, far=0):
    spaces = [pltpu.SMEM] * scalars + [pl.ANY] * far + [pltpu.VMEM] * (len(operands) - scalars - far)
    return pl.pallas_call(
        kernel,
        in_specs=[pl.BlockSpec(memory_space=space) for space in spaces],
        out_specs=[pl.BlockSpec(memory_space=pltpu.VMEM)] * len(outs),
        out_shape=[jax.ShapeDtypeStruct(shape, dtype) for shape, dtype in outs],
        scratch_shapes=[pltpu.VMEM(*s) if isinstance(s, tuple) else s for s in scratch],
        compiler_params=pltpu.CompilerParams(vmem_limit_bytes=VMEM_MIB[name] * 2**20),
        cost_estimate=pl.CostEstimate(flops=int(micros * 1.1e9), bytes_accessed=0, transcendentals=0),
        name=name,
    )(*operands)


def attention_first_kernel(*refs):
    blocks, rest, w_out, scratch, sems = refs[:8], refs[8:-4], refs[-4], refs[-3:-1], refs[-1]
    copies = []
    for at, block in enumerate(blocks):
        c, i = divmod(at, 4)
        rows = block.shape[1] // 4
        for kind in range(4):
            source = block.at[:, kind * rows : (kind + 1) * rows]
            copies.append(pltpu.make_async_copy(source, w_out.at[kind, :, 2 * i + c], sems.at[at, kind]))
    for copy in copies:
        copy.start()
    for copy in copies:
        copy.wait()
    attention_forward_kernel(*rest[:5], w_out, *rest[5:], *scratch)


def attention_forward_kernel(
    in_ref, low_ref, other_ref, mark_ref, barred_ref, w_ref, qb, vb, ob, gain, shift,
    q_out, k_out, v_out, e_out, inv_out, o_out, att_out, unit_out, scale_out, mid_out, kmask, vmask,
):
    rows = in_ref.shape[0]
    wq, wk, wv, wo = (w_ref[kind].reshape(-1, w_ref.shape[-1]) for kind in range(4))
    heads = wq.shape[0] // HEAD_DIM
    zero = jnp.zeros((), LOW)
    low = low_ref[...]
    q_out[...] = (dot_nt(low, wq) + qb[...]).astype(LOW)
    for half, part in enumerate((low, other_ref[...])):
        r = slice(half * rows, (half + 1) * rows)
        k_out[r] = dot_nt(part, wk).astype(LOW)
        v_out[r] = (dot_nt(part, wv) + vb[...]).astype(LOW)
    mark = mark_ref[...]
    first = lane_half(0)
    for p in range(heads // 2):
        cols = slice(p * LANES, (p + 1) * LANES)
        keys, values = k_out[:, cols], v_out[:, cols]
        scaled = q_out[:, cols].astype(F32) * EXP2_SCALE
        high = scaled.astype(LOW)
        rest = (scaled - high.astype(F32)).astype(LOW)
        mixed = []
        for h in range(2):
            keep = lane_half(h)
            query = jnp.concatenate((jnp.where(keep, high, mark), jnp.where(keep, rest, zero)), 1)
            slot = (2 * p + h) % 4
            kmask[slot, :, :LANES] = jnp.where(keep, keys, barred_ref[...])
            kmask[slot, :, LANES:] = jnp.where(keep, keys, zero)
            vmask[slot] = jnp.where(keep, values, jnp.ones((), LOW))
            scores = dot_nt(query, kmask[slot])
            exponent = jnp.exp2(scores - jnp.max(scores, -1, keepdims=True)).astype(LOW)
            e_out[2 * p + h] = exponent
            mixed.append(dot_nn(exponent, vmask[slot]))
        inv = 1.0 / pltpu.roll(jnp.where(first, mixed[1], mixed[0]), HEAD_DIM, 1)
        attended = jnp.where(first, mixed[0], mixed[1]) * inv
        inv_out[:, cols] = inv
        o_out[:, cols] = attended
        att_out[:, cols] = attended.astype(LOW)
    unit, scale = norm(in_ref[...].astype(F32) + dot_nn(att_out[...], wo) + ob[...])
    unit_out[...] = unit
    scale_out[...] = jnp.broadcast_to(scale, scale_out.shape)
    mid_out[...] = unit * gain[...] + shift[...]


def attention_forward(layer_in, low, other, mark, barred, w, blocks=None):
    rows, width = layer_in.shape
    units = w["qb"].shape[1]
    heads = units // HEAD_DIM
    outs = [
        ((rows, units), LOW), ((2 * rows, units), LOW), ((2 * rows, units), LOW), ((heads, rows, 2 * rows), LOW),
        ((rows, units), F32), ((rows, units), F32), ((rows, units), LOW), ((rows, width), F32), ((rows, LANES), F32),
        ((rows, width), F32),
    ]
    scratch = [((4, 2 * rows, 2 * LANES), LOW), ((4, 2 * rows, LANES), LOW)]
    tail = (w["qb"], w["vb"], w["ob"], w["g1"], w["s1"])
    first = (layer_in, low, other, mark, barred)
    if blocks is None:
        return call(attention_forward_kernel, "attention_forward", 8, outs, scratch, *first, w["heads"], *tail)
    scratch.append(pltpu.SemaphoreType.DMA((8, 4)))
    outs.append(((4, 4, 8, units // 32, width), LOW))
    return call(attention_first_kernel, "attention_first", 9, outs, scratch, *blocks, *first, *tail, far=8)


GELU_A = math.sqrt(2.0 / math.pi)
GELU_B = 0.044715


def ffn_first_kernel(*refs):
    blocks, rest, w_out, sems = refs[:8], refs[8:-2], refs[-2], refs[-1]
    copies = []
    for at, block in enumerate(blocks):
        rows = block.shape[1] // 2
        for kind in range(2):
            source = block.at[:, kind * rows : (kind + 1) * rows]
            copies.append(pltpu.make_async_copy(source, w_out.at[kind, at], sems.at[at, kind]))
    for copy in copies:
        copy.start()
    for copy in copies:
        copy.wait()
    ffn_forward_kernel(rest[0], w_out, *rest[1:])


def unit_blocks(w_ref):
    count = w_ref.shape[2] * w_ref.shape[3] * 2
    for at in range(4):
        up, down = (w_ref[kind, 2 * at : 2 * at + 2].reshape(count, -1) for kind in range(2))
        yield slice(at * count, (at + 1) * count), up, down


def ffn_forward_kernel(
    mid_ref, w_ref, upb, db, gain, shift, low_out, act_out, slope_out, unit_out, scale_out, out_out, next_out
):
    middle = mid_ref[...]
    low = middle.astype(LOW)
    low_out[...] = low
    total = middle + db[...]
    for r, up, down in unit_blocks(w_ref):
        hidden = dot_nt(low, up) + upb[:, r]
        square = hidden * hidden
        bent = jnp.tanh(hidden * (GELU_A + GELU_A * GELU_B * square))
        half = 0.5 + 0.5 * bent
        active = (hidden * half).astype(LOW)
        act_out[:, r] = active
        inner = GELU_A + 3.0 * GELU_A * GELU_B * square
        slope_out[:, r] = (half + 0.5 * hidden * (1.0 - bent * bent) * inner).astype(LOW)
        total = total + dot_nn(active, down)
    unit, scale = norm(total)
    unit_out[...] = unit
    scale_out[...] = jnp.broadcast_to(scale, scale_out.shape)
    layer_out = unit * gain[...] + shift[...]
    out_out[...] = layer_out
    next_out[...] = layer_out.astype(LOW)


def ffn_forward(middle, w, blocks=None):
    rows, width = middle.shape
    units = w["upb"].shape[1]
    outs = [
        ((rows, width), LOW), ((rows, units), LOW), ((rows, units), LOW), ((rows, width), F32), ((rows, LANES), F32),
        ((rows, width), F32), ((rows, width), LOW),
    ]
    tail = (w["upb"], w["db"], w["g2"], w["s2"])
    if blocks is None:
        return call(ffn_forward_kernel, "ffn_forward", 5, outs, [], middle, w["ffn"], *tail)
    outs.append(((2, 8, 4, units // 32, width), LOW))
    scratch = [pltpu.SemaphoreType.DMA((8, 2))]
    return call(ffn_first_kernel, "ffn_first", 6, outs, scratch, *blocks, middle, *tail, far=8)


def row_sum(value):
    return jnp.sum(value, 0, keepdims=True)


def ffn_backward_kernel(
    w_ref, grad_ref, unit_two, scale_two, slope, unit_one, scale_one, heads_ref, gain_two, gain_one,
    branch_two_out, hidden_out, pre_one_out, branch_one_out, att_out, sums_out,
):
    grad = grad_ref[...].astype(F32)
    unit = unit_two[...]
    sums_out[0:1] = row_sum(grad * unit)
    sums_out[1:2] = row_sum(grad)
    grad_pre = norm_back(grad, gain_two[...], unit, scale_two[:, :1])
    branch = grad_pre.astype(LOW)
    branch_two_out[...] = branch
    sums_out[2:3] = row_sum(branch.astype(F32))
    grad_middle = grad_pre
    for r, up, down in unit_blocks(w_ref):
        hidden = (dot_nt(branch, down) * slope[:, r].astype(F32)).astype(LOW)
        hidden_out[:, r] = hidden
        grad_middle = grad_middle + dot_nn(hidden, up)
    unit = unit_one[...]
    sums_out[3:4] = row_sum(grad_middle * unit)
    sums_out[4:5] = row_sum(grad_middle)
    grad_pre = norm_back(grad_middle, gain_one[...], unit, scale_one[:, :1])
    pre_one_out[...] = grad_pre
    branch = grad_pre.astype(LOW)
    branch_one_out[...] = branch
    sums_out[5:6] = row_sum(branch.astype(F32))
    sums_out[6:8] = jnp.zeros((2, grad.shape[1]), F32)
    att_out[...] = dot_nt(branch, heads_ref[3].reshape(-1, grad.shape[1])).astype(LOW)


def ffn_backward(grad_out, kept_ffn, kept_attention, w):
    rows, width = grad_out.shape
    units = w["upb"].shape[1]
    outs = [
        ((rows, width), LOW), ((rows, units), LOW), ((rows, width), F32), ((rows, width), LOW),
        ((rows, w["qb"].shape[1]), LOW), ((8, width), F32),
    ]
    return call(
        ffn_backward_kernel, "ffn_backward", 5, outs, [], w["ffn"],
        grad_out, kept_ffn["unit"], kept_ffn["scale"], kept_ffn["slope"], kept_attention["unit"], kept_attention["scale"],
        w["heads"], w["g2"], w["g1"],
    )


def attention_backward_kernel(
    att_ref, pre_ref, q_ref, k_ref, v_ref, e_ref, inv_ref, o_ref, w_ref,
    in_out, sent_out, dq_out, dk_out, dv_out, vmask,
):
    wq, wk, wv = (w_ref[kind].reshape(-1, w_ref.shape[-1]) for kind in range(3))
    rows = att_ref.shape[0]
    heads = wq.shape[0] // HEAD_DIM
    zero = jnp.zeros((), LOW)
    first = lane_half(0)
    spare = lax.broadcasted_iota(jnp.int32, (1, LANES), 1) % HEAD_DIM
    minus = jnp.where(spare < 3, -1.0, 0.0).astype(LOW)
    for p in range(heads // 2):
        cols = slice(p * LANES, (p + 1) * LANES)
        queries, keys, values = q_ref[:, cols], k_ref[:, cols], v_ref[:, cols]
        grad = (att_ref[:, cols].astype(F32) * inv_ref[:, cols]).astype(LOW)
        dots = grad.astype(F32) * o_ref[:, cols]
        dq, dk, dv = [], [], []
        for h in range(2):
            keep = lane_half(h)
            dot = jnp.sum(jnp.where(keep, dots, 0.0), -1, keepdims=True)
            top = dot.astype(LOW)
            left = dot - top.astype(F32)
            mid = left.astype(LOW)
            end = (left - mid.astype(F32)).astype(LOW)
            pieces = jnp.where(spare == 0, top, jnp.where(spare == 1, mid, jnp.where(spare == 2, end, zero)))
            exponent = e_ref[2 * p + h]
            slot = (2 * p + h) % 4
            vmask[slot] = jnp.where(keep, values, minus)
            centered = dot_nt(jnp.where(keep, grad, pieces), vmask[slot])
            grad_scores = (exponent.astype(F32) * centered).astype(LOW)
            dq.append(dot_nn(grad_scores, keys))
            dk.append(dot_tn(grad_scores, queries))
            dv.append(dot_tn(exponent, grad))
        dq_out[:, cols] = (jnp.where(first, dq[0], dq[1]) * INV_SCALE).astype(LOW)
        dk_out[:, cols] = (jnp.where(first, dk[0], dk[1]) * INV_SCALE).astype(LOW)
        dv_out[:, cols] = jnp.where(first, dv[0], dv[1]).astype(LOW)
    dq, dk, dv = dq_out[...], dk_out[...], dv_out[...]
    sent_out[...] = (dot_nn(dk[rows:], wk) + dot_nn(dv[rows:], wv)).astype(LOW)
    in_out[...] = pre_ref[...] + dot_nn(dq, wq) + dot_nn(dk[:rows], wk) + dot_nn(dv[:rows], wv)


def attention_backward(grad_att, grad_pre, kept, w):
    rows, width = grad_pre.shape
    units = w["qb"].shape[1]
    heads = units // HEAD_DIM
    outs = [
        ((rows, width), F32), ((rows, width), LOW), ((rows, units), LOW), ((2 * rows, units), LOW), ((2 * rows, units), LOW),
    ]
    return call(
        attention_backward_kernel, "attention_backward", 12, outs,
        [((4, 2 * rows, LANES), LOW)],
        grad_att, grad_pre, kept["q"], kept["k"], kept["v"], kept["e"], kept["inv"], kept["o"], w["heads"],
    )


def both_layers(firsts, seconds):
    return sum(dot_tn(a[...], b[...]) for a, b in zip(firsts, seconds))


def ffn_grads_kernel(c, *refs):
    actives, branches, hiddens, middles, attendeds, ones_branches = (refs[2 * i : 2 * i + 2] for i in range(6))
    out, bias_out = refs[12:]
    rows, units = actives[0].shape
    step = units // 8
    ur = step // 4
    hr = attendeds[0].shape[1] // 32
    one = jnp.ones((rows, LANES), LOW)
    out_grad = both_layers(attendeds, ones_branches).astype(LOW)
    for i in range(4):
        at = 4 * c + i
        cols = slice(at * step, (at + 1) * step)
        down = both_layers([a.at[:, cols] for a in actives], branches).astype(LOW)
        up = both_layers([h.at[:, cols] for h in hiddens], middles).astype(LOW)
        bias_out[i * step : (i + 1) * step] = sum(dot_tn(h[:, cols], one) for h in hiddens).astype(LOW)
        for j in range(4):
            out[i, j, :ur] = down[j * ur : (j + 1) * ur]
            out[i, j, ur : 2 * ur] = up[j * ur : (j + 1) * ur]
            head = j * LANES + (2 * i + c) * hr
            out[i, j, 2 * ur :] = out_grad[head : head + hr]


def ffn_grads(pairs, c):
    rows, units = pairs[0][0].shape
    width = pairs[1][0].shape[1]
    ur, hr = units // 32, pairs[4][0].shape[1] // 32
    outs = [((4, 4, 2 * ur + hr, width), LOW), ((units // 2, LANES), LOW)]
    return call(functools.partial(ffn_grads_kernel, c), "ffn_grads", 3, outs, [], *[v for pair in pairs for v in pair])


def head_grads_kernel(eighth_ref, *refs):
    dqs, dks, dvs, lows, others, sums = (refs[2 * i : 2 * i + 2] for i in range(6))
    up_biases, (keep, send, shared) = refs[12:14], refs[14:]
    lane = lax.broadcasted_iota(jnp.int32, (1, LANES), 1) // (LANES // 4)
    shared[...] = sums[0][...] + sums[1][...]
    upper = lax.broadcasted_iota(jnp.int32, (16, 1), 0) < 8
    rows, units = dqs[0].shape
    hr = units // 32
    one = jnp.ones((rows, LANES), LOW)

    def halves(grads):
        own = [g.at[:rows] for g in grads]
        return own, [g.at[rows:] for g in grads]

    dk_own, dk_other = halves(dks)
    dv_own, dv_other = halves(dvs)
    grads = [
        both_layers(dqs, lows),
        both_layers(dk_own + dk_other, lows + others),
        both_layers(dv_own + dv_other, lows + others),
    ]
    grads = [g.astype(LOW) for g in grads]
    biases = [sum(dot_tn(g[...], one) for g in part).astype(LOW) for part in (dqs, dv_own + dv_other)]
    for at in range(8):
        c, i = divmod(at, 4)
        line = shared[pl.ds(eighth_ref[0] ^ (2 * i + c), 1)]
        line = jnp.where(upper, line[:, : 2 * LANES], line[:, 2 * LANES :]).astype(LOW)
        for j in range(4):
            out = keep.at[i, j] if c == 0 else send.at[4 * i + j]
            first = j * LANES + (2 * i + c) * hr
            for kind in range(3):
                out[kind * hr : (kind + 1) * hr] = grads[kind][first : first + hr]
            q, v = (bias[first : first + hr] for bias in biases)
            up_bias = up_biases[c]
            first = (4 * i + j) * (up_bias.shape[0] // 16)
            u = [up_bias[first + g * hr : first + (g + 1) * hr] for g in range(4)]
            out[3 * hr :, :LANES] = jnp.where(lane < 1, q, jnp.where(lane < 2, v, jnp.where(lane < 3, u[0], u[1])))
            out[3 * hr :, LANES : 2 * LANES] = jnp.where(lane < 1, u[2], u[3])
            out[3 * hr :, 2 * LANES :] = line


def last_backward_kernel(eighth_ref, *refs):
    given, (dq_two, dk_two, dv_two), lows, others, sums = refs[:9], refs[9:12], refs[12:14], refs[14:16], refs[16:18]
    up_biases, (in_out, keep, send, dq, dk, dv, sent_out, vmask, shared) = refs[18:20], refs[20:]
    attention_backward_kernel(*given, in_out, sent_out, dq, dk, dv, vmask)
    head_grads_kernel(eighth_ref, dq_two, dq, dk_two, dk, dv_two, dv, *lows, *others, *sums, *up_biases, keep, send, shared)
    send[16:] = sent_out[...].reshape(-1, *send.shape[1:])


def last_backward(grad_att, grad_pre, kept, w, pairs, eighth):
    rows, width = grad_pre.shape
    units = w["qb"].shape[1]
    block = 4 * (units // 32)
    outs = [((rows, width), F32), ((4, 4, block, width), LOW), ((16 + rows // block, block, width), LOW)]
    scratch = [((rows, units), LOW), ((2 * rows, units), LOW), ((2 * rows, units), LOW), ((rows, width), LOW)]
    scratch += [((4, 2 * rows, LANES), LOW), ((8, width), F32)]
    return call(
        last_backward_kernel, "last_backward", 16, outs, scratch, eighth, grad_att, grad_pre,
        kept["q"], kept["k"], kept["v"], kept["e"], kept["inv"], kept["o"], w["heads"], *pairs, scalars=1,
    )


def first_row(column):
    return column.T[:1]


def finish_kernel(ur, hr, eighth_ref, *refs):
    blocks, (down_out, up_out, out_out, up_bias) = refs[:8], refs[8:12]
    outs, biases, shared, (up_all, up_bias_all, *scratch) = refs[12:15], refs[15:17], refs[17], refs[18:]
    head = 2 * ur + hr
    for at, block in enumerate(blocks):
        c, i = divmod(at, 4)
        slot = eighth_ref[0] ^ (2 * i + c)
        units = pl.ds(pl.multiple_of(slot * ur, ur), ur)
        down_out[units] = block[:ur].astype(F32)
        up_all[units] = block[ur : 2 * ur].astype(F32)
        out_out[pl.ds(pl.multiple_of(slot * hr, hr), hr)] = block[2 * ur : 2 * ur + hr].astype(F32)
        columns = [
            jnp.broadcast_to(block[head + 3 * hr :, at : at + 1].astype(F32), (hr, LANES))
            for at in range(0, 6 * (LANES // 4), LANES // 4)
        ]
        for g in range(4):
            some = pl.ds(pl.multiple_of(slot * ur + g * hr, hr), hr)
            up_bias_all[some] = columns[2 + g]
        units = pl.ds(pl.multiple_of(slot * hr, hr), hr)
        for kind in range(3):
            scratch[kind][units] = block[head + kind * hr : head + (kind + 1) * hr].astype(F32)
        for kind in range(2):
            scratch[3 + kind][units] = columns[kind]
        line = block[head + 3 * hr :, 2 * LANES :].astype(F32)
        shared[pl.ds(slot, 1)] = jnp.concatenate((line[:1], line[8:9]), 1)
    up_out[...] = up_all[...].T
    up_bias[...] = first_row(up_bias_all[...])
    for kind in range(3):
        outs[kind][...] = scratch[kind][...].T
    for kind in range(2):
        biases[kind][...] = first_row(scratch[3 + kind][...])


def finish(blocks, ur, hr, eighth):
    width = blocks[0].shape[1]
    outs = [((8 * ur, width), F32), ((width, 8 * ur), F32), ((8 * hr, width), F32), ((1, 8 * ur), F32)]
    outs += [((width, 8 * hr), F32)] * 3 + [((1, 8 * hr), F32)] * 2 + [((8, width), F32)]
    scratch = [((8 * ur, width), F32), ((8 * ur, LANES), F32)]
    scratch += [((8 * hr, width), F32)] * 3 + [((8 * hr, LANES), F32)] * 2
    return call(functools.partial(finish_kernel, ur, hr), "finish", 3, outs, scratch, eighth, *blocks, scalars=1)


def per_device(
    inputs, segment_ids, query_weight, query_bias, key_weight, value_weight, value_bias, out_weight, out_bias,
    first_gain, first_shift, up_weight, up_bias, down_weight, down_bias, second_gain, second_shift, cotangent,
):
    rows, width = inputs.shape
    dp, tensor = lax.axis_index("dp"), lax.axis_index("tensor")
    core, eighth = dp % 2, dp % 8
    shard_heads, shard_units = query_weight.shape[1], up_weight.shape[1]
    hr, ur = shard_heads // 8, shard_units // 8

    def columns(weight, count):
        return lax.dynamic_slice_in_dim(weight, eighth * count, count, 1).T

    def own_rows(weight, count):
        return lax.dynamic_slice_in_dim(weight, eighth * count, count, 0)

    first_in = regroup(inputs)
    flat = jnp.concatenate((query_bias, value_bias, up_bias))
    top = lax.reduce_precision(flat, 8, 7)
    mid = lax.reduce_precision(flat - top, 8, 7)
    flat = jnp.concatenate((top, mid, flat - top - mid)).astype(LOW)
    count = flat.shape[0]
    flat = jnp.pad(flat, (0, -count % (16 * width))).reshape(-1, width)
    heads_piece = jnp.concatenate(
        [columns(v, hr) for v in (query_weight, key_weight, value_weight)] + [own_rows(out_weight, hr), flat]
    )
    ffn_piece = jnp.concatenate((columns(up_weight, ur), own_rows(down_weight, ur)))
    shards = jnp.stack([heads_piece] + [swap_tensor(heads_piece, step) for step in (1, 2, 3)])
    heads_own = spread_plane(shards[:, : 4 * hr])
    ffn_own = spread_plane(join_shards(ffn_piece))
    first_in, *heads_own = lax.optimization_barrier((first_in, *heads_own))
    head_blocks = heads_own + [swap_dp(block, 1) for block in heads_own]
    flat = shards[:, 4 * hr :].reshape(4, -1)[:, :count].astype(F32)
    flat = jnp.sum(flat.reshape(4, 3, -1), 1)
    seq = lax.dynamic_slice_in_dim(segment_ids, (tensor // 2) * LEN, LEN)
    seq = jnp.where(core == tensor % 2, seq, swap_dp(seq, 1))
    labels_own = lax.dynamic_slice_in_dim(seq, core * rows, rows)
    labels_all = jnp.concatenate((labels_own, lax.dynamic_slice_in_dim(seq, (1 - core) * rows, rows)))
    code = jnp.arange(LANES) % HEAD_DIM - 1
    mark = (labels_own[:, None] == code).astype(LOW)
    barred = jnp.where(labels_all[:, None] == code, 0.0, BARRED).astype(LOW)

    def bias(start, count):
        return relative_blocks(flat[:, start : start + count].reshape(4, 2, 2, 2, -1))

    w = {
        "qb": bias(0, shard_heads).reshape(1, -1), "vb": bias(shard_heads, shard_heads).reshape(1, -1),
        "upb": bias(2 * shard_heads, shard_units).reshape(4, 4, 2, ur).transpose(2, 1, 0, 3).reshape(1, -1),
        "ob": out_bias[None], "g1": first_gain[None], "s1": first_shift[None], "db": down_bias[None],
        "g2": second_gain[None], "s2": second_shift[None],
    }

    kept = []
    layer_in, low = first_in, first_in
    for position in range(2):
        other = swap_dp(low, 1)
        made = attention_forward(layer_in, low, other, mark, barred, w, None if position else head_blocks)
        q, k, v, e, inv, o, attended, unit_one, scale_one, middle = made[:10]
        if position == 0:
            w["heads"] = made[10]
            middle, cotangent, *ffn_own = lax.optimization_barrier((middle, cotangent, *ffn_own))
            ffn_blocks = ffn_own + [swap_dp(block, 1) for block in ffn_own]
        made = ffn_forward(middle, w, None if position else ffn_blocks)
        middle_low, active, slope, unit_two, scale_two, layer_out, next_low = made[:7]
        if position == 0:
            w["ffn"] = made[7]
        attention = {"q": q, "k": k, "v": v, "e": e, "inv": inv, "o": o, "unit": unit_one, "scale": scale_one, "att": attended}
        ffn = {"slope": slope, "unit": unit_two, "scale": scale_two}
        kept.append((attention, ffn, low, other, middle_low, active))
        layer_in, low = layer_out, next_low
    result = regroup(low)

    grad_flow = regroup(cotangent)
    at = jnp.reshape(eighth, (1,)).astype(jnp.int32)
    attention_two, ffn, low_two, other_two, middle_low, active = kept[1]
    branch_two, grad_hidden, grad_pre, branch_one, grad_att, six_two = ffn_backward(grad_flow, ffn, attention_two, w)
    pairs_two = (active, branch_two, grad_hidden, middle_low, attention_two["att"], branch_one)
    grad_in, sent, dq, dk, dv = attention_backward(grad_att, grad_pre, attention_two, w)
    grad_in, result = lax.optimization_barrier((grad_in, result))
    grad_flow = grad_in + swap_dp(sent, 1).astype(F32)

    attention, ffn, low, low_other, middle_low, active = kept[0]
    branch_two, grad_hidden, grad_pre, branch_one, grad_att, six = ffn_backward(grad_flow, ffn, attention, w)
    pairs_one = (active, branch_two, grad_hidden, middle_low, attention["att"], branch_one)
    ffn_pairs = list(zip(pairs_two, pairs_one))
    send, other_columns = ffn_grads(ffn_pairs, 1)
    other = swap_dp(send, 1)
    keep, own_columns = ffn_grads(ffn_pairs, 0)
    near, near_sent, far, far_sent = pair_halves(keep, other)
    grad_att, near_sent, far_sent = lax.optimization_barrier((grad_att, near_sent, far_sent))
    near_got, far_got = swap_dp(near_sent, 2), swap_dp(far_sent, 4)
    grad_in, keep, send = last_backward(
        grad_att, grad_pre, attention, w,
        (dq, dk, dv, low_two, low, other_two, low_other, six_two, six, own_columns, other_columns), at,
    )
    keep, send, near_got, far_got = lax.optimization_barrier((keep, send, near_got, far_got))
    (near, near_sent), (far, far_sent) = add_halves(near, near_got), add_halves(far, far_got)
    near_sent, far_sent, send = lax.optimization_barrier((near_sent, far_sent, send))
    near_got, far_got = swap_dp(near_sent, 4), swap_dp(far_sent, 2)
    other = swap_dp(send, 1)
    grad_low = (grad_in + other[16:].reshape(rows, width).astype(F32)).astype(LOW)
    near_head, near_sent, far_head, far_sent = pair_halves(keep, other[:16].reshape(keep.shape))
    near_head_got, far_head_got = lax.optimization_barrier((swap_dp(near_sent, 2), swap_dp(far_sent, 4)))
    (near_head, near_sent), (far_head, far_sent) = add_halves(near_head, near_head_got), add_halves(far_head, far_head_got)
    near_head_got, far_head_got = swap_dp(near_sent, 4), swap_dp(far_sent, 2)
    ffn_parts = swap_shards(add_shards(near, near_got, far, far_got))
    ffn_parts = lax.optimization_barrier((*ffn_parts, near_head_got, far_head_got))[:4]
    ffn_own = sum_shards(ffn_parts)
    head_own = sum_shards(swap_shards(add_shards(near_head, near_head_got, far_head, far_head_got)))
    own = jnp.concatenate((ffn_own, head_own))
    own, grad_low = lax.optimization_barrier((own, grad_low))
    own, *others = spread_plane(own)
    own, *others, input_grad = lax.optimization_barrier((own, *others, regroup(grad_low)))
    input_grad = input_grad.astype(F32)
    plane = [own] + others
    blocks = plane + [swap_dp(block, 1) for block in plane]
    (
        down_grad, up_grad, out_grad, up_bias_grad, q_grad, k_grad, v_grad, q_bias_grad, v_bias_grad, shared,
    ) = finish(blocks, ur, hr, at)
    return (
        result, input_grad, q_grad, q_bias_grad[0], k_grad, v_grad, v_bias_grad[0], out_grad, shared[5], shared[3], shared[4],
        up_grad, up_bias_grad[0], down_grad, shared[2], shared[0], shared[1],
    )


def solution(mesh):
    split = P(("dp", "tensor"), None)
    columns, rows, part = P(None, "tensor"), P("tensor", None), P("tensor")
    return jax.shard_map(
        per_device,
        mesh=mesh,
        in_specs=(
            split, P("dp"), columns, part, columns, columns, part, rows, P(), P(), P(), columns, part, rows, P(), P(),
            P(), split,
        ),
        out_specs=(
            split, split, columns, part, columns, columns, part, rows, P(), P(), P(), columns, part, rows, P(), P(), P(),
        ),
        check_vma=False,
    )
```

```python
import functools
import math

import jax
import jax.numpy as jnp
from jax import lax
from jax.experimental import pallas as pl
from jax.experimental.pallas import tpu as pltpu
from jax.sharding import PartitionSpec as P

HEAD_DIM = 64
LEN = 1024
EPS = 1e-05
LANES = 128
LOW = jnp.bfloat16
F32 = jnp.float32
EXP2_SCALE = math.log2(math.e) / math.sqrt(HEAD_DIM)
INV_SCALE = 1.0 / math.sqrt(HEAD_DIM)
BARRED = -1e9


def swap_dp(value, bits):
    count = lax.axis_size("dp")
    return lax.ppermute(value, "dp", [(i, i ^ bits) for i in range(count)])


def swap_tensor(value, step):
    count = lax.axis_size("tensor")
    return lax.ppermute(value, "tensor", [(i, i ^ step) for i in range(count)])


def regroup(block):
    dp, tensor = lax.axis_size("dp"), lax.axis_size("tensor")
    pairs = [
        ((2 * k + c) * tensor + 2 * a + b, (2 * k + b) * tensor + 2 * a + c)
        for k in range(dp // 2)
        for c in range(2)
        for a in range(tensor // 2)
        for b in range(2)
        if b != c
    ]
    moved = lax.ppermute(block, ("dp", "tensor"), pairs)
    stays = (lax.axis_index("dp") % 2) == (lax.axis_index("tensor") % 2)
    return jnp.where(stays, block, moved)


def join_shards(piece):
    pieces = jnp.stack((piece, swap_tensor(piece, 2)))
    other = swap_tensor(pieces, 1)
    return jnp.stack((pieces[0], other[0], pieces[1], other[1]))


def spread_plane(block):
    return [block] + [swap_dp(block, bits) for bits in (2, 4, 6)]


def sum_parts(parts):
    total = parts[0].astype(F32)
    for part in parts[1:]:
        total = total + part.astype(F32)
    return total


def pair_halves(keep, other):
    def pair(first, second, shards):
        return jnp.stack([sum_parts((keep[i, shards], other[i, shards])).astype(LOW) for i in (first, second)])

    near, far = slice(0, 2), slice(2, 4)
    return pair(0, 2, near), pair(1, 3, near), pair(0, 1, far), pair(2, 3, far)


def add_halves(kept, got):
    return [sum_parts((kept[i], got[i])).astype(LOW) for i in range(2)]


def add_shards(near, near_got, far, far_got):
    return [sum_parts((a[j], b[j])).astype(LOW) for a, b in ((near, near_got), (far, far_got)) for j in range(2)]


def swap_shards(parts):
    return [parts[0]] + [swap_tensor(parts[j], j) for j in (1, 2, 3)]


def sum_shards(parts):
    total = sum_parts(parts)
    bits = 8
    while bits < lax.axis_size("dp"):
        total = total + swap_dp(total.astype(LOW), bits).astype(F32)
        bits *= 2
    return total.astype(LOW)


def flip(value, axis, wanted):
    return jnp.where(wanted, jnp.flip(value, axis), value)


def relative_blocks(blocks):
    dp = lax.axis_index("dp")
    return flip(flip(flip(blocks, 3, (dp & 1) != 0), 2, (dp & 2) != 0), 1, (dp & 4) != 0)


def dot_nt(a, b):
    return lax.dot_general(a, b, (((1,), (1,)), ((), ())), preferred_element_type=F32)


def dot_tn(a, b):
    return lax.dot_general(a, b, (((0,), (0,)), ((), ())), preferred_element_type=F32)


def dot_nn(a, b):
    return jnp.dot(a, b, preferred_element_type=F32)


def norm(value):
    center = value - jnp.mean(value, -1, keepdims=True)
    scale = lax.rsqrt(jnp.mean(center * center, -1, keepdims=True) + EPS)
    return center * scale, scale


def norm_back(grad, gain, unit, scale):
    scaled = grad * gain
    mean_a = jnp.mean(scaled, -1, keepdims=True)
    mean_b = jnp.mean(scaled * unit, -1, keepdims=True)
    return (scaled - mean_a - unit * mean_b) * scale


def lane_half(which):
    first = lax.broadcasted_iota(jnp.int32, (1, LANES), 1) < HEAD_DIM
    return first if which == 0 else jnp.logical_not(first)


VMEM_MIB = {
    "attention_first": 10, "attention_forward": 10, "ffn_first": 5, "ffn_forward": 5, "ffn_backward": 4, "ffn_grads": 3,
    "attention_backward": 6, "last_backward": 10, "finish": 7,
}


def call(kernel, name, micros, outs, scratch, *operands, scalars=0, far=0):
    spaces = [pltpu.SMEM] * scalars + [pl.ANY] * far + [pltpu.VMEM] * (len(operands) - scalars - far)
    return pl.pallas_call(
        kernel,
        in_specs=[pl.BlockSpec(memory_space=space) for space in spaces],
        out_specs=[pl.BlockSpec(memory_space=pltpu.VMEM)] * len(outs),
        out_shape=[jax.ShapeDtypeStruct(shape, dtype) for shape, dtype in outs],
        scratch_shapes=[pltpu.VMEM(*s) if isinstance(s, tuple) else s for s in scratch],
        compiler_params=pltpu.CompilerParams(vmem_limit_bytes=VMEM_MIB[name] * 2**20),
        cost_estimate=pl.CostEstimate(flops=int(micros * 1.1e9), bytes_accessed=0, transcendentals=0),
        name=name,
    )(*operands)


def attention_first_kernel(*refs):
    blocks, rest, w_out, scratch, sems = refs[:8], refs[8:-4], refs[-4], refs[-3:-1], refs[-1]
    copies = []
    for at, block in enumerate(blocks):
        c, i = divmod(at, 4)
        rows = block.shape[1] // 4
        for kind in range(4):
            source = block.at[:, kind * rows : (kind + 1) * rows]
            copies.append(pltpu.make_async_copy(source, w_out.at[kind, :, 2 * i + c], sems.at[at, kind]))
    for copy in copies:
        copy.start()
    for copy in copies:
        copy.wait()
    attention_forward_kernel(*rest[:5], w_out, *rest[5:], *scratch)


def attention_forward_kernel(
    in_ref, low_ref, other_ref, mark_ref, barred_ref, w_ref, qb, vb, ob, gain, shift,
    q_out, k_out, v_out, e_out, inv_out, o_out, att_out, unit_out, scale_out, mid_out, kmask, vmask,
):
    rows = in_ref.shape[0]
    wq, wk, wv, wo = (w_ref[kind].reshape(-1, w_ref.shape[-1]) for kind in range(4))
    heads = wq.shape[0] // HEAD_DIM
    zero = jnp.zeros((), LOW)
    low = low_ref[...]
    q_out[...] = (dot_nt(low, wq) + qb[...]).astype(LOW)
    for half, part in enumerate((low, other_ref[...])):
        r = slice(half * rows, (half + 1) * rows)
        k_out[r] = dot_nt(part, wk).astype(LOW)
        v_out[r] = (dot_nt(part, wv) + vb[...]).astype(LOW)
    mark = mark_ref[...]
    first = lane_half(0)
    for p in range(heads // 2):
        cols = slice(p * LANES, (p + 1) * LANES)
        keys, values = k_out[:, cols], v_out[:, cols]
        scaled = q_out[:, cols].astype(F32) * EXP2_SCALE
        high = scaled.astype(LOW)
        rest = (scaled - high.astype(F32)).astype(LOW)
        mixed = []
        for h in range(2):
            keep = lane_half(h)
            query = jnp.concatenate((jnp.where(keep, high, mark), jnp.where(keep, rest, zero)), 1)
            slot = (2 * p + h) % 4
            kmask[slot, :, :LANES] = jnp.where(keep, keys, barred_ref[...])
            kmask[slot, :, LANES:] = jnp.where(keep, keys, zero)
            vmask[slot] = jnp.where(keep, values, jnp.ones((), LOW))
            scores = dot_nt(query, kmask[slot])
            exponent = jnp.exp2(scores - jnp.max(scores, -1, keepdims=True)).astype(LOW)
            e_out[2 * p + h] = exponent
            mixed.append(dot_nn(exponent, vmask[slot]))
        inv = 1.0 / pltpu.roll(jnp.where(first, mixed[1], mixed[0]), HEAD_DIM, 1)
        attended = jnp.where(first, mixed[0], mixed[1]) * inv
        inv_out[:, cols] = inv
        o_out[:, cols] = attended
        att_out[:, cols] = attended.astype(LOW)
    unit, scale = norm(in_ref[...].astype(F32) + dot_nn(att_out[...], wo) + ob[...])
    unit_out[...] = unit
    scale_out[...] = jnp.broadcast_to(scale, scale_out.shape)
    mid_out[...] = unit * gain[...] + shift[...]


def attention_forward(layer_in, low, other, mark, barred, w, blocks=None):
    rows, width = layer_in.shape
    units = w["qb"].shape[1]
    heads = units // HEAD_DIM
    outs = [
        ((rows, units), LOW), ((2 * rows, units), LOW), ((2 * rows, units), LOW), ((heads, rows, 2 * rows), LOW),
        ((rows, units), F32), ((rows, units), F32), ((rows, units), LOW), ((rows, width), F32), ((rows, LANES), F32),
        ((rows, width), F32),
    ]
    scratch = [((4, 2 * rows, 2 * LANES), LOW), ((4, 2 * rows, LANES), LOW)]
    tail = (w["qb"], w["vb"], w["ob"], w["g1"], w["s1"])
    first = (layer_in, low, other, mark, barred)
    if blocks is None:
        return call(attention_forward_kernel, "attention_forward", 8, outs, scratch, *first, w["heads"], *tail)
    scratch.append(pltpu.SemaphoreType.DMA((8, 4)))
    outs.append(((4, 4, 8, units // 32, width), LOW))
    return call(attention_first_kernel, "attention_first", 9, outs, scratch, *blocks, *first, *tail, far=8)


GELU_A = math.sqrt(2.0 / math.pi)
GELU_B = 0.044715


def ffn_first_kernel(*refs):
    blocks, rest, w_out, sems = refs[:8], refs[8:-2], refs[-2], refs[-1]
    copies = []
    for at, block in enumerate(blocks):
        rows = block.shape[1] // 2
        for kind in range(2):
            source = block.at[:, kind * rows : (kind + 1) * rows]
            copies.append(pltpu.make_async_copy(source, w_out.at[kind, at], sems.at[at, kind]))
    for copy in copies:
        copy.start()
    for copy in copies:
        copy.wait()
    ffn_forward_kernel(rest[0], w_out, *rest[1:])


def unit_blocks(w_ref):
    count = w_ref.shape[2] * w_ref.shape[3] * 2
    for at in range(4):
        up, down = (w_ref[kind, 2 * at : 2 * at + 2].reshape(count, -1) for kind in range(2))
        yield slice(at * count, (at + 1) * count), up, down


def ffn_forward_kernel(
    mid_ref, w_ref, upb, db, gain, shift, low_out, act_out, slope_out, unit_out, scale_out, out_out, next_out
):
    middle = mid_ref[...]
    low = middle.astype(LOW)
    low_out[...] = low
    total = middle + db[...]
    for r, up, down in unit_blocks(w_ref):
        hidden = dot_nt(low, up) + upb[:, r]
        square = hidden * hidden
        bent = jnp.tanh(hidden * (GELU_A + GELU_A * GELU_B * square))
        half = 0.5 + 0.5 * bent
        active = (hidden * half).astype(LOW)
        act_out[:, r] = active
        inner = GELU_A + 3.0 * GELU_A * GELU_B * square
        slope_out[:, r] = (half + 0.5 * hidden * (1.0 - bent * bent) * inner).astype(LOW)
        total = total + dot_nn(active, down)
    unit, scale = norm(total)
    unit_out[...] = unit
    scale_out[...] = jnp.broadcast_to(scale, scale_out.shape)
    layer_out = unit * gain[...] + shift[...]
    out_out[...] = layer_out
    next_out[...] = layer_out.astype(LOW)


def ffn_forward(middle, w, blocks=None):
    rows, width = middle.shape
    units = w["upb"].shape[1]
    outs = [
        ((rows, width), LOW), ((rows, units), LOW), ((rows, units), LOW), ((rows, width), F32), ((rows, LANES), F32),
        ((rows, width), F32), ((rows, width), LOW),
    ]
    tail = (w["upb"], w["db"], w["g2"], w["s2"])
    if blocks is None:
        return call(ffn_forward_kernel, "ffn_forward", 5, outs, [], middle, w["ffn"], *tail)
    outs.append(((2, 8, 4, units // 32, width), LOW))
    scratch = [pltpu.SemaphoreType.DMA((8, 2))]
    return call(ffn_first_kernel, "ffn_first", 6, outs, scratch, *blocks, middle, *tail, far=8)


def row_sum(value):
    return jnp.sum(value, 0, keepdims=True)


def ffn_backward_kernel(
    w_ref, grad_ref, unit_two, scale_two, slope, unit_one, scale_one, heads_ref, gain_two, gain_one,
    branch_two_out, hidden_out, pre_one_out, branch_one_out, att_out, sums_out,
):
    grad = grad_ref[...].astype(F32)
    unit = unit_two[...]
    sums_out[0:1] = row_sum(grad * unit)
    sums_out[1:2] = row_sum(grad)
    grad_pre = norm_back(grad, gain_two[...], unit, scale_two[:, :1])
    branch = grad_pre.astype(LOW)
    branch_two_out[...] = branch
    sums_out[2:3] = row_sum(branch.astype(F32))
    grad_middle = grad_pre
    for r, up, down in unit_blocks(w_ref):
        hidden = (dot_nt(branch, down) * slope[:, r].astype(F32)).astype(LOW)
        hidden_out[:, r] = hidden
        grad_middle = grad_middle + dot_nn(hidden, up)
    unit = unit_one[...]
    sums_out[3:4] = row_sum(grad_middle * unit)
    sums_out[4:5] = row_sum(grad_middle)
    grad_pre = norm_back(grad_middle, gain_one[...], unit, scale_one[:, :1])
    pre_one_out[...] = grad_pre
    branch = grad_pre.astype(LOW)
    branch_one_out[...] = branch
    sums_out[5:6] = row_sum(branch.astype(F32))
    sums_out[6:8] = jnp.zeros((2, grad.shape[1]), F32)
    att_out[...] = dot_nt(branch, heads_ref[3].reshape(-1, grad.shape[1])).astype(LOW)


def ffn_backward(grad_out, kept_ffn, kept_attention, w):
    rows, width = grad_out.shape
    units = w["upb"].shape[1]
    outs = [
        ((rows, width), LOW), ((rows, units), LOW), ((rows, width), F32), ((rows, width), LOW),
        ((rows, w["qb"].shape[1]), LOW), ((8, width), F32),
    ]
    return call(
        ffn_backward_kernel, "ffn_backward", 5, outs, [], w["ffn"],
        grad_out, kept_ffn["unit"], kept_ffn["scale"], kept_ffn["slope"], kept_attention["unit"], kept_attention["scale"],
        w["heads"], w["g2"], w["g1"],
    )


def attention_backward_kernel(
    att_ref, pre_ref, q_ref, k_ref, v_ref, e_ref, inv_ref, o_ref, w_ref,
    in_out, sent_out, dq_out, dk_out, dv_out, vmask,
):
    wq, wk, wv = (w_ref[kind].reshape(-1, w_ref.shape[-1]) for kind in range(3))
    rows = att_ref.shape[0]
    heads = wq.shape[0] // HEAD_DIM
    zero = jnp.zeros((), LOW)
    first = lane_half(0)
    spare = lax.broadcasted_iota(jnp.int32, (1, LANES), 1) % HEAD_DIM
    minus = jnp.where(spare < 3, -1.0, 0.0).astype(LOW)
    for p in range(heads // 2):
        cols = slice(p * LANES, (p + 1) * LANES)
        queries, keys, values = q_ref[:, cols], k_ref[:, cols], v_ref[:, cols]
        grad = (att_ref[:, cols].astype(F32) * inv_ref[:, cols]).astype(LOW)
        dots = grad.astype(F32) * o_ref[:, cols]
        dq, dk, dv = [], [], []
        for h in range(2):
            keep = lane_half(h)
            dot = jnp.sum(jnp.where(keep, dots, 0.0), -1, keepdims=True)
            top = dot.astype(LOW)
            left = dot - top.astype(F32)
            mid = left.astype(LOW)
            end = (left - mid.astype(F32)).astype(LOW)
            pieces = jnp.where(spare == 0, top, jnp.where(spare == 1, mid, jnp.where(spare == 2, end, zero)))
            exponent = e_ref[2 * p + h]
            slot = (2 * p + h) % 4
            vmask[slot] = jnp.where(keep, values, minus)
            centered = dot_nt(jnp.where(keep, grad, pieces), vmask[slot])
            grad_scores = (exponent.astype(F32) * centered).astype(LOW)
            dq.append(dot_nn(grad_scores, keys))
            dk.append(dot_tn(grad_scores, queries))
            dv.append(dot_tn(exponent, grad))
        dq_out[:, cols] = (jnp.where(first, dq[0], dq[1]) * INV_SCALE).astype(LOW)
        dk_out[:, cols] = (jnp.where(first, dk[0], dk[1]) * INV_SCALE).astype(LOW)
        dv_out[:, cols] = jnp.where(first, dv[0], dv[1]).astype(LOW)
    dq, dk, dv = dq_out[...], dk_out[...], dv_out[...]
    sent_out[...] = (dot_nn(dk[rows:], wk) + dot_nn(dv[rows:], wv)).astype(LOW)
    in_out[...] = pre_ref[...] + dot_nn(dq, wq) + dot_nn(dk[:rows], wk) + dot_nn(dv[:rows], wv)


def attention_backward(grad_att, grad_pre, kept, w):
    rows, width = grad_pre.shape
    units = w["qb"].shape[1]
    heads = units // HEAD_DIM
    outs = [
        ((rows, width), F32), ((rows, width), LOW), ((rows, units), LOW), ((2 * rows, units), LOW), ((2 * rows, units), LOW),
    ]
    return call(
        attention_backward_kernel, "attention_backward", 12, outs,
        [((4, 2 * rows, LANES), LOW)],
        grad_att, grad_pre, kept["q"], kept["k"], kept["v"], kept["e"], kept["inv"], kept["o"], w["heads"],
    )


def both_layers(firsts, seconds):
    return sum(dot_tn(a[...], b[...]) for a, b in zip(firsts, seconds))


def ffn_grads_kernel(c, *refs):
    actives, branches, hiddens, middles, attendeds, ones_branches = (refs[2 * i : 2 * i + 2] for i in range(6))
    out, bias_out = refs[12:]
    rows, units = actives[0].shape
    step = units // 8
    ur = step // 4
    hr = attendeds[0].shape[1] // 32
    one = jnp.ones((rows, LANES), LOW)
    out_grad = both_layers(attendeds, ones_branches).astype(LOW)
    for i in range(4):
        at = 4 * c + i
        cols = slice(at * step, (at + 1) * step)
        down = both_layers([a.at[:, cols] for a in actives], branches).astype(LOW)
        up = both_layers([h.at[:, cols] for h in hiddens], middles).astype(LOW)
        bias_out[i * step : (i + 1) * step] = sum(dot_tn(h[:, cols], one) for h in hiddens).astype(LOW)
        for j in range(4):
            out[i, j, :ur] = down[j * ur : (j + 1) * ur]
            out[i, j, ur : 2 * ur] = up[j * ur : (j + 1) * ur]
            head = j * LANES + (2 * i + c) * hr
            out[i, j, 2 * ur :] = out_grad[head : head + hr]


def ffn_grads(pairs, c):
    rows, units = pairs[0][0].shape
    width = pairs[1][0].shape[1]
    ur, hr = units // 32, pairs[4][0].shape[1] // 32
    outs = [((4, 4, 2 * ur + hr, width), LOW), ((units // 2, LANES), LOW)]
    return call(functools.partial(ffn_grads_kernel, c), "ffn_grads", 3, outs, [], *[v for pair in pairs for v in pair])


def head_grads_kernel(eighth_ref, *refs):
    dqs, dks, dvs, lows, others, sums = (refs[2 * i : 2 * i + 2] for i in range(6))
    up_biases, (keep, send, shared) = refs[12:14], refs[14:]
    lane = lax.broadcasted_iota(jnp.int32, (1, LANES), 1) // (LANES // 4)
    shared[...] = sums[0][...] + sums[1][...]
    upper = lax.broadcasted_iota(jnp.int32, (16, 1), 0) < 8
    rows, units = dqs[0].shape
    hr = units // 32
    one = jnp.ones((rows, LANES), LOW)

    def halves(grads):
        own = [g.at[:rows] for g in grads]
        return own, [g.at[rows:] for g in grads]

    dk_own, dk_other = halves(dks)
    dv_own, dv_other = halves(dvs)
    grads = [
        both_layers(dqs, lows),
        both_layers(dk_own + dk_other, lows + others),
        both_layers(dv_own + dv_other, lows + others),
    ]
    grads = [g.astype(LOW) for g in grads]
    biases = [sum(dot_tn(g[...], one) for g in part).astype(LOW) for part in (dqs, dv_own + dv_other)]
    for at in range(8):
        c, i = divmod(at, 4)
        line = shared[pl.ds(eighth_ref[0] ^ (2 * i + c), 1)]
        line = jnp.where(upper, line[:, : 2 * LANES], line[:, 2 * LANES :]).astype(LOW)
        for j in range(4):
            out = keep.at[i, j] if c == 0 else send.at[4 * i + j]
            first = j * LANES + (2 * i + c) * hr
            for kind in range(3):
                out[kind * hr : (kind + 1) * hr] = grads[kind][first : first + hr]
            q, v = (bias[first : first + hr] for bias in biases)
            up_bias = up_biases[c]
            first = (4 * i + j) * (up_bias.shape[0] // 16)
            u = [up_bias[first + g * hr : first + (g + 1) * hr] for g in range(4)]
            out[3 * hr :, :LANES] = jnp.where(lane < 1, q, jnp.where(lane < 2, v, jnp.where(lane < 3, u[0], u[1])))
            out[3 * hr :, LANES : 2 * LANES] = jnp.where(lane < 1, u[2], u[3])
            out[3 * hr :, 2 * LANES :] = line


def last_backward_kernel(eighth_ref, *refs):
    given, (dq_two, dk_two, dv_two), lows, others, sums = refs[:9], refs[9:12], refs[12:14], refs[14:16], refs[16:18]
    up_biases, (in_out, keep, send, dq, dk, dv, sent_out, vmask, shared) = refs[18:20], refs[20:]
    attention_backward_kernel(*given, in_out, sent_out, dq, dk, dv, vmask)
    head_grads_kernel(eighth_ref, dq_two, dq, dk_two, dk, dv_two, dv, *lows, *others, *sums, *up_biases, keep, send, shared)
    send[16:] = sent_out[...].reshape(-1, *send.shape[1:])


def last_backward(grad_att, grad_pre, kept, w, pairs, eighth):
    rows, width = grad_pre.shape
    units = w["qb"].shape[1]
    block = 4 * (units // 32)
    outs = [((rows, width), F32), ((4, 4, block, width), LOW), ((16 + rows // block, block, width), LOW)]
    scratch = [((rows, units), LOW), ((2 * rows, units), LOW), ((2 * rows, units), LOW), ((rows, width), LOW)]
    scratch += [((4, 2 * rows, LANES), LOW), ((8, width), F32)]
    return call(
        last_backward_kernel, "last_backward", 16, outs, scratch, eighth, grad_att, grad_pre,
        kept["q"], kept["k"], kept["v"], kept["e"], kept["inv"], kept["o"], w["heads"], *pairs, scalars=1,
    )


def first_row(column):
    return column.T[:1]


def finish_kernel(ur, hr, eighth_ref, *refs):
    blocks, (down_out, up_out, out_out, up_bias) = refs[:8], refs[8:12]
    outs, biases, shared, (up_all, up_bias_all, *scratch) = refs[12:15], refs[15:17], refs[17], refs[18:]
    head = 2 * ur + hr
    for at, block in enumerate(blocks):
        c, i = divmod(at, 4)
        slot = eighth_ref[0] ^ (2 * i + c)
        units = pl.ds(pl.multiple_of(slot * ur, ur), ur)
        down_out[units] = block[:ur].astype(F32)
        up_all[units] = block[ur : 2 * ur].astype(F32)
        out_out[pl.ds(pl.multiple_of(slot * hr, hr), hr)] = block[2 * ur : 2 * ur + hr].astype(F32)
        columns = [
            jnp.broadcast_to(block[head + 3 * hr :, at : at + 1].astype(F32), (hr, LANES))
            for at in range(0, 6 * (LANES // 4), LANES // 4)
        ]
        for g in range(4):
            some = pl.ds(pl.multiple_of(slot * ur + g * hr, hr), hr)
            up_bias_all[some] = columns[2 + g]
        units = pl.ds(pl.multiple_of(slot * hr, hr), hr)
        for kind in range(3):
            scratch[kind][units] = block[head + kind * hr : head + (kind + 1) * hr].astype(F32)
        for kind in range(2):
            scratch[3 + kind][units] = columns[kind]
        line = block[head + 3 * hr :, 2 * LANES :].astype(F32)
        shared[pl.ds(slot, 1)] = jnp.concatenate((line[:1], line[8:9]), 1)
    up_out[...] = up_all[...].T
    up_bias[...] = first_row(up_bias_all[...])
    for kind in range(3):
        outs[kind][...] = scratch[kind][...].T
    for kind in range(2):
        biases[kind][...] = first_row(scratch[3 + kind][...])


def finish(blocks, ur, hr, eighth):
    width = blocks[0].shape[1]
    outs = [((8 * ur, width), F32), ((width, 8 * ur), F32), ((8 * hr, width), F32), ((1, 8 * ur), F32)]
    outs += [((width, 8 * hr), F32)] * 3 + [((1, 8 * hr), F32)] * 2 + [((8, width), F32)]
    scratch = [((8 * ur, width), F32), ((8 * ur, LANES), F32)]
    scratch += [((8 * hr, width), F32)] * 3 + [((8 * hr, LANES), F32)] * 2
    return call(functools.partial(finish_kernel, ur, hr), "finish", 3, outs, scratch, eighth, *blocks, scalars=1)


def per_device(
    inputs, segment_ids, query_weight, query_bias, key_weight, value_weight, value_bias, out_weight, out_bias,
    first_gain, first_shift, up_weight, up_bias, down_weight, down_bias, second_gain, second_shift, cotangent,
):
    rows, width = inputs.shape
    dp, tensor = lax.axis_index("dp"), lax.axis_index("tensor")
    core, eighth = dp % 2, dp % 8
    shard_heads, shard_units = query_weight.shape[1], up_weight.shape[1]
    hr, ur = shard_heads // 8, shard_units // 8

    def columns(weight, count):
        return lax.dynamic_slice_in_dim(weight, eighth * count, count, 1).T

    def own_rows(weight, count):
        return lax.dynamic_slice_in_dim(weight, eighth * count, count, 0)

    first_in = regroup(inputs)
    flat = (
        jnp.pad(query_bias, (0, shard_heads + shard_units))
        + jnp.pad(value_bias, (shard_heads, shard_units))
        + jnp.pad(up_bias, (2 * shard_heads, 0))
    )
    top = lax.reduce_precision(flat, 8, 7)
    mid = lax.reduce_precision(flat - top, 8, 7)
    flat = jnp.concatenate((top, mid, flat - top - mid)).astype(LOW)
    count = flat.shape[0]
    flat = jnp.pad(flat, (0, -count % (16 * width))).reshape(-1, width)
    heads_piece = jnp.concatenate(
        [columns(v, hr) for v in (query_weight, key_weight, value_weight)] + [own_rows(out_weight, hr), flat]
    )
    ffn_piece = jnp.concatenate((columns(up_weight, ur), own_rows(down_weight, ur)))
    shards = jnp.stack([heads_piece] + [swap_tensor(heads_piece, step) for step in (1, 2, 3)])
    heads_own = spread_plane(shards[:, : 4 * hr])
    ffn_own = spread_plane(join_shards(ffn_piece))
    first_in, *heads_own = lax.optimization_barrier((first_in, *heads_own))
    head_blocks = heads_own + [swap_dp(block, 1) for block in heads_own]
    flat = shards[:, 4 * hr :].reshape(4, -1)[:, :count].astype(F32)
    flat = jnp.sum(flat.reshape(4, 3, -1), 1)
    seq = lax.dynamic_slice_in_dim(segment_ids, (tensor // 2) * LEN, LEN)
    seq = jnp.where(core == tensor % 2, seq, swap_dp(seq, 1))
    labels_own = lax.dynamic_slice_in_dim(seq, core * rows, rows)
    labels_all = jnp.concatenate((labels_own, lax.dynamic_slice_in_dim(seq, (1 - core) * rows, rows)))
    code = jnp.arange(LANES) % HEAD_DIM - 1
    mark = (labels_own[:, None] == code).astype(LOW)
    barred = jnp.where(labels_all[:, None] == code, 0.0, BARRED).astype(LOW)

    def bias(start, count):
        return relative_blocks(flat[:, start : start + count].reshape(4, 2, 2, 2, -1))

    w = {
        "qb": bias(0, shard_heads).reshape(1, -1), "vb": bias(shard_heads, shard_heads).reshape(1, -1),
        "upb": bias(2 * shard_heads, shard_units).reshape(4, 4, 2, ur).transpose(2, 1, 0, 3).reshape(1, -1),
        "ob": out_bias[None], "g1": first_gain[None], "s1": first_shift[None], "db": down_bias[None],
        "g2": second_gain[None], "s2": second_shift[None],
    }

    kept = []
    layer_in, low = first_in, first_in
    for position in range(2):
        other = swap_dp(low, 1)
        made = attention_forward(layer_in, low, other, mark, barred, w, None if position else head_blocks)
        q, k, v, e, inv, o, attended, unit_one, scale_one, middle = made[:10]
        if position == 0:
            w["heads"] = made[10]
            middle, cotangent, *ffn_own = lax.optimization_barrier((middle, cotangent, *ffn_own))
            ffn_blocks = ffn_own + [swap_dp(block, 1) for block in ffn_own]
        made = ffn_forward(middle, w, None if position else ffn_blocks)
        middle_low, active, slope, unit_two, scale_two, layer_out, next_low = made[:7]
        if position == 0:
            w["ffn"] = made[7]
        attention = {"q": q, "k": k, "v": v, "e": e, "inv": inv, "o": o, "unit": unit_one, "scale": scale_one, "att": attended}
        ffn = {"slope": slope, "unit": unit_two, "scale": scale_two}
        kept.append((attention, ffn, low, other, middle_low, active))
        layer_in, low = layer_out, next_low
    result = regroup(low)

    grad_flow = regroup(cotangent)
    at = jnp.reshape(eighth, (1,)).astype(jnp.int32)
    attention_two, ffn, low_two, other_two, middle_low, active = kept[1]
    branch_two, grad_hidden, grad_pre, branch_one, grad_att, six_two = ffn_backward(grad_flow, ffn, attention_two, w)
    pairs_two = (active, branch_two, grad_hidden, middle_low, attention_two["att"], branch_one)
    grad_in, sent, dq, dk, dv = attention_backward(grad_att, grad_pre, attention_two, w)
    grad_in, result = lax.optimization_barrier((grad_in, result))
    grad_flow = grad_in + swap_dp(sent, 1).astype(F32)

    attention, ffn, low, low_other, middle_low, active = kept[0]
    branch_two, grad_hidden, grad_pre, branch_one, grad_att, six = ffn_backward(grad_flow, ffn, attention, w)
    pairs_one = (active, branch_two, grad_hidden, middle_low, attention["att"], branch_one)
    ffn_pairs = list(zip(pairs_two, pairs_one))
    send, other_columns = ffn_grads(ffn_pairs, 1)
    other = swap_dp(send, 1)
    keep, own_columns = ffn_grads(ffn_pairs, 0)
    near, near_sent, far, far_sent = pair_halves(keep, other)
    grad_att, near_sent, far_sent = lax.optimization_barrier((grad_att, near_sent, far_sent))
    near_got, far_got = swap_dp(near_sent, 2), swap_dp(far_sent, 4)
    grad_in, keep, send = last_backward(
        grad_att, grad_pre, attention, w,
        (dq, dk, dv, low_two, low, other_two, low_other, six_two, six, own_columns, other_columns), at,
    )
    keep, send, near_got, far_got = lax.optimization_barrier((keep, send, near_got, far_got))
    (near, near_sent), (far, far_sent) = add_halves(near, near_got), add_halves(far, far_got)
    near_sent, far_sent, send = lax.optimization_barrier((near_sent, far_sent, send))
    near_got, far_got = swap_dp(near_sent, 4), swap_dp(far_sent, 2)
    other = swap_dp(send, 1)
    grad_low = (grad_in + other[16:].reshape(rows, width).astype(F32)).astype(LOW)
    near_head, near_sent, far_head, far_sent = pair_halves(keep, other[:16].reshape(keep.shape))
    near_head_got, far_head_got = lax.optimization_barrier((swap_dp(near_sent, 2), swap_dp(far_sent, 4)))
    (near_head, near_sent), (far_head, far_sent) = add_halves(near_head, near_head_got), add_halves(far_head, far_head_got)
    near_head_got, far_head_got = swap_dp(near_sent, 4), swap_dp(far_sent, 2)
    ffn_parts = swap_shards(add_shards(near, near_got, far, far_got))
    ffn_parts = lax.optimization_barrier((*ffn_parts, near_head_got, far_head_got))[:4]
    ffn_own = sum_shards(ffn_parts)
    head_own = sum_shards(swap_shards(add_shards(near_head, near_head_got, far_head, far_head_got)))
    own = jnp.concatenate((ffn_own, head_own))
    own, grad_low = lax.optimization_barrier((own, grad_low))
    own, *others = spread_plane(own)
    own, *others, input_grad = lax.optimization_barrier((own, *others, regroup(grad_low)))
    input_grad = input_grad.astype(F32)
    plane = [own] + others
    blocks = plane + [swap_dp(block, 1) for block in plane]
    (
        down_grad, up_grad, out_grad, up_bias_grad, q_grad, k_grad, v_grad, q_bias_grad, v_bias_grad, shared,
    ) = finish(blocks, ur, hr, at)
    return (
        result, input_grad, q_grad, q_bias_grad[0], k_grad, v_grad, v_bias_grad[0], out_grad, shared[5], shared[3], shared[4],
        up_grad, up_bias_grad[0], down_grad, shared[2], shared[0], shared[1],
    )


def solution(mesh):
    split = P(("dp", "tensor"), None)
    columns, rows, part = P(None, "tensor"), P("tensor", None), P("tensor")
    return jax.shard_map(
        per_device,
        mesh=mesh,
        in_specs=(
            split, P("dp"), columns, part, columns, columns, part, rows, P(), P(), P(), columns, part, rows, P(), P(),
            P(), split,
        ),
        out_specs=(
            split, split, columns, part, columns, columns, part, rows, P(), P(), P(), columns, part, rows, P(), P(), P(),
        ),
        check_vma=False,
    )
```

```python
import functools
import math

import jax
import jax.numpy as jnp
from jax import lax
from jax.experimental import pallas as pl
from jax.experimental.pallas import tpu as pltpu
from jax.sharding import PartitionSpec as P

HEAD_DIM = 64
LEN = 1024
EPS = 1e-05
LANES = 128
LOW = jnp.bfloat16
F32 = jnp.float32
EXP2_SCALE = math.log2(math.e) / math.sqrt(HEAD_DIM)
INV_SCALE = 1.0 / math.sqrt(HEAD_DIM)
BARRED = -1e9


def swap_dp(value, bits):
    count = lax.axis_size("dp")
    return lax.ppermute(value, "dp", [(i, i ^ bits) for i in range(count)])


def swap_tensor(value, step):
    count = lax.axis_size("tensor")
    return lax.ppermute(value, "tensor", [(i, i ^ step) for i in range(count)])


def regroup(block):
    dp, tensor = lax.axis_size("dp"), lax.axis_size("tensor")
    pairs = [
        ((2 * k + c) * tensor + 2 * a + b, (2 * k + b) * tensor + 2 * a + c)
        for k in range(dp // 2)
        for c in range(2)
        for a in range(tensor // 2)
        for b in range(2)
        if b != c
    ]
    moved = lax.ppermute(block, ("dp", "tensor"), pairs)
    stays = (lax.axis_index("dp") % 2) == (lax.axis_index("tensor") % 2)
    return jnp.where(stays, block, moved)


def join_shards(piece):
    pieces = jnp.stack((piece, swap_tensor(piece, 2)))
    other = swap_tensor(pieces, 1)
    return jnp.stack((pieces[0], other[0], pieces[1], other[1]))


def spread_plane(block):
    return [block] + [swap_dp(block, bits) for bits in (2, 4, 6)]


def sum_parts(parts):
    total = parts[0].astype(F32)
    for part in parts[1:]:
        total = total + part.astype(F32)
    return total


def pair_halves(keep, other):
    def pair(first, second, shards):
        return jnp.stack([sum_parts((keep[i, shards], other[i, shards])).astype(LOW) for i in (first, second)])

    near, far = slice(0, 2), slice(2, 4)
    return pair(0, 2, near), pair(1, 3, near), pair(0, 1, far), pair(2, 3, far)


def add_halves(kept, got):
    return [sum_parts((kept[i], got[i])).astype(LOW) for i in range(2)]


def add_shards(near, near_got, far, far_got):
    return [sum_parts((a[j], b[j])).astype(LOW) for a, b in ((near, near_got), (far, far_got)) for j in range(2)]


def swap_shards(parts):
    return [parts[0]] + [swap_tensor(parts[j], j) for j in (1, 2, 3)]


def sum_shards(parts):
    total = sum_parts(parts)
    bits = 8
    while bits < lax.axis_size("dp"):
        total = total + swap_dp(total.astype(LOW), bits).astype(F32)
        bits *= 2
    return total.astype(LOW)


def flip(value, axis, wanted):
    return jnp.where(wanted, jnp.flip(value, axis), value)


def relative_blocks(blocks):
    dp = lax.axis_index("dp")
    return flip(flip(flip(blocks, 3, (dp & 1) != 0), 2, (dp & 2) != 0), 1, (dp & 4) != 0)


def dot_nt(a, b):
    return lax.dot_general(a, b, (((1,), (1,)), ((), ())), preferred_element_type=F32)


def dot_tn(a, b):
    return lax.dot_general(a, b, (((0,), (0,)), ((), ())), preferred_element_type=F32)


def dot_nn(a, b):
    return jnp.dot(a, b, preferred_element_type=F32)


def norm(value):
    center = value - jnp.mean(value, -1, keepdims=True)
    scale = lax.rsqrt(jnp.mean(center * center, -1, keepdims=True) + EPS)
    return center * scale, scale


def norm_back(grad, gain, unit, scale):
    scaled = grad * gain
    mean_a = jnp.mean(scaled, -1, keepdims=True)
    mean_b = jnp.mean(scaled * unit, -1, keepdims=True)
    return (scaled - mean_a - unit * mean_b) * scale


def lane_half(which):
    first = lax.broadcasted_iota(jnp.int32, (1, LANES), 1) < HEAD_DIM
    return first if which == 0 else jnp.logical_not(first)


VMEM_MIB = {
    "attention_first": 10, "attention_forward": 10, "ffn_first": 5, "ffn_forward": 5, "ffn_backward": 4, "ffn_grads": 3,
    "attention_backward": 6, "last_backward": 10, "finish": 7,
}


def call(kernel, name, micros, outs, scratch, *operands, scalars=0, far=0):
    spaces = [pltpu.SMEM] * scalars + [pl.ANY] * far + [pltpu.VMEM] * (len(operands) - scalars - far)
    return pl.pallas_call(
        kernel,
        in_specs=[pl.BlockSpec(memory_space=space) for space in spaces],
        out_specs=[pl.BlockSpec(memory_space=pltpu.VMEM)] * len(outs),
        out_shape=[jax.ShapeDtypeStruct(shape, dtype) for shape, dtype in outs],
        scratch_shapes=[pltpu.VMEM(*s) if isinstance(s, tuple) else s for s in scratch],
        compiler_params=pltpu.CompilerParams(vmem_limit_bytes=VMEM_MIB[name] * 2**20),
        cost_estimate=pl.CostEstimate(flops=int(micros * 1.1e9), bytes_accessed=0, transcendentals=0),
        name=name,
    )(*operands)


def attention_first_kernel(*refs):
    blocks, rest, w_out, scratch, sems = refs[:8], refs[8:-4], refs[-4], refs[-3:-1], refs[-1]
    copies = []
    for at, block in enumerate(blocks):
        c, i = divmod(at, 4)
        rows = block.shape[1] // 4
        for kind in range(4):
            source = block.at[:, kind * rows : (kind + 1) * rows]
            copies.append(pltpu.make_async_copy(source, w_out.at[kind, :, 2 * i + c], sems.at[at, kind]))
    for copy in copies:
        copy.start()
    for copy in copies:
        copy.wait()
    attention_forward_kernel(*rest[:5], w_out, *rest[5:], *scratch)


def attention_forward_kernel(
    in_ref, low_ref, other_ref, mark_ref, barred_ref, w_ref, qb, vb, ob, gain, shift,
    q_out, k_out, v_out, e_out, inv_out, o_out, att_out, unit_out, scale_out, mid_out, kmask, vmask,
):
    rows = in_ref.shape[0]
    wq, wk, wv, wo = (w_ref[kind].reshape(-1, w_ref.shape[-1]) for kind in range(4))
    heads = wq.shape[0] // HEAD_DIM
    zero = jnp.zeros((), LOW)
    low = low_ref[...]
    q_out[...] = (dot_nt(low, wq) + qb[...]).astype(LOW)
    for half, part in enumerate((low, other_ref[...])):
        r = slice(half * rows, (half + 1) * rows)
        k_out[r] = dot_nt(part, wk).astype(LOW)
        v_out[r] = (dot_nt(part, wv) + vb[...]).astype(LOW)
    mark = mark_ref[...]
    first = lane_half(0)
    for p in range(heads // 2):
        cols = slice(p * LANES, (p + 1) * LANES)
        keys, values = k_out[:, cols], v_out[:, cols]
        scaled = q_out[:, cols].astype(F32) * EXP2_SCALE
        high = scaled.astype(LOW)
        rest = (scaled - high.astype(F32)).astype(LOW)
        mixed = []
        for h in range(2):
            keep = lane_half(h)
            query = jnp.concatenate((jnp.where(keep, high, mark), jnp.where(keep, rest, zero)), 1)
            slot = (2 * p + h) % 4
            kmask[slot, :, :LANES] = jnp.where(keep, keys, barred_ref[...])
            kmask[slot, :, LANES:] = jnp.where(keep, keys, zero)
            vmask[slot] = jnp.where(keep, values, jnp.ones((), LOW))
            scores = dot_nt(query, kmask[slot])
            exponent = jnp.exp2(scores - jnp.max(scores, -1, keepdims=True)).astype(LOW)
            e_out[2 * p + h] = exponent
            mixed.append(dot_nn(exponent, vmask[slot]))
        inv = 1.0 / pltpu.roll(jnp.where(first, mixed[1], mixed[0]), HEAD_DIM, 1)
        attended = jnp.where(first, mixed[0], mixed[1]) * inv
        inv_out[:, cols] = inv
        o_out[:, cols] = attended
        att_out[:, cols] = attended.astype(LOW)
    unit, scale = norm(in_ref[...].astype(F32) + dot_nn(att_out[...], wo) + ob[...])
    unit_out[...] = unit
    scale_out[...] = jnp.broadcast_to(scale, scale_out.shape)
    mid_out[...] = unit * gain[...] + shift[...]


def attention_forward(layer_in, low, other, mark, barred, w, blocks=None):
    rows, width = layer_in.shape
    units = w["qb"].shape[1]
    heads = units // HEAD_DIM
    outs = [
        ((rows, units), LOW), ((2 * rows, units), LOW), ((2 * rows, units), LOW), ((heads, rows, 2 * rows), LOW),
        ((rows, units), F32), ((rows, units), F32), ((rows, units), LOW), ((rows, width), F32), ((rows, LANES), F32),
        ((rows, width), F32),
    ]
    scratch = [((4, 2 * rows, 2 * LANES), LOW), ((4, 2 * rows, LANES), LOW)]
    tail = (w["qb"], w["vb"], w["ob"], w["g1"], w["s1"])
    first = (layer_in, low, other, mark, barred)
    if blocks is None:
        return call(attention_forward_kernel, "attention_forward", 8, outs, scratch, *first, w["heads"], *tail)
    scratch.append(pltpu.SemaphoreType.DMA((8, 4)))
    outs.append(((4, 4, 8, units // 32, width), LOW))
    return call(attention_first_kernel, "attention_first", 9, outs, scratch, *blocks, *first, *tail, far=8)


GELU_A = math.sqrt(2.0 / math.pi)
GELU_B = 0.044715


def ffn_first_kernel(*refs):
    blocks, rest, w_out, sems = refs[:8], refs[8:-2], refs[-2], refs[-1]
    copies = []
    for at, block in enumerate(blocks):
        rows = block.shape[1] // 2
        for kind in range(2):
            source = block.at[:, kind * rows : (kind + 1) * rows]
            copies.append(pltpu.make_async_copy(source, w_out.at[kind, at], sems.at[at, kind]))
    for copy in copies:
        copy.start()
    for copy in copies:
        copy.wait()
    ffn_forward_kernel(rest[0], w_out, *rest[1:])


def unit_blocks(w_ref):
    count = w_ref.shape[2] * w_ref.shape[3] * 2
    for at in range(4):
        up, down = (w_ref[kind, 2 * at : 2 * at + 2].reshape(count, -1) for kind in range(2))
        yield slice(at * count, (at + 1) * count), up, down


def ffn_forward_kernel(
    mid_ref, w_ref, upb, db, gain, shift, low_out, act_out, slope_out, unit_out, scale_out, out_out, next_out
):
    middle = mid_ref[...]
    low = middle.astype(LOW)
    low_out[...] = low
    total = middle + db[...]
    for r, up, down in unit_blocks(w_ref):
        hidden = dot_nt(low, up) + upb[:, r]
        square = hidden * hidden
        bent = jnp.tanh(hidden * (GELU_A + GELU_A * GELU_B * square))
        half = 0.5 + 0.5 * bent
        active = (hidden * half).astype(LOW)
        act_out[:, r] = active
        inner = GELU_A + 3.0 * GELU_A * GELU_B * square
        slope_out[:, r] = (half + 0.5 * hidden * (1.0 - bent * bent) * inner).astype(LOW)
        total = total + dot_nn(active, down)
    unit, scale = norm(total)
    unit_out[...] = unit
    scale_out[...] = jnp.broadcast_to(scale, scale_out.shape)
    layer_out = unit * gain[...] + shift[...]
    out_out[...] = layer_out
    next_out[...] = layer_out.astype(LOW)


def ffn_forward(middle, w, blocks=None):
    rows, width = middle.shape
    units = w["upb"].shape[1]
    outs = [
        ((rows, width), LOW), ((rows, units), LOW), ((rows, units), LOW), ((rows, width), F32), ((rows, LANES), F32),
        ((rows, width), F32), ((rows, width), LOW),
    ]
    tail = (w["upb"], w["db"], w["g2"], w["s2"])
    if blocks is None:
        return call(ffn_forward_kernel, "ffn_forward", 5, outs, [], middle, w["ffn"], *tail)
    outs.append(((2, 8, 4, units // 32, width), LOW))
    scratch = [pltpu.SemaphoreType.DMA((8, 2))]
    return call(ffn_first_kernel, "ffn_first", 6, outs, scratch, *blocks, middle, *tail, far=8)


def row_sum(value):
    return jnp.sum(value, 0, keepdims=True)


def ffn_backward_kernel(
    w_ref, grad_ref, unit_two, scale_two, slope, unit_one, scale_one, heads_ref, gain_two, gain_one,
    branch_two_out, hidden_out, pre_one_out, branch_one_out, att_out, sums_out,
):
    grad = grad_ref[...].astype(F32)
    unit = unit_two[...]
    sums_out[0:1] = row_sum(grad * unit)
    sums_out[1:2] = row_sum(grad)
    grad_pre = norm_back(grad, gain_two[...], unit, scale_two[:, :1])
    branch = grad_pre.astype(LOW)
    branch_two_out[...] = branch
    sums_out[2:3] = row_sum(branch.astype(F32))
    grad_middle = grad_pre
    for r, up, down in unit_blocks(w_ref):
        hidden = (dot_nt(branch, down) * slope[:, r].astype(F32)).astype(LOW)
        hidden_out[:, r] = hidden
        grad_middle = grad_middle + dot_nn(hidden, up)
    unit = unit_one[...]
    sums_out[3:4] = row_sum(grad_middle * unit)
    sums_out[4:5] = row_sum(grad_middle)
    grad_pre = norm_back(grad_middle, gain_one[...], unit, scale_one[:, :1])
    pre_one_out[...] = grad_pre
    branch = grad_pre.astype(LOW)
    branch_one_out[...] = branch
    sums_out[5:6] = row_sum(branch.astype(F32))
    sums_out[6:8] = jnp.zeros((2, grad.shape[1]), F32)
    att_out[...] = dot_nt(branch, heads_ref[3].reshape(-1, grad.shape[1])).astype(LOW)


def ffn_backward(grad_out, kept_ffn, kept_attention, w):
    rows, width = grad_out.shape
    units = w["upb"].shape[1]
    outs = [
        ((rows, width), LOW), ((rows, units), LOW), ((rows, width), F32), ((rows, width), LOW),
        ((rows, w["qb"].shape[1]), LOW), ((8, width), F32),
    ]
    return call(
        ffn_backward_kernel, "ffn_backward", 5, outs, [], w["ffn"],
        grad_out, kept_ffn["unit"], kept_ffn["scale"], kept_ffn["slope"], kept_attention["unit"], kept_attention["scale"],
        w["heads"], w["g2"], w["g1"],
    )


def attention_backward_kernel(
    att_ref, pre_ref, q_ref, k_ref, v_ref, e_ref, inv_ref, o_ref, w_ref,
    in_out, sent_out, dq_out, dk_out, dv_out, vmask,
):
    wq, wk, wv = (w_ref[kind].reshape(-1, w_ref.shape[-1]) for kind in range(3))
    rows = att_ref.shape[0]
    heads = wq.shape[0] // HEAD_DIM
    zero = jnp.zeros((), LOW)
    first = lane_half(0)
    spare = lax.broadcasted_iota(jnp.int32, (1, LANES), 1) % HEAD_DIM
    minus = jnp.where(spare < 3, -1.0, 0.0).astype(LOW)
    for p in range(heads // 2):
        cols = slice(p * LANES, (p + 1) * LANES)
        queries, keys, values = q_ref[:, cols], k_ref[:, cols], v_ref[:, cols]
        grad = (att_ref[:, cols].astype(F32) * inv_ref[:, cols]).astype(LOW)
        dots = grad.astype(F32) * o_ref[:, cols]
        dq, dk, dv = [], [], []
        for h in range(2):
            keep = lane_half(h)
            dot = jnp.sum(jnp.where(keep, dots, 0.0), -1, keepdims=True)
            top = dot.astype(LOW)
            left = dot - top.astype(F32)
            mid = left.astype(LOW)
            end = (left - mid.astype(F32)).astype(LOW)
            pieces = jnp.where(spare == 0, top, jnp.where(spare == 1, mid, jnp.where(spare == 2, end, zero)))
            exponent = e_ref[2 * p + h]
            slot = (2 * p + h) % 4
            vmask[slot] = jnp.where(keep, values, minus)
            centered = dot_nt(jnp.where(keep, grad, pieces), vmask[slot])
            grad_scores = (exponent.astype(F32) * centered).astype(LOW)
            dq.append(dot_nn(grad_scores, keys))
            dk.append(dot_tn(grad_scores, queries))
            dv.append(dot_tn(exponent, grad))
        dq_out[:, cols] = (jnp.where(first, dq[0], dq[1]) * INV_SCALE).astype(LOW)
        dk_out[:, cols] = (jnp.where(first, dk[0], dk[1]) * INV_SCALE).astype(LOW)
        dv_out[:, cols] = jnp.where(first, dv[0], dv[1]).astype(LOW)
    dq, dk, dv = dq_out[...], dk_out[...], dv_out[...]
    sent_out[...] = (dot_nn(dk[rows:], wk) + dot_nn(dv[rows:], wv)).astype(LOW)
    in_out[...] = pre_ref[...] + dot_nn(dq, wq) + dot_nn(dk[:rows], wk) + dot_nn(dv[:rows], wv)


def attention_backward(grad_att, grad_pre, kept, w):
    rows, width = grad_pre.shape
    units = w["qb"].shape[1]
    heads = units // HEAD_DIM
    outs = [
        ((rows, width), F32), ((rows, width), LOW), ((rows, units), LOW), ((2 * rows, units), LOW), ((2 * rows, units), LOW),
    ]
    return call(
        attention_backward_kernel, "attention_backward", 12, outs,
        [((4, 2 * rows, LANES), LOW)],
        grad_att, grad_pre, kept["q"], kept["k"], kept["v"], kept["e"], kept["inv"], kept["o"], w["heads"],
    )


def both_layers(firsts, seconds):
    return sum(dot_tn(a[...], b[...]) for a, b in zip(firsts, seconds))


def ffn_grads_kernel(c, *refs):
    actives, branches, hiddens, middles, attendeds, ones_branches = (refs[2 * i : 2 * i + 2] for i in range(6))
    out, bias_out = refs[12:]
    rows, units = actives[0].shape
    step = units // 8
    ur = step // 4
    hr = attendeds[0].shape[1] // 32
    one = jnp.ones((rows, LANES), LOW)
    out_grad = both_layers(attendeds, ones_branches).astype(LOW)
    for i in range(4):
        at = 4 * c + i
        cols = slice(at * step, (at + 1) * step)
        down = both_layers([a.at[:, cols] for a in actives], branches).astype(LOW)
        up = both_layers([h.at[:, cols] for h in hiddens], middles).astype(LOW)
        bias_out[i * step : (i + 1) * step] = sum(dot_tn(h[:, cols], one) for h in hiddens).astype(LOW)
        for j in range(4):
            out[i, j, :ur] = down[j * ur : (j + 1) * ur]
            out[i, j, ur : 2 * ur] = up[j * ur : (j + 1) * ur]
            head = j * LANES + (2 * i + c) * hr
            out[i, j, 2 * ur :] = out_grad[head : head + hr]


def ffn_grads(pairs, c):
    rows, units = pairs[0][0].shape
    width = pairs[1][0].shape[1]
    ur, hr = units // 32, pairs[4][0].shape[1] // 32
    outs = [((4, 4, 2 * ur + hr, width), LOW), ((units // 2, LANES), LOW)]
    return call(functools.partial(ffn_grads_kernel, c), "ffn_grads", 3, outs, [], *[v for pair in pairs for v in pair])


def head_grads_kernel(eighth_ref, *refs):
    dqs, dks, dvs, lows, others, sums = (refs[2 * i : 2 * i + 2] for i in range(6))
    up_biases, (keep, send, shared) = refs[12:14], refs[14:]
    lane = lax.broadcasted_iota(jnp.int32, (1, LANES), 1) // (LANES // 4)
    shared[...] = sums[0][...] + sums[1][...]
    upper = lax.broadcasted_iota(jnp.int32, (16, 1), 0) < 8
    rows, units = dqs[0].shape
    hr = units // 32
    one = jnp.ones((rows, LANES), LOW)

    def halves(grads):
        own = [g.at[:rows] for g in grads]
        return own, [g.at[rows:] for g in grads]

    dk_own, dk_other = halves(dks)
    dv_own, dv_other = halves(dvs)
    grads = [
        both_layers(dqs, lows),
        both_layers(dk_own + dk_other, lows + others),
        both_layers(dv_own + dv_other, lows + others),
    ]
    grads = [g.astype(LOW) for g in grads]
    biases = [sum(dot_tn(g[...], one) for g in part).astype(LOW) for part in (dqs, dv_own + dv_other)]
    for at in range(8):
        c, i = divmod(at, 4)
        line = shared[pl.ds(eighth_ref[0] ^ (2 * i + c), 1)]
        line = jnp.where(upper, line[:, : 2 * LANES], line[:, 2 * LANES :]).astype(LOW)
        for j in range(4):
            out = keep.at[i, j] if c == 0 else send.at[4 * i + j]
            first = j * LANES + (2 * i + c) * hr
            for kind in range(3):
                out[kind * hr : (kind + 1) * hr] = grads[kind][first : first + hr]
            q, v = (bias[first : first + hr] for bias in biases)
            up_bias = up_biases[c]
            first = (4 * i + j) * (up_bias.shape[0] // 16)
            u = [up_bias[first + g * hr : first + (g + 1) * hr] for g in range(4)]
            out[3 * hr :, :LANES] = jnp.where(lane < 1, q, jnp.where(lane < 2, v, jnp.where(lane < 3, u[0], u[1])))
            out[3 * hr :, LANES : 2 * LANES] = jnp.where(lane < 1, u[2], u[3])
            out[3 * hr :, 2 * LANES :] = line


def last_backward_kernel(eighth_ref, *refs):
    given, (dq_two, dk_two, dv_two), lows, others, sums = refs[:9], refs[9:12], refs[12:14], refs[14:16], refs[16:18]
    up_biases, (in_out, keep, send, dq, dk, dv, sent_out, vmask, shared) = refs[18:20], refs[20:]
    attention_backward_kernel(*given, in_out, sent_out, dq, dk, dv, vmask)
    head_grads_kernel(eighth_ref, dq_two, dq, dk_two, dk, dv_two, dv, *lows, *others, *sums, *up_biases, keep, send, shared)
    send[16:] = sent_out[...].reshape(-1, *send.shape[1:])


def last_backward(grad_att, grad_pre, kept, w, pairs, eighth):
    rows, width = grad_pre.shape
    units = w["qb"].shape[1]
    block = 4 * (units // 32)
    outs = [((rows, width), F32), ((4, 4, block, width), LOW), ((16 + rows // block, block, width), LOW)]
    scratch = [((rows, units), LOW), ((2 * rows, units), LOW), ((2 * rows, units), LOW), ((rows, width), LOW)]
    scratch += [((4, 2 * rows, LANES), LOW), ((8, width), F32)]
    return call(
        last_backward_kernel, "last_backward", 16, outs, scratch, eighth, grad_att, grad_pre,
        kept["q"], kept["k"], kept["v"], kept["e"], kept["inv"], kept["o"], w["heads"], *pairs, scalars=1,
    )


def first_row(column):
    return column.T[:1]


def finish_kernel(ur, hr, eighth_ref, *refs):
    blocks, (down_out, up_out, out_out, up_bias) = refs[:8], refs[8:12]
    outs, biases, shared, (up_all, up_bias_all, *scratch) = refs[12:15], refs[15:17], refs[17], refs[18:]
    head = 2 * ur + hr
    for at, block in enumerate(blocks):
        c, i = divmod(at, 4)
        slot = eighth_ref[0] ^ (2 * i + c)
        units = pl.ds(pl.multiple_of(slot * ur, ur), ur)
        down_out[units] = block[:ur].astype(F32)
        up_all[units] = block[ur : 2 * ur].astype(F32)
        out_out[pl.ds(pl.multiple_of(slot * hr, hr), hr)] = block[2 * ur : 2 * ur + hr].astype(F32)
        columns = [
            jnp.broadcast_to(block[head + 3 * hr :, at : at + 1].astype(F32), (hr, LANES))
            for at in range(0, 6 * (LANES // 4), LANES // 4)
        ]
        for g in range(4):
            some = pl.ds(pl.multiple_of(slot * ur + g * hr, hr), hr)
            up_bias_all[some] = columns[2 + g]
        units = pl.ds(pl.multiple_of(slot * hr, hr), hr)
        for kind in range(3):
            scratch[kind][units] = block[head + kind * hr : head + (kind + 1) * hr].astype(F32)
        for kind in range(2):
            scratch[3 + kind][units] = columns[kind]
        line = block[head + 3 * hr :, 2 * LANES :].astype(F32)
        shared[pl.ds(slot, 1)] = jnp.concatenate((line[:1], line[8:9]), 1)
    up_out[...] = up_all[...].T
    up_bias[...] = first_row(up_bias_all[...])
    for kind in range(3):
        outs[kind][...] = scratch[kind][...].T
    for kind in range(2):
        biases[kind][...] = first_row(scratch[3 + kind][...])


def finish(blocks, ur, hr, eighth):
    width = blocks[0].shape[1]
    outs = [((8 * ur, width), F32), ((width, 8 * ur), F32), ((8 * hr, width), F32), ((1, 8 * ur), F32)]
    outs += [((width, 8 * hr), F32)] * 3 + [((1, 8 * hr), F32)] * 2 + [((8, width), F32)]
    scratch = [((8 * ur, width), F32), ((8 * ur, LANES), F32)]
    scratch += [((8 * hr, width), F32)] * 3 + [((8 * hr, LANES), F32)] * 2
    return call(functools.partial(finish_kernel, ur, hr), "finish", 3, outs, scratch, eighth, *blocks, scalars=1)


def per_device(
    inputs, segment_ids, query_weight, query_bias, key_weight, value_weight, value_bias, out_weight, out_bias,
    first_gain, first_shift, up_weight, up_bias, down_weight, down_bias, second_gain, second_shift, cotangent,
):
    rows, width = inputs.shape
    dp, tensor = lax.axis_index("dp"), lax.axis_index("tensor")
    core, eighth = dp % 2, dp % 8
    shard_heads, shard_units = query_weight.shape[1], up_weight.shape[1]
    hr, ur = shard_heads // 8, shard_units // 8

    def columns(weight, count):
        return lax.dynamic_slice_in_dim(weight, eighth * count, count, 1).T

    def own_rows(weight, count):
        return lax.dynamic_slice_in_dim(weight, eighth * count, count, 0)

    first_in = regroup(inputs)
    flat = (
        jnp.pad(query_bias, (0, shard_heads + shard_units))
        + jnp.pad(value_bias, (shard_heads, shard_units))
        + jnp.pad(up_bias, (2 * shard_heads, 0))
    )
    top = lax.reduce_precision(flat, 8, 7)
    mid = lax.reduce_precision(flat - top, 8, 7)
    flat = jnp.concatenate((top, mid, flat - top - mid)).astype(LOW)
    count = flat.shape[0]
    flat = jnp.pad(flat, (0, -count % (16 * width))).reshape(-1, width)
    heads_piece = jnp.concatenate(
        [columns(v, hr) for v in (query_weight, key_weight, value_weight)] + [own_rows(out_weight, hr), flat]
    )
    ffn_piece = jnp.concatenate((columns(up_weight, ur), own_rows(down_weight, ur)))
    shards = jnp.stack([heads_piece] + [swap_tensor(heads_piece, step) for step in (1, 2, 3)])
    heads_own = spread_plane(shards[:, : 4 * hr])
    ffn_own = spread_plane(join_shards(ffn_piece))
    first_in, *heads_own = lax.optimization_barrier((first_in, *heads_own))
    head_blocks = heads_own + [swap_dp(block, 1) for block in heads_own]
    flat = shards[:, 4 * hr :].reshape(4, -1)[:, :count].astype(F32)
    flat = jnp.sum(flat.reshape(4, 3, -1), 1)
    seq = lax.dynamic_slice_in_dim(segment_ids, (tensor // 2) * LEN, LEN)
    seq = jnp.where(core == tensor % 2, seq, swap_dp(seq, 1))
    labels_own = lax.dynamic_slice_in_dim(seq, core * rows, rows)
    labels_all = jnp.concatenate((labels_own, lax.dynamic_slice_in_dim(seq, (1 - core) * rows, rows)))
    code = jnp.arange(LANES) % HEAD_DIM - 1
    mark = (labels_own[:, None] == code).astype(LOW)
    barred = jnp.where(labels_all[:, None] == code, 0.0, BARRED).astype(LOW)

    def bias(start, count):
        return relative_blocks(flat[:, start : start + count].reshape(4, 2, 2, 2, -1))

    w = {
        "qb": bias(0, shard_heads).reshape(1, -1), "vb": bias(shard_heads, shard_heads).reshape(1, -1),
        "upb": bias(2 * shard_heads, shard_units).reshape(4, 4, 2, ur).transpose(2, 1, 0, 3).reshape(1, -1),
        "ob": out_bias[None], "g1": first_gain[None], "s1": first_shift[None], "db": down_bias[None],
        "g2": second_gain[None], "s2": second_shift[None],
    }

    kept = []
    layer_in, low = first_in, first_in
    for position in range(2):
        other = swap_dp(low, 1)
        made = attention_forward(layer_in, low, other, mark, barred, w, None if position else head_blocks)
        q, k, v, e, inv, o, attended, unit_one, scale_one, middle = made[:10]
        if position == 0:
            w["heads"] = made[10]
            middle, cotangent, *ffn_own = lax.optimization_barrier((middle, cotangent, *ffn_own))
            ffn_blocks = ffn_own + [swap_dp(block, 1) for block in ffn_own]
        made = ffn_forward(middle, w, None if position else ffn_blocks)
        middle_low, active, slope, unit_two, scale_two, layer_out, next_low = made[:7]
        if position == 0:
            w["ffn"] = made[7]
        attention = {"q": q, "k": k, "v": v, "e": e, "inv": inv, "o": o, "unit": unit_one, "scale": scale_one, "att": attended}
        ffn = {"slope": slope, "unit": unit_two, "scale": scale_two}
        kept.append((attention, ffn, low, other, middle_low, active))
        layer_in, low = layer_out, next_low
    result = low

    grad_flow = regroup(cotangent)
    at = jnp.reshape(eighth, (1,)).astype(jnp.int32)
    attention_two, ffn, low_two, other_two, middle_low, active = kept[1]
    branch_two, grad_hidden, grad_pre, branch_one, grad_att, six_two = ffn_backward(grad_flow, ffn, attention_two, w)
    pairs_two = (active, branch_two, grad_hidden, middle_low, attention_two["att"], branch_one)
    grad_in, sent, dq, dk, dv = attention_backward(grad_att, grad_pre, attention_two, w)
    grad_flow = grad_in + swap_dp(sent, 1).astype(F32)

    attention, ffn, low, low_other, middle_low, active = kept[0]
    branch_two, grad_hidden, grad_pre, branch_one, grad_att, six = ffn_backward(grad_flow, ffn, attention, w)
    pairs_one = (active, branch_two, grad_hidden, middle_low, attention["att"], branch_one)
    ffn_pairs = list(zip(pairs_two, pairs_one))
    send, other_columns = ffn_grads(ffn_pairs, 1)
    other = swap_dp(send, 1)
    keep, own_columns = ffn_grads(ffn_pairs, 0)
    near, near_sent, far, far_sent = pair_halves(keep, other)
    grad_att, near_sent, far_sent = lax.optimization_barrier((grad_att, near_sent, far_sent))
    near_got, far_got = swap_dp(near_sent, 2), swap_dp(far_sent, 4)
    grad_in, keep, send = last_backward(
        grad_att, grad_pre, attention, w,
        (dq, dk, dv, low_two, low, other_two, low_other, six_two, six, own_columns, other_columns), at,
    )
    keep, send, near_got, far_got = lax.optimization_barrier((keep, send, near_got, far_got))
    (near, near_sent), (far, far_sent) = add_halves(near, near_got), add_halves(far, far_got)
    near_sent, far_sent, send = lax.optimization_barrier((near_sent, far_sent, send))
    near_got, far_got = swap_dp(near_sent, 4), swap_dp(far_sent, 2)
    other = swap_dp(send, 1)
    grad_low = (grad_in + other[16:].reshape(rows, width).astype(F32)).astype(LOW)
    near_head, near_sent, far_head, far_sent = pair_halves(keep, other[:16].reshape(keep.shape))
    near_head_got, far_head_got = lax.optimization_barrier((swap_dp(near_sent, 2), swap_dp(far_sent, 4)))
    (near_head, near_sent), (far_head, far_sent) = add_halves(near_head, near_head_got), add_halves(far_head, far_head_got)
    near_head_got, far_head_got = swap_dp(near_sent, 4), swap_dp(far_sent, 2)
    ffn_parts = swap_shards(add_shards(near, near_got, far, far_got))
    ffn_parts = lax.optimization_barrier((*ffn_parts, near_head_got, far_head_got))[:4]
    ffn_own = sum_shards(ffn_parts)
    head_own = sum_shards(swap_shards(add_shards(near_head, near_head_got, far_head, far_head_got)))
    own = jnp.concatenate((ffn_own, head_own))
    own, grad_low = lax.optimization_barrier((own, grad_low))
    own, *others = spread_plane(own)
    own, *others, home = lax.optimization_barrier((own, *others, regroup(jnp.stack((result, grad_low)))))
    result, input_grad = home[0], home[1].astype(F32)
    plane = [own] + others
    blocks = plane + [swap_dp(block, 1) for block in plane]
    (
        down_grad, up_grad, out_grad, up_bias_grad, q_grad, k_grad, v_grad, q_bias_grad, v_bias_grad, shared,
    ) = finish(blocks, ur, hr, at)
    return (
        result, input_grad, q_grad, q_bias_grad[0], k_grad, v_grad, v_bias_grad[0], out_grad, shared[5], shared[3], shared[4],
        up_grad, up_bias_grad[0], down_grad, shared[2], shared[0], shared[1],
    )


def solution(mesh):
    split = P(("dp", "tensor"), None)
    columns, rows, part = P(None, "tensor"), P("tensor", None), P("tensor")
    return jax.shard_map(
        per_device,
        mesh=mesh,
        in_specs=(
            split, P("dp"), columns, part, columns, columns, part, rows, P(), P(), P(), columns, part, rows, P(), P(),
            P(), split,
        ),
        out_specs=(
            split, split, columns, part, columns, columns, part, rows, P(), P(), P(), columns, part, rows, P(), P(), P(),
        ),
        check_vma=False,
    )
```
